32 devices in a mesh: rep: 2 (over core), fsdp: 16 (over z, y, x).
Axes of the slice: x: 2, y: 2, z: 4, core: 2. Of those that a mesh axis runs over, the one named last changes fastest.
Arguments:
- inputs: bfloat16 [32, 1024, 768], P(('rep', 'fsdp')), may hold values from -6 to 6
- cotangent: bfloat16 [32, 1024, 768], P(('rep', 'fsdp')), may hold values from -6 to 6
- seg_sizes: int32 [32, 8], P(('rep', 'fsdp')), may hold values from 0 to 1024, as said below
- seq_lengths: int32 [32, 8], P(('rep', 'fsdp')), may hold values from 0 to 1024, as said below
- timesteps: int32 [32, 8], P(('rep', 'fsdp')), may hold values from 0 to 999
- absorbed: int32 [32, 1024], P(('rep', 'fsdp')), may hold values 0 or 1
- qkv_weight: float32 [768, 2304], P('fsdp'), may hold values from -0.2 to 0.2
- out_weight: float32 [768, 768], P('fsdp'), may hold values from -2.5 to 2.5
- up_weight: float32 [768, 3072], P('fsdp'), may hold values from -0.25 to 0.25
- down_weight: float32 [3072, 768], P('fsdp'), may hold values from -0.7 to 0.7
- mod_weight: float32 [128, 4608], P(None, 'fsdp'), may hold values from -4 to 4
- qkv_first: float32 [768, 2304], P('fsdp'), may hold values from -27.1529 to 27.1529
- out_first: float32 [768, 768], P('fsdp'), may hold values from -2.2627417 to 2.2627417
- up_first: float32 [768, 3072], P('fsdp'), may hold values from -108.6116 to 108.6116
- down_first: float32 [3072, 768], P('fsdp'), may hold values from -43.44464 to 43.44464
- mod_first: float32 [128, 4608], P(None, 'fsdp'), may hold values from -23.532514 to 23.532514
- qkv_second: float32 [768, 2304], P('fsdp'), may hold values from 0 to 18.56
- out_second: float32 [768, 768], P('fsdp'), may hold values from 0 to 0.1312
- up_second: float32 [768, 3072], P('fsdp'), may hold values from 0 to 298.1888
- down_second: float32 [3072, 768], P('fsdp'), may hold values from 0 to 49.152
- mod_second: float32 [128, 4608], P(None, 'fsdp'), may hold values from 0 to 13.1072
- vectors: float32 [9984], P('fsdp'), may hold values from -1.2 to 3.8
- vectors_first: float32 [9984], P('fsdp'), may hold values from -38.01406 to 38.01406
- vectors_second: float32 [9984], P('fsdp'), may hold values from 0 to 36.0448
Outputs:
- out_hidden: bfloat16 [32, 1024, 768], P(('rep', 'fsdp'))
- grad_inputs: float32 [32, 1024, 768], P(('rep', 'fsdp'))
- qkv_updated: float32 [768, 2304], P('fsdp')
- out_updated: float32 [768, 768], P('fsdp')
- up_updated: float32 [768, 3072], P('fsdp')
- down_updated: float32 [3072, 768], P('fsdp')
- mod_updated: float32 [128, 4608], P(None, 'fsdp')
- qkv_moment: float32 [768, 2304], P('fsdp')
- out_moment: float32 [768, 768], P('fsdp')
- up_moment: float32 [768, 3072], P('fsdp')
- down_moment: float32 [3072, 768], P('fsdp')
- mod_moment: float32 [128, 4608], P(None, 'fsdp')
- qkv_variance: float32 [768, 2304], P('fsdp')
- out_variance: float32 [768, 768], P('fsdp')
- up_variance: float32 [768, 3072], P('fsdp')
- down_variance: float32 [3072, 768], P('fsdp')
- mod_variance: float32 [128, 4608], P(None, 'fsdp')
- vectors_updated: float32 [9984], P('fsdp')
- vectors_moment: float32 [9984], P('fsdp')
- vectors_variance: float32 [9984], P('fsdp')
- weight_norms: float32 [2, 5], replicated
The draws below stay inside these ranges and needn't reach their ends.
Inputs may be any that keep to these rules, and one draw needn't show every extreme that they name: `seg_sizes`: in every row the nonzero entries come first, each is 1024, 512 or 128, and they sum to 1024; the rest are zero. `seq_lengths`: each entry lies between half of the matching seg_sizes entry and all of it; zero where that entry is zero.
All inputs are finite; a program needn't handle non-finite values. No bound on the sum of `absorbed` on one device may be relied on, other than what follows from the above.
Results may differ from the reference program's by a relative error of at most 0.025.
The reference program's roundings to bfloat16 on the way count: a program that leaves them out, or rounds other values in their place, can miss the bound.
Values may be sent and summed in bfloat16 or wider, within the bound.
No kernel may reach another device: no remote copies, remote signals or barrier semaphores. Data moves between devices by JAX's collectives and lax.ppermute only.
A program may use at most 320 MiB of HBM per device.

```python
import math
import jax
import jax.numpy as jnp
import numpy as np
from jax import lax

D = 768
HEADS = 12
HDIM = 64
FF = 3072
COND = 128
SLOTS = 1024
NSEG = 8
QBLOCK = 512
STEP = 10
ROWS = 32
TOKENS = 32768


LAYOUTS = np.array([[8, 0, 0, 0, 0, 0, 0, 0], [4, 4, 0, 0, 0, 0, 0, 0], [4, 1, 1, 1, 1, 0, 0, 0], [1, 1, 1, 1, 1, 1, 1, 1]], dtype=np.int32)


def layout_draw(key):
    picks = jax.random.randint(jax.random.fold_in(key, 101), (ROWS,), 0, 20)
    kinds = (picks >= 11).astype(jnp.int32) + (picks >= 15).astype(jnp.int32) + (picks >= 18).astype(jnp.int32)
    kinds = kinds.at[0].set(0)
    table = jnp.asarray(LAYOUTS)
    return table[kinds] * (SLOTS // 8)


def draw_seg_sizes(key, part):
    return layout_draw(key)


def draw_seq_lengths(key, part):
    widths = layout_draw(key)
    key = jax.random.fold_in(key, 7)
    extra = jax.random.randint(key, widths.shape, 0, SLOTS + 1)
    lengths = widths // 2 + extra % (widths // 2 + 1)
    return lengths.at[0, 0].set(SLOTS)


def noise(key, shape):
    keys = jax.random.split(key, 1)
    gauss = jnp.clip(jax.random.normal(keys[0], shape, jnp.float32), -4.0, 4.0)
    return gauss


def ramp(count, low_end, high_end):
    return low_end + (high_end - low_end) * jnp.arange(count, dtype=jnp.float32) / (count - 1)


def shaped_ramp(shape, axis, low_end, high_end):
    line = ramp(shape[axis], low_end, high_end)
    if len(shape) == 1:
        return line
    return line[:, None] if axis == 0 else line[None, :]


def rising(key, shape, axis, factor, low_end, high_end):
    return factor * shaped_ramp(shape, axis, low_end, high_end) * noise(key, shape)


def first_moment(key, shape, axis, magnitude):
    keys = jax.random.split(key)
    signs = jnp.where(jax.random.uniform(keys[0], shape) < 0.5, -1.0, 1.0)
    spread = jnp.exp(jax.random.uniform(keys[1], shape, jnp.float32, math.log(0.5), math.log(2.0)))
    return 0.1 / 0.9 * magnitude * signs * spread * shaped_ramp(shape, axis, 0.6, 1.8)


def second_moment(key, shape, magnitude):
    spread = jnp.exp(jax.random.uniform(key, shape, jnp.float32, 0.0, math.log(4.0)))
    return 0.001 / 0.999 * magnitude * magnitude * spread


def qkv_size():
    return 12.0 * math.sqrt(TOKENS / SLOTS)


def out_size():
    return math.sqrt(TOKENS / SLOTS)


def draw_qkv_weight(key, part):
    key = jax.random.fold_in(key, 1)
    return rising(key, (D, 3 * D), 0, 0.3 / math.sqrt(D), 0.6, 1.8)


def draw_out_weight(key, part):
    key = jax.random.fold_in(key, 2)
    return rising(key, (D, D), 0, 4.0 / math.sqrt(D), 0.6, 1.8)


def draw_up_weight(key, part):
    key = jax.random.fold_in(key, 3)
    return rising(key, (D, FF), 0, 0.4 / math.sqrt(D), 0.6, 1.8)


def draw_down_weight(key, part):
    key = jax.random.fold_in(key, 4)
    return rising(key, (FF, D), 0, 1.0 / math.sqrt(FF), 0.6, 1.8)


def draw_mod_weight(key, part):
    key = jax.random.fold_in(key, 5)
    return rising(key, (COND, 6 * D), 1, 1.5 / math.sqrt(COND), 0.6, 1.8)


def draw_qkv_first(key, part):
    key = jax.random.fold_in(key, 11)
    return first_moment(key, (D, 3 * D), 0, qkv_size())


def draw_out_first(key, part):
    key = jax.random.fold_in(key, 12)
    return first_moment(key, (D, D), 0, out_size())


def draw_up_first(key, part):
    key = jax.random.fold_in(key, 13)
    return first_moment(key, (D, FF), 0, 1.5 * math.sqrt(TOKENS))


def draw_down_first(key, part):
    key = jax.random.fold_in(key, 14)
    return first_moment(key, (FF, D), 0, 0.6 * math.sqrt(TOKENS))


def draw_mod_first(key, part):
    key = jax.random.fold_in(key, 15)
    return first_moment(key, (COND, 6 * D), 1, 0.3 * math.sqrt(TOKENS))


def draw_qkv_second(key, part):
    key = jax.random.fold_in(key, 21)
    return second_moment(key, (D, 3 * D), qkv_size())


def draw_out_second(key, part):
    key = jax.random.fold_in(key, 22)
    return second_moment(key, (D, D), out_size())


def draw_up_second(key, part):
    key = jax.random.fold_in(key, 23)
    return second_moment(key, (D, FF), 1.5 * math.sqrt(TOKENS))


def draw_down_second(key, part):
    key = jax.random.fold_in(key, 24)
    return second_moment(key, (FF, D), 0.6 * math.sqrt(TOKENS))


def draw_mod_second(key, part):
    key = jax.random.fold_in(key, 25)
    return second_moment(key, (COND, 6 * D), 0.3 * math.sqrt(TOKENS))


def vector_draw(key, low_end, high_end):
    keys = jax.random.split(key)
    rough = jnp.exp(jax.random.uniform(keys[0], (2 * D,), jnp.float32, -0.22, 0.22))
    gains = jnp.concatenate([ramp(D, low_end, high_end), ramp(D, low_end, high_end)]) * rough
    biases = 0.3 * noise(keys[1], (FF + 7 * D,))
    return jnp.concatenate([gains, biases])


def draw_vectors(key, part):
    key = jax.random.fold_in(key, 31)
    return vector_draw(key, 1.0, 3.0)


def draw_vectors_first(key, part):
    key = jax.random.fold_in(key, 32)
    return first_moment(key, (9 * D + FF,), 0, 0.5 * math.sqrt(TOKENS))


def draw_vectors_second(key, part):
    key = jax.random.fold_in(key, 33)
    return second_moment(key, (9 * D + FF,), 0.5 * math.sqrt(TOKENS))


def place_ends(values, own_key, low, high):
    shape = values.shape
    place = [jax.random.randint(jax.random.fold_in(own_key, axis), (), 0, shape[axis]) for axis in range(len(shape))]
    values = values.at[tuple(place)].set(low)
    longest = shape.index(max(shape))
    place[longest] = (place[longest] + 1) % shape[longest]
    return values.at[tuple(place)].set(high)


def block_scale(rng, dims, shards, smallest, high):
    factor_of = 1.0
    for dim, blocks in shards:
        heights = jax.random.uniform(jax.random.fold_in(jax.random.fold_in(rng, 6), dim), (blocks,), jnp.float32, smallest / len(shards), high / len(shards))
        factor_of = factor_of * jnp.repeat(jnp.exp(heights), dims[dim] // blocks).reshape((-1,) + (1,) * (len(dims) - 1 - dim))
    return factor_of


def gaussian(own_key, extent, width, reach, cuts=(), kind=jnp.bfloat16):
    values = width * jax.random.normal(own_key, extent, jnp.float32)
    if cuts:
        values = values * block_scale(own_key, extent, cuts, -0.22, 0.18)
    return jnp.clip(values, -reach, reach).astype(kind)


def setup_inputs(seed: int = 0) -> dict:
    seeds = jax.random.split(jax.random.key(seed), 25)
    inputs = gaussian(seeds[0], (ROWS, SLOTS, D), 1.0, 6.0, ((0, 32),))
    cotangent = gaussian(seeds[1], (ROWS, SLOTS, D), 1.0, 6.0, ((0, 32),))
    seg_sizes = draw_seg_sizes(jax.random.fold_in(seeds[24], 71), 0)
    seq_lengths = draw_seq_lengths(jax.random.fold_in(seeds[24], 71), 0)
    timesteps = place_ends(jax.random.randint(seeds[4], (ROWS, NSEG), 0, 1000), jax.random.fold_in(seeds[4], 1), 0, 999).astype(jnp.int32)
    absorbed = place_ends((jax.random.randint(seeds[5], (ROWS, SLOTS), 0, 2) < 1).astype(jnp.int32), jax.random.fold_in(seeds[5], 1), 0, 1)
    qkv_weight = draw_qkv_weight(jax.random.fold_in(seeds[24], 71), 0)
    out_weight = draw_out_weight(jax.random.fold_in(seeds[24], 71), 0)
    up_weight = draw_up_weight(jax.random.fold_in(seeds[24], 71), 0)
    down_weight = draw_down_weight(jax.random.fold_in(seeds[24], 71), 0)
    mod_weight = draw_mod_weight(jax.random.fold_in(seeds[24], 71), 0)
    qkv_first = draw_qkv_first(jax.random.fold_in(seeds[24], 71), 0)
    out_first = draw_out_first(jax.random.fold_in(seeds[24], 71), 0)
    up_first = draw_up_first(jax.random.fold_in(seeds[24], 71), 0)
    down_first = draw_down_first(jax.random.fold_in(seeds[24], 71), 0)
    mod_first = draw_mod_first(jax.random.fold_in(seeds[24], 71), 0)
    qkv_second = draw_qkv_second(jax.random.fold_in(seeds[24], 71), 0)
    out_second = draw_out_second(jax.random.fold_in(seeds[24], 71), 0)
    up_second = draw_up_second(jax.random.fold_in(seeds[24], 71), 0)
    down_second = draw_down_second(jax.random.fold_in(seeds[24], 71), 0)
    mod_second = draw_mod_second(jax.random.fold_in(seeds[24], 71), 0)
    vectors = draw_vectors(jax.random.fold_in(seeds[24], 71), 0)
    vectors_first = draw_vectors_first(jax.random.fold_in(seeds[24], 71), 0)
    vectors_second = draw_vectors_second(jax.random.fold_in(seeds[24], 71), 0)
    return dict(inputs=inputs, cotangent=cotangent, seg_sizes=seg_sizes, seq_lengths=seq_lengths, timesteps=timesteps, absorbed=absorbed, qkv_weight=qkv_weight, out_weight=out_weight, up_weight=up_weight, down_weight=down_weight, mod_weight=mod_weight, qkv_first=qkv_first, out_first=out_first, up_first=up_first, down_first=down_first, mod_first=mod_first, qkv_second=qkv_second, out_second=out_second, up_second=up_second, down_second=down_second, mod_second=mod_second, vectors=vectors, vectors_first=vectors_first, vectors_second=vectors_second)


@jax.custom_vjp
def low(v):
    return lax.optimization_barrier(v.astype(jnp.bfloat16)).astype(jnp.float32)

@jax.custom_vjp
def low_back(v):
    return v

def low_keep(v):
    return (low(v), None)

def low_pass(kept, grad):
    return (grad,)

def back_keep(v):
    return (v, None)

def back_low(kept, grad):
    return (low(grad),)
low.defvjp(low_keep, low_pass)
low_back.defvjp(back_keep, back_low)
HIGHEST = lax.Precision.HIGHEST
BETA_ONE = 0.9
BETA_TWO = 0.999
EPSILON = 1e-06
DECAY_RATE = 0.01
MATRIX_RATE = 0.3
VECTOR_RATE = 1.0

def matmul(left_side, right_side):
    return jnp.dot(left_side, right_side, precision=HIGHEST, preferred_element_type=jnp.float32)

def einsum_high(pattern, left_side, right_side):
    return jnp.einsum(pattern, left_side, right_side, precision=HIGHEST, preferred_element_type=jnp.float32)

def normalize(values):
    average = lax.optimization_barrier(jnp.mean(values, axis=-1, keepdims=True))
    centered = values - average
    return centered * lax.rsqrt(lax.optimization_barrier(jnp.mean(centered * centered, axis=-1, keepdims=True)) + 1e-05)

def modulate(values, gain_in, shift_in, scale_in):
    return normalize(values) * gain_in * (1.0 + scale_in) + shift_in

def rotate(values, position):
    half_dim = values.shape[-1] // 2
    inverse = jnp.exp(jnp.arange(half_dim, dtype=jnp.float32) * (-math.log(10000.0) / half_dim))
    angles = position.astype(jnp.float32)[:, None] * inverse[None, :]
    cosine = jnp.cos(angles)[:, None, :]
    sine_of = jnp.sin(angles)[:, None, :]
    leading = values[..., :half_dim]
    trailing = values[..., half_dim:]
    return jnp.concatenate([leading * cosine - trailing * sine_of, trailing * cosine + leading * sine_of], axis=-1)

def layout_tables(sizes_row, lengths_row):
    slot_ids = jnp.arange(SLOTS, dtype=jnp.int32)
    seg_ends = jnp.cumsum(sizes_row).astype(jnp.int32)
    starts = (seg_ends - sizes_row).astype(jnp.int32)
    segment = lax.optimization_barrier(jnp.sum((slot_ids[:, None] >= seg_ends[None, :]).astype(jnp.int32), axis=1)).astype(jnp.int32)
    member = segment[:, None] == jnp.arange(NSEG, dtype=jnp.int32)[None, :]
    offset = lax.optimization_barrier(jnp.sum(jnp.where(member, starts[None, :], 0), axis=1)).astype(jnp.int32)
    length_of = lax.optimization_barrier(jnp.sum(jnp.where(member, lengths_row[None, :], 0), axis=1)).astype(jnp.int32)
    position = (slot_ids - offset).astype(jnp.int32)
    return (segment, member, position, position < length_of)

def condition(steps_row):
    half_cond = COND // 2
    frequency = jnp.exp(jnp.arange(half_cond, dtype=jnp.float32) * (-math.log(10000.0) / half_cond))
    angles = steps_row.astype(jnp.float32)[:, None] * frequency[None, :]
    return jax.nn.silu(jnp.concatenate([jnp.cos(angles), jnp.sin(angles)], axis=1))

def attention(query_low, key_low, value_low, segment, valid_slot):
    scale_by = HDIM ** (-0.5)

    def one_block(begin_at):
        block_query = lax.dynamic_slice_in_dim(query_low, begin_at, QBLOCK, 0)
        block_segment = lax.dynamic_slice_in_dim(segment, begin_at, QBLOCK, 0)
        allowed = (block_segment[:, None] == segment[None, :]) & valid_slot[None, :]
        scores = low_back(einsum_high('qhd,khd->hqk', block_query, key_low)) * scale_by
        masked = jnp.where(allowed[None], scores, -1e+30)
        row_peak = lax.optimization_barrier(jnp.max(masked, axis=-1, keepdims=True))
        weights_exp = jnp.exp(masked - row_peak)
        row_total = lax.optimization_barrier(jnp.sum(weights_exp, axis=-1, keepdims=True))
        chances = low(weights_exp / row_total)
        return einsum_high('hqk,khd->qhd', chances, value_low)
    begins = jnp.arange(SLOTS // QBLOCK, dtype=jnp.int32) * QBLOCK
    blocks = lax.map(jax.checkpoint(one_block), begins)
    return blocks.reshape(SLOTS, D)

def row_layer(packed, mats_low, vecs_low):
    row_inputs, sizes_row, lengths_row, steps_row = packed
    qkv_low, out_low, up_low, down_low, mod_low = mats_low
    gain_one = vecs_low[:D]
    gain_two = vecs_low[D:2 * D]
    bias_up = vecs_low[2 * D:2 * D + FF]
    bias_down = vecs_low[2 * D + FF:3 * D + FF]
    bias_mod = vecs_low[3 * D + FF:]
    segment, member, position, valid_slot = layout_tables(sizes_row, lengths_row)
    condition_low = low(condition(steps_row))
    modulation = matmul(condition_low, mod_low) + bias_mod
    per_slot = matmul(member.astype(jnp.float32), modulation)
    shift_one, scale_one, gate_one, shift_two, scale_two, gate_two = jnp.split(per_slot, 6, axis=1)
    first_low = low(modulate(row_inputs, gain_one, shift_one, scale_one))
    mixed_qkv = low_back(matmul(first_low, qkv_low))
    heads_shape = (SLOTS, HEADS, HDIM)
    query_low = low(rotate(mixed_qkv[:, :D].reshape(heads_shape), position))
    key_low = low(rotate(mixed_qkv[:, D:2 * D].reshape(heads_shape), position))
    value_low = low(mixed_qkv[:, 2 * D:].reshape(heads_shape))
    attended = attention(query_low, key_low, value_low, segment, valid_slot)
    attended_low = low(low_back(attended))
    branch = low_back(matmul(attended_low, out_low))
    middle = row_inputs + gate_one * branch
    second_low = low(modulate(middle, gain_two, shift_two, scale_two))
    up_values = low_back(matmul(second_low, up_low) + bias_up)
    hidden_low = low(jax.nn.gelu(up_values, approximate=True))
    feed_out = low_back(matmul(hidden_low, down_low) + bias_down)
    return middle + gate_two * feed_out

def adam_direction(weight, first_old, second_old, gradient, decay_rate):
    first_new = BETA_ONE * first_old + (1.0 - BETA_ONE) * gradient
    second_new = BETA_TWO * second_old + (1.0 - BETA_TWO) * gradient * gradient
    direction = first_new / (1.0 - BETA_ONE ** STEP) / (jnp.sqrt(second_new / (1.0 - BETA_TWO ** STEP)) + EPSILON) + decay_rate * weight
    return (first_new, second_new, direction)

def reference(inputs, cotangent, seg_sizes, seq_lengths, timesteps, absorbed, qkv_weight, out_weight, up_weight, down_weight, mod_weight, qkv_first, out_first, up_first, down_first, mod_first, qkv_second, out_second, up_second, down_second, mod_second, vectors, vectors_first, vectors_second):
    matrices = (qkv_weight, out_weight, up_weight, down_weight, mod_weight)
    firsts = (qkv_first, out_first, up_first, down_first, mod_first)
    seconds = (qkv_second, out_second, up_second, down_second, mod_second)

    def forward(hidden_in, mats, vecs):
        mats_low = tuple((low(weight) for weight in mats))
        vecs_low = low(vecs)

        def one_row(packed):
            return row_layer(packed, mats_low, vecs_low)
        return lax.map(jax.checkpoint(one_row), (hidden_in, seg_sizes, seq_lengths, timesteps))
    result, pullback = jax.vjp(forward, inputs.astype(jnp.float32), matrices, vectors)

    def valid_of(sizes_row, lengths_row):
        return layout_tables(sizes_row, lengths_row)[3].astype(jnp.int32)
    valid_all = jax.vmap(valid_of)(seg_sizes, seq_lengths)
    weight_mask = (absorbed * valid_all).astype(jnp.float32)
    grad_out = cotangent.astype(jnp.float32) * weight_mask[:, :, None]
    grad_inputs, grad_mats, grad_vecs = pullback(grad_out)
    renewed = []
    moments = []
    variances = []
    weight_roots = []
    update_roots = []
    for number in range(5):
        first_new, second_new, direction = adam_direction(matrices[number], firsts[number], seconds[number], grad_mats[number], DECAY_RATE)
        weight_sq = jnp.sum(matrices[number] * matrices[number])
        update_sq = jnp.sum(direction * direction)
        trust_ratio = jnp.sqrt(weight_sq) / (jnp.sqrt(update_sq) + EPSILON)
        renewed.append(matrices[number] - MATRIX_RATE * trust_ratio * direction)
        moments.append(first_new)
        variances.append(second_new)
        weight_roots.append(jnp.sqrt(weight_sq))
        update_roots.append(jnp.sqrt(update_sq))
    vector_first, vector_second, vector_direction = adam_direction(vectors, vectors_first, vectors_second, grad_vecs, 0.0)
    vector_renewed = vectors - VECTOR_RATE * vector_direction
    weight_norms = jnp.stack([jnp.stack(weight_roots), jnp.stack(update_roots)])
    return (result.astype(jnp.bfloat16), grad_inputs, renewed[0], renewed[1], renewed[2], renewed[3], renewed[4], moments[0], moments[1], moments[2], moments[3], moments[4], variances[0], variances[1], variances[2], variances[3], variances[4], vector_renewed, vector_first, vector_second, weight_norms)
```

```python
import functools
import math

import jax
import jax.numpy as jnp
import numpy as np
from jax import lax
from jax.experimental import pallas as pl
from jax.experimental.pallas import tpu as pltpu
from jax.sharding import PartitionSpec as P

D = 768
HEADS = 12
HDIM = 64
FF = 3072
COND = 128
SLOTS = 1024
NSEG = 8
STEP = 10
TILE = 128
BLOCKS = SLOTS // TILE

BETA_ONE = 0.9
BETA_TWO = 0.999
EPSILON = 1e-06
DECAY_RATE = 0.01
MATRIX_RATE = 0.3
VECTOR_RATE = 1.0

PAIR = 128
NT = (((1,), (1,)), ((), ()))
NN = (((1,), (0,)), ((), ()))
TN = (((0,), (0,)), ((), ()))
BF = jnp.bfloat16
F32 = jnp.float32


def mm(a, b, dims=NN):
    return lax.dot_general(a, b, dims, preferred_element_type=F32)


def swap_halves(v):
    lane = lax.broadcasted_iota(jnp.int32, v.shape, 1)
    return jnp.where(lane % 64 < 32, pltpu.roll(v, PAIR - 32, 1), pltpu.roll(v, 32, 1))


def attention_forward_kernel(block, q_ref, k_ref, v_ref, cos_ref, sin_ref, fq_ref, fk_ref,
                             o_ref, qr_ref, kr_ref, vr_ref, fo_ref, ka, kb, va, vb):
    slots = q_ref.shape[0]
    low_all = lax.broadcasted_iota(jnp.int32, (slots, PAIR), 1) < 64
    cos, sin = cos_ref[...], sin_ref[...]
    q = q_ref[...]
    k = k_ref[...]
    qr_ref[...] = ((q * cos + swap_halves(q) * sin) * 0.125).astype(BF)
    k_low = (k * cos + swap_halves(k) * sin).astype(BF)
    v_low = v_ref[...].astype(BF)
    kr_ref[...] = k_low
    vr_ref[...] = v_low
    fk = fk_ref[...]
    one = jnp.ones((slots, PAIR), BF)
    ka[...] = jnp.where(low_all, k_low, fk)
    kb[...] = jnp.where(low_all, fk, k_low)
    va[...] = jnp.where(low_all, v_low, one)
    vb[...] = jnp.where(low_all, one, v_low)
    lane = lax.broadcasted_iota(jnp.int32, (block, PAIR), 1)
    low = lane < 64
    spot = lane % 64

    def step(i, carry):
        at = pl.ds(pl.multiple_of(i * block, block), block)
        qb_ = qr_ref[at, :]
        fq = fq_ref[at, :]
        sa = mm(jnp.where(low, qb_, fq), ka[...], NT)
        sb = mm(jnp.where(low, fq, qb_), kb[...], NT)
        ma = jnp.max(sa, axis=1, keepdims=True)
        mb = jnp.max(sb, axis=1, keepdims=True)
        pa = jnp.exp(sa - ma).astype(BF)
        pb = jnp.exp(sb - mb).astype(BF)
        oa = mm(pa, va[...])
        ob = mm(pb, vb[...])
        o = jnp.where(low, oa / pltpu.roll(oa, 64, 1), ob / pltpu.roll(ob, 64, 1))
        o_ref[at, :] = o.astype(o_ref.dtype)
        neg = jnp.where(low, -(mb + jnp.log(ob)), -(ma + jnp.log(oa)))
        hi = neg.astype(BF)
        rest = neg - hi.astype(F32)
        mid = rest.astype(BF)
        last = (rest - mid.astype(F32)).astype(BF)
        fo_ref[at, :] = jnp.where(spot == 8, hi, jnp.where(spot == 9, mid, jnp.where(spot == 10, last, fq)))
        return carry

    lax.fori_loop(0, slots // block, step, 0)


def attention_forward(mixed, cos, sin, fq, fk, first, count, block=256):
    slots, width = mixed.shape
    pairs = width // 3 // PAIR
    blk = lambda off: pl.BlockSpec((slots, PAIR), lambda p: (0, off + p))
    fixed = pl.BlockSpec((slots, PAIR), lambda p: (0, 0))
    out = pl.BlockSpec((slots, PAIR), lambda p: (0, p))
    w = count * PAIR
    elements = 2 * count * slots * slots
    bf = jax.ShapeDtypeStruct((slots, w), BF)
    return pl.pallas_call(
        functools.partial(attention_forward_kernel, block),
        grid=(count,),
        in_specs=[blk(first), blk(pairs + first), blk(2 * pairs + first), fixed, fixed, fixed, fixed],
        out_specs=[out] * 5,
        out_shape=[bf, bf, bf, bf, bf],
        scratch_shapes=[pltpu.VMEM((slots, PAIR), BF)] * 4,
        cost_estimate=pl.CostEstimate(flops=elements * 1000, bytes_accessed=8 * slots * w * 3, transcendentals=elements),
        compiler_params=pltpu.CompilerParams(vmem_limit_bytes=48 * 2**20),
    )(mixed, mixed, mixed, cos, sin, fq, fk)


def attention_backward_kernel(block, qr_ref, kr_ref, vr_ref, fo_ref, fk_ref, do_ref, o_ref, cos_ref, sin_ref,
                              g_ref, ka, kb, va, vb, kt, dka, dkb, dva, dvb):
    slots = qr_ref.shape[0]
    lane_all = lax.broadcasted_iota(jnp.int32, (slots, PAIR), 1)
    low_all = lane_all < 64
    fk = fk_ref[...]
    k_low = kr_ref[...]
    v_low = vr_ref[...]
    one = jnp.where(lane_all % 64 < 2, 1.0, 0.0).astype(BF)
    ka[...] = jnp.where(low_all, k_low, fk)
    kb[...] = jnp.where(low_all, fk, k_low)
    va[...] = jnp.where(low_all, v_low, one)
    vb[...] = jnp.where(low_all, one, v_low)
    kt[...] = k_low.T
    dka[...] = jnp.zeros_like(dka)
    dkb[...] = jnp.zeros_like(dkb)
    dva[...] = jnp.zeros_like(dva)
    dvb[...] = jnp.zeros_like(dvb)
    lane = lax.broadcasted_iota(jnp.int32, (block, PAIR), 1)
    low = lane < 64
    spot = lane % 64
    top = lax.broadcasted_iota(jnp.int32, (PAIR, block), 0) < 64

    def step(i, carry):
        at = pl.ds(pl.multiple_of(i * block, block), block)
        q = qr_ref[at, :]
        fq = fo_ref[at, :]
        do = do_ref[at, :]
        both = do.astype(F32) * o_ref[at, :].astype(F32)
        da = jnp.sum(jnp.where(low, both, 0.0), axis=1, keepdims=True)
        db = jnp.sum(jnp.where(low, 0.0, both), axis=1, keepdims=True)
        neg = jnp.where(low, -db, -da)
        hi = neg.astype(BF)
        rest = (neg - hi.astype(F32)).astype(BF)
        fd = jnp.where(spot == 0, hi, jnp.where(spot == 1, rest, jnp.zeros_like(hi)))
        sa = mm(ka[...], jnp.where(low, q, fq), NT)
        sb = mm(kb[...], jnp.where(low, fq, q), NT)
        ea = mm(va[...], jnp.where(low, do, fd), NT)
        eb = mm(vb[...], jnp.where(low, fd, do), NT)
        pa = jnp.exp(sa)
        pb = jnp.exp(sb)
        dsa = (pa * ea).astype(BF)
        dsb = (pb * eb).astype(BF)
        dva[...] += mm(pa.astype(BF), do)
        dvb[...] += mm(pb.astype(BF), do)
        dka[...] += mm(dsa, q)
        dkb[...] += mm(dsb, q)
        dqt = jnp.where(top, mm(kt[...], dsa), mm(kt[...], dsb))
        dq = dqt.T * 0.125
        g_ref[0, at, :] = (dq * cos_ref[at, :] - swap_halves(dq) * sin_ref[at, :]).astype(BF)
        return carry

    lax.fori_loop(0, slots // block, step, 0)
    dk = jnp.where(low_all, dka[...], dkb[...])
    g_ref[1] = (dk * cos_ref[...] - swap_halves(dk) * sin_ref[...]).astype(BF)
    g_ref[2] = jnp.where(low_all, dva[...], dvb[...]).astype(BF)


def attention_backward(qr, kr, vr, fo, fk, do, o, cos, sin, count, block=256):
    slots, width = qr.shape
    mine = pl.BlockSpec((slots, PAIR), lambda p: (0, p))
    fixed = pl.BlockSpec((slots, PAIR), lambda p: (0, 0))
    w = count * PAIR
    return pl.pallas_call(
        functools.partial(attention_backward_kernel, block),
        grid=(count,),
        in_specs=[mine, mine, mine, mine, fixed, mine, mine, fixed, fixed],
        out_specs=pl.BlockSpec((3, slots, PAIR), lambda p: (0, 0, p)),
        out_shape=jax.ShapeDtypeStruct((3, slots, w), BF),
        scratch_shapes=[pltpu.VMEM((slots, PAIR), BF)] * 4 + [pltpu.VMEM((PAIR, slots), BF)]
        + [pltpu.VMEM((slots, PAIR), F32)] * 4,
        cost_estimate=pl.CostEstimate(
            flops=4 * count * slots * slots * 1000, bytes_accessed=16 * slots * w, transcendentals=2 * count * slots * slots
        ),
        compiler_params=pltpu.CompilerParams(vmem_limit_bytes=48 * 2**20),
    )(qr, kr, vr, fo, fk, do, o, cos, sin)


def attention_tables(segment, position, valid_slot):
    inverse = jnp.exp(jnp.arange(32, dtype=F32) * (-math.log(10000.0) / 32))
    angles = position.astype(F32)[:, None] * inverse[None, :]
    c, s = jnp.cos(angles), jnp.sin(angles)
    cos = jnp.concatenate([c, c, c, c], axis=1)
    sin = jnp.concatenate([-s, s, -s, s], axis=1)
    spot = jnp.arange(PAIR) % 64
    same = segment[:, None] == spot[None, :]
    fq = same.astype(BF)
    fk = jnp.where((spot < 8)[None, :], jnp.where(same & valid_slot[:, None], 0.0, -1e30),
                   jnp.where((spot < 11)[None, :], 1.0, 0.0)).astype(BF)
    return cos, sin, fq, fk


CHIPS = 16
ALONG_X, ALONG_Y, ALONG_Z = (1, 0, 0), (0, 1, 0), (0, 0, 1)
ROUNDS = (
    (((0, 0, 0), ALONG_X), ((0, 0, 0), ALONG_Y), ((0, 0, 0), ALONG_Z)),
    (((0, 1, 0), ALONG_X), ((0, 0, 1), ALONG_Y), ((0, 0, 1), ALONG_Z)),
    (((0, 1, 1), ALONG_X), ((0, 0, 2), ALONG_Y), ((0, 0, 2), ALONG_Z)),
    (((0, 0, 1), ALONG_X), ((0, 0, 3), ALONG_Y), ((1, 1, 1), ALONG_Z)),
    (((0, 0, 3), ALONG_X), ((1, 1, 2), ALONG_Y), ((1, 1, 2), ALONG_Z)),
)
OFFSETS = tuple((a, b, c) for c in range(4) for b in range(2) for a in range(2))


def moved(chip, step, sign=1):
    return ((chip & 1) ^ step[0]) + 2 * (((chip >> 1) & 1) ^ step[1]) + 4 * (((chip >> 2) + sign * step[2]) % 4)


def added(offset, step):
    return (offset[0] ^ step[0], offset[1] ^ step[1], (offset[2] + step[2]) % 4)


ORIGIN = np.array([[moved(chip, offset, -1) for offset in OFFSETS] for chip in range(CHIPS)], np.int32)


def pass_on(values, step, sign=1):
    return lax.ppermute(values, "fsdp", [(chip, moved(chip, step, sign)) for chip in range(CHIPS)])


def swap_core(values):
    return lax.ppermute(values, "rep", [(0, 1), (1, 0)])


def gather_units(unit):
    held = {OFFSETS[0]: unit}
    for round_steps in ROUNDS:
        arrived = [(added(offset, step), pass_on(held[offset], step)) for offset, step in round_steps]
        held.update(arrived)
    return [held[offset] for offset in OFFSETS]


def scatter_units(units, origins):
    sums = {
        offset: lax.dynamic_index_in_dim(units, origins[place], 0, keepdims=False).astype(F32)
        for place, offset in enumerate(OFFSETS)
    }
    for round_steps in reversed(ROUNDS):
        arrived = [
            (offset, pass_on(sums[added(offset, step)].astype(BF), step, -1)) for offset, step in round_steps
        ]
        for offset, values in arrived:
            sums[offset] = sums[offset] + values.astype(F32)
    return sums[OFFSETS[0]]


def sum_small(values):
    for step in (ALONG_X, ALONG_Y, (0, 0, 2)):
        values = values + pass_on(values, step)
    return values + lax.ppermute(values, "fsdp", [(chip, chip ^ 4) for chip in range(CHIPS)])


def place_kernel(plan, count, *refs):
    order_ref, core_ref = refs[:2]
    units = refs[2 : 2 + 2 * CHIPS]
    outs = refs[2 + 2 * CHIPS : -1]
    sems = refs[-1]
    copies = []
    for half in range(2):
        side = core_ref[0] if half == 0 else 1 - core_ref[0]
        for place in range(CHIPS):
            origin = order_ref[place]
            for out, rows, column, width, by_origin, by_side, row, column_side, both in plan:
                if half == 1 and not both:
                    continue
                to_row = pl.multiple_of(origin * by_origin + side * by_side + row, 16)
                to_column = pl.multiple_of(side * column_side, 128) if column_side else 0
                copies.append(
                    pltpu.make_async_copy(
                        units[half * CHIPS + place].at[pl.ds(0, rows), pl.ds(column, width)],
                        outs[out].at[pl.ds(to_row, rows), pl.ds(to_column, width)],
                        sems.at[len(copies)],
                    )
                )
    assert len(copies) == count
    for copy in copies:
        copy.start()
    for copy in copies:
        copy.wait()


def place_units(own, other, order, core, plan, shapes):
    count = sum((2 if piece[-1] else 1) * CHIPS for piece in plan)
    anywhere = pl.BlockSpec(memory_space=pl.ANY)
    scalar = pl.BlockSpec(memory_space=pltpu.SMEM)
    return pl.pallas_call(
        functools.partial(place_kernel, plan, count),
        in_specs=[scalar, scalar] + [anywhere] * (2 * CHIPS),
        out_specs=[anywhere] * len(shapes),
        out_shape=[jax.ShapeDtypeStruct(shape, BF) for shape in shapes],
        scratch_shapes=[pltpu.SemaphoreType.DMA((count,))],
    )(order, core, *own, *other)


SMALL = 128
PLAN_FIRST = (
    (0, 48, 0, 1152, 48, 0, 0, 1152, True),
    (1, 48, 1152, 128, 288, 144, 0, 0, True),
    (1, 48, 1280, 128, 288, 144, 48, 0, True),
    (1, 48, 1408, 128, 288, 144, 96, 0, True),
    (2, 16, 1536, 128, 16, 0, 0, 0, False),
)
PLAN_SECOND = (
    (0, 48, 0, 384, 48, 0, 0, 384, True),
    (1, 48, 384, 1536, 48, 0, 0, 1536, True),
    (2, 48, 1920, 768, 192, 96, 0, 0, True),
    (2, 48, 2688, 768, 192, 96, 48, 0, True),
)


def side_columns(matrix, core, width):
    return lax.dynamic_slice_in_dim(matrix, core * width, width, axis=1)


def side_rows(blocks, core):
    return lax.dynamic_index_in_dim(blocks, core, 1, keepdims=False)


def pack_vectors(rows):
    count = rows.shape[0]
    padded = jnp.pad(rows, ((0, 0), (0, 640 - rows.shape[1]))).reshape(count, 5, 128)
    return jnp.pad(padded, ((0, 0), (0, 43), (0, 0)))


def pack_first(qkv, mod_turned, small, core):
    count = small.shape[0]
    mod_blocks = side_rows(mod_turned.reshape(count, 2, 3, 48, 128), core)
    return jnp.concatenate(
        [
            side_columns(qkv, core, 1152).reshape(count, 48, 1152),
            mod_blocks.transpose(0, 2, 1, 3).reshape(count, 48, 384),
            pack_vectors(small),
        ],
        axis=2,
    )


def pack_second(out, up, down, core):
    count = out.shape[0] // 48
    down_blocks = side_rows(down.reshape(count, 2, 2, 48, D), core)
    return jnp.concatenate(
        [
            side_columns(out, core, 384).reshape(count, 48, 384),
            side_columns(up, core, 1536).reshape(count, 48, 1536),
            down_blocks.transpose(0, 2, 1, 3).reshape(count, 48, 2 * D),
        ],
        axis=2,
    )


def gather_first(qkv, mod, vectors, chip, core):
    if lax.axis_size("fsdp") != CHIPS:
        return (
            lax.all_gather(qkv, "fsdp", axis=0, tiled=True),
            lax.all_gather(mod, "fsdp", axis=1, tiled=True).T,
            lax.all_gather(vectors, "fsdp", axis=0, tiled=True),
        )
    unit = pack_first(qkv, mod.T, vectors[None], core)[0]
    own = gather_units(unit)
    other = [swap_core(one) for one in own]
    qkv_all, mod_all, small = place_units(
        own, other, jnp.asarray(ORIGIN)[chip], core[None], PLAN_FIRST, ((D, 3 * D), (6 * D, COND), (256, 128))
    )
    return (qkv_all, mod_all, small.reshape(CHIPS, 2048)[:, :624].reshape(-1))


def gather_second(out, up, down, chip, core):
    if lax.axis_size("fsdp") != CHIPS:
        return tuple(lax.all_gather(part, "fsdp", axis=0, tiled=True) for part in (out, up, down))
    own = gather_units(pack_second(out, up, down, core)[0])
    other = [swap_core(one) for one in own]
    return place_units(
        own, other, jnp.asarray(ORIGIN)[chip], core[None], PLAN_SECOND, ((D, D), (D, FF), (FF, D))
    )


def reduce_packed(pack, chip, core):
    arrived = swap_core(pack(1 - core).astype(BF))
    units = (pack(core).astype(F32) + arrived.astype(F32)).astype(BF)
    mine = scatter_units(units, jnp.asarray(ORIGIN)[chip]).astype(BF)
    other = swap_core(mine)
    first = jnp.where(core == 0, mine, other).astype(F32)
    second = jnp.where(core == 0, other, mine).astype(F32)
    return (first, second)


def reduce_plain(grad, axis):
    part = lax.psum_scatter(grad.astype(F32), "fsdp", scatter_dimension=axis, tiled=True)
    return lax.psum(part.astype(BF), "rep").astype(F32)


def reduce_first(qkv, mod_turned, vectors, chip, core):
    if lax.axis_size("fsdp") != CHIPS:
        return (reduce_plain(qkv, 0), reduce_plain(mod_turned.T, 1), reduce_plain(vectors, 0))
    small = vectors.reshape(CHIPS, -1)
    first, second = reduce_packed(lambda side: pack_first(qkv, mod_turned, small.astype(BF), side), chip, core)
    turned = jnp.concatenate(
        [half[:, 1152 + 128 * part : 1280 + 128 * part] for half in (first, second) for part in range(3)], axis=0
    )
    return (
        jnp.concatenate([first[:, :1152], second[:, :1152]], axis=1),
        turned.T,
        first[:5, 1536:].reshape(-1)[:624],
    )


def reduce_second(out, up, down, chip, core):
    if lax.axis_size("fsdp") != CHIPS:
        return (reduce_plain(out, 0), reduce_plain(up, 0), reduce_plain(down, 0))
    first, second = reduce_packed(lambda side: pack_second(out, up, down, side), chip, core)
    return (
        jnp.concatenate([first[:, :384], second[:, :384]], axis=1),
        jnp.concatenate([first[:, 384:1920], second[:, 384:1920]], axis=1),
        jnp.concatenate([half[:, 1920 + D * part : 2688 + D * part] for half in (first, second) for part in range(2)], axis=0),
    )


def sum_over_chips(values):
    if lax.axis_size("fsdp") != CHIPS:
        return lax.psum(values, "fsdp")
    return sum_small(values)


def linear(left_side, right_side, dims=NN):
    return lax.dot_general(left_side, right_side, dims, preferred_element_type=F32)


def precise(left_side, right_side, dims=NN):
    return lax.dot_general(
        left_side, right_side, dims, precision=lax.Precision.HIGHEST, preferred_element_type=F32
    )


def layout_tables(sizes_row, lengths_row):
    slot_ids = jnp.arange(SLOTS, dtype=jnp.int32)
    seg_ends = jnp.cumsum(sizes_row)
    starts = seg_ends - sizes_row
    segment = jnp.sum((slot_ids[:, None] >= seg_ends[None, :]).astype(jnp.int32), axis=1)
    member = segment[:, None] == jnp.arange(NSEG, dtype=jnp.int32)[None, :]
    offset = jnp.sum(jnp.where(member, starts[None, :], 0), axis=1)
    length_of = jnp.sum(jnp.where(member, lengths_row[None, :], 0), axis=1)
    position = slot_ids - offset
    return (segment, member, position, position < length_of)


def condition(steps_row):
    half_cond = COND // 2
    frequency = jnp.exp(jnp.arange(half_cond, dtype=F32) * (-math.log(10000.0) / half_cond))
    angles = steps_row.astype(F32)[:, None] * frequency[None, :]
    return jax.nn.silu(jnp.concatenate([jnp.cos(angles), jnp.sin(angles)], axis=1))


def normalize(values):
    average = jnp.mean(values, axis=-1, keepdims=True)
    centered = values - average
    root = lax.rsqrt(jnp.mean(centered * centered, axis=-1, keepdims=True) + 1e-05)
    return (centered * root, root)


def normalize_back(grad, normal, root, gain):
    scaled = grad * gain
    inner = jnp.mean(scaled * normal, axis=-1, keepdims=True)
    return root * (scaled - jnp.mean(scaled, axis=-1, keepdims=True) - normal * inner)


def gelu_slope(values):
    factor = math.sqrt(2.0 / math.pi)
    square = values * values
    bent = jnp.tanh(factor * values * (1.0 + 0.044715 * square))
    return 0.5 * (1.0 + bent) + 0.5 * values * (1.0 - bent * bent) * factor * (1.0 + 3 * 0.044715 * square)


def tiled(values):
    return values.reshape(BLOCKS, TILE, values.shape[-1])


def flat(values):
    return values.reshape(SLOTS, values.shape[-1])


def adam_direction(weight, first_old, second_old, gradient, decay_rate):
    first_new = BETA_ONE * first_old + (1.0 - BETA_ONE) * gradient
    second_new = BETA_TWO * second_old + (1.0 - BETA_TWO) * gradient * gradient
    direction = (
        first_new
        / (1.0 - BETA_ONE**STEP)
        / (jnp.sqrt(second_new / (1.0 - BETA_TWO**STEP)) + EPSILON)
        + decay_rate * weight
    )
    return (first_new, second_new, direction)


GROUPS = 3


def on_device(
    inputs, cotangent, seg_sizes, seq_lengths, timesteps, absorbed,
    qkv_weight, out_weight, up_weight, down_weight, mod_weight,
    qkv_first, out_first, up_first, down_first, mod_first,
    qkv_second, out_second, up_second, down_second, mod_second,
    vectors, vectors_first, vectors_second,
):
    chip = lax.axis_index("fsdp")
    core = lax.axis_index("rep")
    matrices = (qkv_weight, out_weight, up_weight, down_weight, mod_weight)
    weight_squares = jnp.stack([jnp.sum(matrix * matrix) for matrix in matrices])
    low = [matrix.astype(BF) for matrix in matrices]
    qkv_low, mod_turned, vector_low = gather_first(low[0], low[4], vectors.astype(BF), chip, core)
    out_low, up_low, down_low = gather_second(low[1], low[2], low[3], chip, core)

    vector_all = vector_low.astype(F32)
    gain_one, gain_two = vector_all[:D], vector_all[D : 2 * D]
    bias_up = vector_all[2 * D : 2 * D + FF]
    bias_down = vector_all[2 * D + FF : 3 * D + FF]
    bias_mod = vector_all[3 * D + FF :]

    segment, member, position, valid_slot = layout_tables(seg_sizes[0], seq_lengths[0])
    member_tile = member.reshape(BLOCKS, TILE, NSEG)[:, 0].astype(F32)
    condition_low = condition(timesteps[0]).astype(BF)
    modulation = linear(condition_low, mod_turned, NT) + bias_mod
    per_tile = precise(member_tile, modulation)[:, None, :]
    shift_one, scale_one, gate_one, shift_two, scale_two, gate_two = jnp.split(per_tile, 6, axis=2)
    cos, sin, feature_query, feature_key = attention_tables(segment, position, valid_slot)

    wide = tiled(inputs[0].astype(F32))
    normal_one, root_one = normalize(wide)
    first_low = flat(normal_one * gain_one * (1.0 + scale_one) + shift_one).astype(BF)
    mixed = linear(first_low, qkv_low)
    per_call = HEADS // 2 // GROUPS
    forward = [
        attention_forward(mixed, cos, sin, feature_query, feature_key, number * per_call, per_call)
        for number in range(GROUPS)
    ]
    attended_low = jnp.concatenate([part[0] for part in forward], axis=1)
    branch = tiled(linear(attended_low, out_low))
    middle = wide + gate_one * branch
    normal_two, root_two = normalize(middle)
    second_low = flat(normal_two * gain_two * (1.0 + scale_two) + shift_two).astype(BF)
    up_values = linear(second_low, up_low) + bias_up
    hidden_low = jax.nn.gelu(up_values, approximate=True).astype(BF)
    feed_out = tiled(linear(hidden_low, down_low) + bias_down)
    out_hidden = flat(middle + gate_two * feed_out).astype(BF)

    weight_mask = (absorbed[0] * valid_slot.astype(jnp.int32)).astype(F32)
    grad_out = tiled(cotangent[0].astype(F32) * weight_mask[:, None])
    grad_mlp = flat(grad_out * gate_two).astype(BF)
    grad_gate_two = jnp.sum(grad_out * feed_out, axis=1)
    grad_down = linear(hidden_low, grad_mlp, TN).astype(BF)
    grad_up = (linear(grad_mlp, down_low, NT) * gelu_slope(up_values)).astype(BF)
    grad_up_weight = linear(second_low, grad_up, TN).astype(BF)
    grad_second = tiled(linear(grad_up, up_low, NT))
    sum_two = jnp.sum(grad_second, axis=1)
    inner_two = jnp.sum(grad_second * normal_two, axis=1)
    grad_middle = grad_out + normalize_back(grad_second, normal_two, root_two, gain_two * (1.0 + scale_two))
    grad_gate_one = jnp.sum(grad_middle * branch, axis=1)
    grad_branch = flat(grad_middle * gate_one).astype(BF)
    grad_attn_out = linear(attended_low, grad_branch, TN).astype(BF)
    grad_attended = linear(grad_branch, out_low, NT).astype(BF)
    later = reduce_second(grad_attn_out, grad_up_weight, grad_down, chip, core)

    backward = []
    for number, (part, query, key, value, feature) in enumerate(forward):
        width = per_call * PAIR
        grad_part = grad_attended[:, number * width : (number + 1) * width]
        backward.append(attention_backward(query, key, value, feature, feature_key, grad_part, part, cos, sin, per_call))
    grad_mixed = jnp.concatenate([part[kind] for kind in range(3) for part in backward], axis=1)
    grad_qkv = linear(first_low, grad_mixed, TN).astype(BF)
    grad_first = tiled(linear(grad_mixed, qkv_low, NT))
    sum_one = jnp.sum(grad_first, axis=1)
    inner_one = jnp.sum(grad_first * normal_one, axis=1)
    grad_in = flat(grad_middle + normalize_back(grad_first, normal_one, root_one, gain_one * (1.0 + scale_one)))

    tile_grads = jnp.concatenate(
        [sum_one, inner_one * gain_one, grad_gate_one, sum_two, inner_two * gain_two, grad_gate_two], axis=1
    )
    grad_modulation = precise(member_tile, tile_grads, TN)
    grad_mod = precise(grad_modulation, condition_low.astype(F32), TN).astype(BF)
    grad_vectors = jnp.concatenate(
        [
            jnp.sum(inner_one * (1.0 + scale_one[:, 0]), axis=0),
            jnp.sum(inner_two * (1.0 + scale_two[:, 0]), axis=0),
            jnp.sum(grad_up.astype(F32), axis=0),
            jnp.sum(grad_mlp.astype(F32), axis=0),
            jnp.sum(grad_modulation, axis=0),
        ]
    )
    sooner = reduce_first(grad_qkv, grad_mod, grad_vectors, chip, core)

    grads = (sooner[0], later[0], later[1], later[2], sooner[1])
    firsts = (qkv_first, out_first, up_first, down_first, mod_first)
    seconds = (qkv_second, out_second, up_second, down_second, mod_second)
    results = [
        adam_direction(matrices[number], firsts[number], seconds[number], grads[number], DECAY_RATE)
        for number in range(5)
    ]
    update_squares = jnp.stack([jnp.sum(record[2] * record[2]) for record in results])
    norm_roots = jnp.sqrt(sum_over_chips(jnp.stack([weight_squares, update_squares])))
    trust = norm_roots[0] / (norm_roots[1] + EPSILON)
    renewed = [
        matrices[number] - MATRIX_RATE * trust[number] * results[number][2] for number in range(5)
    ]
    vector_record = adam_direction(vectors, vectors_first, vectors_second, sooner[2], 0.0)
    return (
        out_hidden[None],
        grad_in[None],
        *renewed,
        *[record[0] for record in results],
        *[record[1] for record in results],
        vectors - VECTOR_RATE * vector_record[2],
        vector_record[0],
        vector_record[1],
        norm_roots,
    )


def solution(mesh):
    rows = P(("rep", "fsdp"))
    matrix, turned, vector = P("fsdp", None), P(None, "fsdp"), P("fsdp")
    five = (matrix, matrix, matrix, matrix, turned)
    return jax.shard_map(
        on_device,
        mesh=mesh,
        in_specs=(rows,) * 6 + five * 3 + (vector,) * 3,
        out_specs=(rows, rows) + five * 3 + (vector,) * 3 + (P(),),
        check_vma=False,
    )
```

```python
import functools
import math

import jax
import jax.numpy as jnp
import numpy as np
from jax import lax
from jax.experimental import pallas as pl
from jax.experimental.pallas import tpu as pltpu
from jax.sharding import PartitionSpec as P

D = 768
HEADS = 12
HDIM = 64
FF = 3072
COND = 128
SLOTS = 1024
NSEG = 8
STEP = 10
TILE = 128
BLOCKS = SLOTS // TILE

BETA_ONE = 0.9
BETA_TWO = 0.999
EPSILON = 1e-06
DECAY_RATE = 0.01
MATRIX_RATE = 0.3
VECTOR_RATE = 1.0

PAIR = 128
NT = (((1,), (1,)), ((), ()))
NN = (((1,), (0,)), ((), ()))
TN = (((0,), (0,)), ((), ()))
BF = jnp.bfloat16
F32 = jnp.float32


def mm(a, b, dims=NN):
    return lax.dot_general(a, b, dims, preferred_element_type=F32)


def swap_halves(v):
    lane = lax.broadcasted_iota(jnp.int32, v.shape, 1)
    return jnp.where(lane % 64 < 32, pltpu.roll(v, PAIR - 32, 1), pltpu.roll(v, 32, 1))


def attention_forward_kernel(block, q_ref, k_ref, v_ref, cos_ref, sin_ref, fq_ref, fk_ref,
                             o_ref, qr_ref, kr_ref, vr_ref, fo_ref, ka, kb, va, vb):
    slots = q_ref.shape[0]
    low_all = lax.broadcasted_iota(jnp.int32, (slots, PAIR), 1) < 64
    cos, sin = cos_ref[...], sin_ref[...]
    q = q_ref[...]
    k = k_ref[...]
    qr_ref[...] = ((q * cos + swap_halves(q) * sin) * 0.125).astype(BF)
    k_low = (k * cos + swap_halves(k) * sin).astype(BF)
    v_low = v_ref[...].astype(BF)
    kr_ref[...] = k_low
    vr_ref[...] = v_low
    fk = fk_ref[...]
    one = jnp.ones((slots, PAIR), BF)
    ka[...] = jnp.where(low_all, k_low, fk)
    kb[...] = jnp.where(low_all, fk, k_low)
    va[...] = jnp.where(low_all, v_low, one)
    vb[...] = jnp.where(low_all, one, v_low)
    lane = lax.broadcasted_iota(jnp.int32, (block, PAIR), 1)
    low = lane < 64
    spot = lane % 64

    def step(i, carry):
        at = pl.ds(pl.multiple_of(i * block, block), block)
        qb_ = qr_ref[at, :]
        fq = fq_ref[at, :]
        sa = mm(jnp.where(low, qb_, fq), ka[...], NT)
        sb = mm(jnp.where(low, fq, qb_), kb[...], NT)
        ma = jnp.max(sa, axis=1, keepdims=True)
        mb = jnp.max(sb, axis=1, keepdims=True)
        pa = jnp.exp(sa - ma).astype(BF)
        pb = jnp.exp(sb - mb).astype(BF)
        oa = mm(pa, va[...])
        ob = mm(pb, vb[...])
        o = jnp.where(low, oa / pltpu.roll(oa, 64, 1), ob / pltpu.roll(ob, 64, 1))
        o_ref[at, :] = o.astype(o_ref.dtype)
        neg = jnp.where(low, -(mb + jnp.log(ob)), -(ma + jnp.log(oa)))
        hi = neg.astype(BF)
        rest = neg - hi.astype(F32)
        mid = rest.astype(BF)
        last = (rest - mid.astype(F32)).astype(BF)
        fo_ref[at, :] = jnp.where(spot == 8, hi, jnp.where(spot == 9, mid, jnp.where(spot == 10, last, fq)))
        return carry

    lax.fori_loop(0, slots // block, step, 0)


def attention_forward(mixed, cos, sin, fq, fk, first, count, block=256):
    slots, width = mixed.shape
    pairs = width // 3 // PAIR
    blk = lambda off: pl.BlockSpec((slots, PAIR), lambda p: (0, off + p))
    fixed = pl.BlockSpec((slots, PAIR), lambda p: (0, 0))
    out = pl.BlockSpec((slots, PAIR), lambda p: (0, p))
    w = count * PAIR
    elements = 2 * count * slots * slots
    bf = jax.ShapeDtypeStruct((slots, w), BF)
    return pl.pallas_call(
        functools.partial(attention_forward_kernel, block),
        grid=(count,),
        in_specs=[blk(first), blk(pairs + first), blk(2 * pairs + first), fixed, fixed, fixed, fixed],
        out_specs=[out] * 5,
        out_shape=[bf, bf, bf, bf, bf],
        scratch_shapes=[pltpu.VMEM((slots, PAIR), BF)] * 4,
        cost_estimate=pl.CostEstimate(flops=elements * 1000, bytes_accessed=8 * slots * w * 3, transcendentals=elements),
        compiler_params=pltpu.CompilerParams(vmem_limit_bytes=48 * 2**20),
    )(mixed, mixed, mixed, cos, sin, fq, fk)


def attention_backward_kernel(block, qr_ref, kr_ref, vr_ref, fo_ref, fk_ref, do_ref, o_ref, cos_ref, sin_ref,
                              g_ref, ka, kb, va, vb, kt, dka, dkb, dva, dvb):
    slots = qr_ref.shape[0]
    lane_all = lax.broadcasted_iota(jnp.int32, (slots, PAIR), 1)
    low_all = lane_all < 64
    fk = fk_ref[...]
    k_low = kr_ref[...]
    v_low = vr_ref[...]
    one = jnp.where(lane_all % 64 < 2, 1.0, 0.0).astype(BF)
    ka[...] = jnp.where(low_all, k_low, fk)
    kb[...] = jnp.where(low_all, fk, k_low)
    va[...] = jnp.where(low_all, v_low, one)
    vb[...] = jnp.where(low_all, one, v_low)
    kt[...] = k_low.T
    dka[...] = jnp.zeros_like(dka)
    dkb[...] = jnp.zeros_like(dkb)
    dva[...] = jnp.zeros_like(dva)
    dvb[...] = jnp.zeros_like(dvb)
    lane = lax.broadcasted_iota(jnp.int32, (block, PAIR), 1)
    low = lane < 64
    spot = lane % 64
    top = lax.broadcasted_iota(jnp.int32, (PAIR, block), 0) < 64

    def step(i, carry):
        at = pl.ds(pl.multiple_of(i * block, block), block)
        q = qr_ref[at, :]
        fq = fo_ref[at, :]
        do = do_ref[at, :]
        both = do.astype(F32) * o_ref[at, :].astype(F32)
        da = jnp.sum(jnp.where(low, both, 0.0), axis=1, keepdims=True)
        db = jnp.sum(jnp.where(low, 0.0, both), axis=1, keepdims=True)
        neg = jnp.where(low, -db, -da)
        hi = neg.astype(BF)
        rest = (neg - hi.astype(F32)).astype(BF)
        fd = jnp.where(spot == 0, hi, jnp.where(spot == 1, rest, jnp.zeros_like(hi)))
        sa = mm(ka[...], jnp.where(low, q, fq), NT)
        sb = mm(kb[...], jnp.where(low, fq, q), NT)
        ea = mm(va[...], jnp.where(low, do, fd), NT)
        eb = mm(vb[...], jnp.where(low, fd, do), NT)
        pa = jnp.exp(sa)
        pb = jnp.exp(sb)
        dsa = (pa * ea).astype(BF)
        dsb = (pb * eb).astype(BF)
        dva[...] += mm(pa.astype(BF), do)
        dvb[...] += mm(pb.astype(BF), do)
        dka[...] += mm(dsa, q)
        dkb[...] += mm(dsb, q)
        dqt = jnp.where(top, mm(kt[...], dsa), mm(kt[...], dsb))
        dq = dqt.T * 0.125
        g_ref[0, at, :] = (dq * cos_ref[at, :] - swap_halves(dq) * sin_ref[at, :]).astype(BF)
        return carry

    lax.fori_loop(0, slots // block, step, 0)
    dk = jnp.where(low_all, dka[...], dkb[...])
    g_ref[1] = (dk * cos_ref[...] - swap_halves(dk) * sin_ref[...]).astype(BF)
    g_ref[2] = jnp.where(low_all, dva[...], dvb[...]).astype(BF)


def attention_backward(qr, kr, vr, fo, fk, do, o, cos, sin, count, block=256):
    slots, width = qr.shape
    mine = pl.BlockSpec((slots, PAIR), lambda p: (0, p))
    fixed = pl.BlockSpec((slots, PAIR), lambda p: (0, 0))
    w = count * PAIR
    return pl.pallas_call(
        functools.partial(attention_backward_kernel, block),
        grid=(count,),
        in_specs=[mine, mine, mine, mine, fixed, mine, mine, fixed, fixed],
        out_specs=pl.BlockSpec((3, slots, PAIR), lambda p: (0, 0, p)),
        out_shape=jax.ShapeDtypeStruct((3, slots, w), BF),
        scratch_shapes=[pltpu.VMEM((slots, PAIR), BF)] * 4 + [pltpu.VMEM((PAIR, slots), BF)]
        + [pltpu.VMEM((slots, PAIR), F32)] * 4,
        cost_estimate=pl.CostEstimate(
            flops=4 * count * slots * slots * 1000, bytes_accessed=16 * slots * w, transcendentals=2 * count * slots * slots
        ),
        compiler_params=pltpu.CompilerParams(vmem_limit_bytes=48 * 2**20),
    )(qr, kr, vr, fo, fk, do, o, cos, sin)


def attention_tables(segment, position, valid_slot):
    inverse = jnp.exp(jnp.arange(32, dtype=F32) * (-math.log(10000.0) / 32))
    angles = position.astype(F32)[:, None] * inverse[None, :]
    c, s = jnp.cos(angles), jnp.sin(angles)
    cos = jnp.concatenate([c, c, c, c], axis=1)
    sin = jnp.concatenate([-s, s, -s, s], axis=1)
    spot = jnp.arange(PAIR) % 64
    same = segment[:, None] == spot[None, :]
    fq = same.astype(BF)
    fk = jnp.where((spot < 8)[None, :], jnp.where(same & valid_slot[:, None], 0.0, -1e30),
                   jnp.where((spot < 11)[None, :], 1.0, 0.0)).astype(BF)
    return cos, sin, fq, fk


CHIPS = 16
ALONG_X, ALONG_Y, ALONG_Z = (1, 0, 0), (0, 1, 0), (0, 0, 1)
ROUNDS = (
    (((0, 0, 0), ALONG_X), ((0, 0, 0), ALONG_Y), ((0, 0, 0), ALONG_Z)),
    (((0, 1, 0), ALONG_X), ((0, 0, 1), ALONG_Y), ((0, 0, 1), ALONG_Z)),
    (((0, 1, 1), ALONG_X), ((0, 0, 2), ALONG_Y), ((0, 0, 2), ALONG_Z)),
    (((0, 0, 1), ALONG_X), ((0, 0, 3), ALONG_Y), ((1, 1, 1), ALONG_Z)),
    (((0, 0, 3), ALONG_X), ((1, 1, 2), ALONG_Y), ((1, 1, 2), ALONG_Z)),
)
OFFSETS = tuple((a, b, c) for c in range(4) for b in range(2) for a in range(2))


def moved(chip, step, sign=1):
    return ((chip & 1) ^ step[0]) + 2 * (((chip >> 1) & 1) ^ step[1]) + 4 * (((chip >> 2) + sign * step[2]) % 4)


def added(offset, step):
    return (offset[0] ^ step[0], offset[1] ^ step[1], (offset[2] + step[2]) % 4)


ORIGIN = np.array([[moved(chip, offset, -1) for offset in OFFSETS] for chip in range(CHIPS)], np.int32)


def pass_on(values, step, sign=1):
    return lax.ppermute(values, "fsdp", [(chip, moved(chip, step, sign)) for chip in range(CHIPS)])


def swap_core(values):
    return lax.ppermute(values, "rep", [(0, 1), (1, 0)])


def gather_units(unit):
    held = {OFFSETS[0]: unit}
    for round_steps in ROUNDS:
        arrived = [(added(offset, step), pass_on(held[offset], step)) for offset, step in round_steps]
        held.update(arrived)
    return [held[offset] for offset in OFFSETS]


def hold_back(later, sooner):
    return lax.optimization_barrier((later, sooner))


def scatter_start(units, origins):
    return {
        offset: lax.dynamic_index_in_dim(units, origins[place], 0, keepdims=False).astype(F32)
        for place, offset in enumerate(OFFSETS)
    }


def scatter_send(sums, number):
    return [
        (offset, pass_on(sums[added(offset, step)].astype(BF), step, -1)) for offset, step in ROUNDS[4 - number]
    ]


def scatter_add(sums, arrived):
    sums = dict(sums)
    for offset, values in arrived:
        sums[offset] = sums[offset] + values.astype(F32)
    return sums


def sum_small(values):
    for step in (ALONG_X, ALONG_Y, (0, 0, 2)):
        values = values + pass_on(values, step)
    return values + lax.ppermute(values, "fsdp", [(chip, chip ^ 4) for chip in range(CHIPS)])


def place_kernel(plan, count, *refs):
    order_ref, core_ref = refs[:2]
    units = refs[2 : 2 + 2 * CHIPS]
    outs = refs[2 + 2 * CHIPS : -1]
    sems = refs[-1]
    copies = []
    for half in range(2):
        side = core_ref[0] if half == 0 else 1 - core_ref[0]
        for place in range(CHIPS):
            origin = order_ref[place]
            for out, rows, column, width, by_origin, by_side, row, column_side, both in plan:
                if half == 1 and not both:
                    continue
                to_row = pl.multiple_of(origin * by_origin + side * by_side + row, 16)
                to_column = pl.multiple_of(side * column_side, 128) if column_side else 0
                copies.append(
                    pltpu.make_async_copy(
                        units[half * CHIPS + place].at[pl.ds(0, rows), pl.ds(column, width)],
                        outs[out].at[pl.ds(to_row, rows), pl.ds(to_column, width)],
                        sems.at[len(copies)],
                    )
                )
    assert len(copies) == count
    for copy in copies:
        copy.start()
    for copy in copies:
        copy.wait()


def place_units(own, other, order, core, plan, shapes):
    count = sum((2 if piece[-1] else 1) * CHIPS for piece in plan)
    anywhere = pl.BlockSpec(memory_space=pl.ANY)
    scalar = pl.BlockSpec(memory_space=pltpu.SMEM)
    return pl.pallas_call(
        functools.partial(place_kernel, plan, count),
        in_specs=[scalar, scalar] + [anywhere] * (2 * CHIPS),
        out_specs=[pl.BlockSpec(memory_space=pltpu.VMEM)] * len(shapes),
        out_shape=[jax.ShapeDtypeStruct(shape, BF) for shape in shapes],
        scratch_shapes=[pltpu.SemaphoreType.DMA((count,))],
        compiler_params=pltpu.CompilerParams(vmem_limit_bytes=32 * 2**20),
    )(order, core, *own, *other)


SMALL = 128
PLAN_FIRST = (
    (0, 48, 0, 1152, 48, 0, 0, 1152, True),
    (1, 48, 1152, 128, 288, 144, 0, 0, True),
    (1, 48, 1280, 128, 288, 144, 48, 0, True),
    (1, 48, 1408, 128, 288, 144, 96, 0, True),
    (2, 16, 1536, 128, 16, 0, 0, 0, False),
)
PLAN_SECOND = (
    (0, 48, 0, 384, 48, 0, 0, 384, True),
    (1, 48, 384, 1536, 48, 0, 0, 1536, True),
    (2, 48, 1920, 768, 192, 96, 0, 0, True),
    (2, 48, 2688, 768, 192, 96, 48, 0, True),
)


def side_columns(matrix, core, width):
    return lax.dynamic_slice_in_dim(matrix, core * width, width, axis=1)


def side_rows(blocks, core):
    return lax.dynamic_index_in_dim(blocks, core, 1, keepdims=False)


def pack_vectors(rows):
    count = rows.shape[0]
    padded = jnp.pad(rows, ((0, 0), (0, 640 - rows.shape[1]))).reshape(count, 5, 128)
    return jnp.pad(padded, ((0, 0), (0, 43), (0, 0)))


def pack_first(qkv, mod_turned, small, core):
    count = small.shape[0]
    mod_blocks = side_rows(mod_turned.reshape(count, 2, 3, 48, 128), core)
    return jnp.concatenate(
        [
            side_columns(qkv, core, 1152).reshape(count, 48, 1152),
            mod_blocks.transpose(0, 2, 1, 3).reshape(count, 48, 384),
            pack_vectors(small),
        ],
        axis=2,
    )


def pack_second(out, up, down, core):
    count = out.shape[0] // 48
    down_blocks = side_rows(down.reshape(count, 2, 2, 48, D), core)
    return jnp.concatenate(
        [
            side_columns(out, core, 384).reshape(count, 48, 384),
            side_columns(up, core, 1536).reshape(count, 48, 1536),
            down_blocks.transpose(0, 2, 1, 3).reshape(count, 48, 2 * D),
        ],
        axis=2,
    )


def gather_first(qkv, mod, vectors, chip, core):
    if lax.axis_size("fsdp") != CHIPS:
        return (
            lax.all_gather(qkv, "fsdp", axis=0, tiled=True),
            lax.all_gather(mod, "fsdp", axis=1, tiled=True).T,
            lax.all_gather(vectors, "fsdp", axis=0, tiled=True),
        )
    unit = pack_first(qkv, mod.T, vectors[None], core)[0]
    own = gather_units(unit)
    other = [swap_core(one) for one in own]
    qkv_all, mod_all, small = place_units(
        own, other, jnp.asarray(ORIGIN)[chip], core[None], PLAN_FIRST, ((D, 3 * D), (6 * D, COND), (256, 128))
    )
    return (qkv_all, mod_all, small.reshape(CHIPS, 2048)[:, :624].reshape(-1))


def gather_second(out, up, down, chip, core):
    if lax.axis_size("fsdp") != CHIPS:
        return tuple(lax.all_gather(part, "fsdp", axis=0, tiled=True) for part in (out, up, down))
    own = gather_units(pack_second(out, up, down, core)[0])
    other = [swap_core(one) for one in own]
    return place_units(
        own, other, jnp.asarray(ORIGIN)[chip], core[None], PLAN_SECOND, ((D, D), (D, FF), (FF, D))
    )


def reduce_packed(pack, chip, core, waiting=()):
    arrived = swap_core(pack(1 - core).astype(BF))
    units = (pack(core).astype(F32) + arrived.astype(F32)).astype(BF)
    sums = scatter_start(units, jnp.asarray(ORIGIN)[chip])
    came = None
    for number in range(5):
        sent = scatter_send(sums, number)
        if number < len(waiting):
            waiting[number](came)
        came = [values for _, values in sent]
        sums = scatter_add(sums, sent)
    for rest in waiting[5:]:
        rest(came)
        came = None
    mine = sums[OFFSETS[0]].astype(BF)
    other = swap_core(mine)
    first = jnp.where(core == 0, mine, other).astype(F32)
    second = jnp.where(core == 0, other, mine).astype(F32)
    return (first, second)


def reduce_plain(grad, axis):
    part = lax.psum_scatter(grad.astype(F32), "fsdp", scatter_dimension=axis, tiled=True)
    return lax.psum(part.astype(BF), "rep").astype(F32)


def reduce_first(qkv, mod_turned, vectors, chip, core):
    if lax.axis_size("fsdp") != CHIPS:
        return (reduce_plain(qkv, 0), reduce_plain(mod_turned.T, 1), reduce_plain(vectors, 0))
    small = vectors.reshape(CHIPS, -1)
    first, second = reduce_packed(lambda side: pack_first(qkv, mod_turned, small.astype(BF), side), chip, core)
    turned = jnp.concatenate(
        [half[:, 1152 + 128 * part : 1280 + 128 * part] for half in (first, second) for part in range(3)], axis=0
    )
    return (
        jnp.concatenate([first[:, :1152], second[:, :1152]], axis=1),
        turned.T,
        first[:5, 1536:].reshape(-1)[:624],
    )


def reduce_second(out, up, down, chip, core, waiting):
    if lax.axis_size("fsdp") != CHIPS:
        for rest in waiting:
            rest(None)
        return (reduce_plain(out, 0), reduce_plain(up, 0), reduce_plain(down, 0))
    first, second = reduce_packed(lambda side: pack_second(out, up, down, side), chip, core, waiting)
    return (
        jnp.concatenate([first[:, :384], second[:, :384]], axis=1),
        jnp.concatenate([first[:, 384:1920], second[:, 384:1920]], axis=1),
        jnp.concatenate([half[:, 1920 + D * part : 2688 + D * part] for half in (first, second) for part in range(2)], axis=0),
    )


def sum_over_chips(values):
    if lax.axis_size("fsdp") != CHIPS:
        return lax.psum(values, "fsdp")
    return sum_small(values)


def linear(left_side, right_side, dims=NN):
    return lax.dot_general(left_side, right_side, dims, preferred_element_type=F32)


def precise(left_side, right_side, dims=NN):
    return lax.dot_general(
        left_side, right_side, dims, precision=lax.Precision.HIGHEST, preferred_element_type=F32
    )


def layout_tables(sizes_row, lengths_row):
    slot_ids = jnp.arange(SLOTS, dtype=jnp.int32)
    seg_ends = jnp.cumsum(sizes_row)
    starts = seg_ends - sizes_row
    segment = jnp.sum((slot_ids[:, None] >= seg_ends[None, :]).astype(jnp.int32), axis=1)
    member = segment[:, None] == jnp.arange(NSEG, dtype=jnp.int32)[None, :]
    offset = jnp.sum(jnp.where(member, starts[None, :], 0), axis=1)
    length_of = jnp.sum(jnp.where(member, lengths_row[None, :], 0), axis=1)
    position = slot_ids - offset
    return (segment, member, position, position < length_of)


def condition(steps_row):
    half_cond = COND // 2
    frequency = jnp.exp(jnp.arange(half_cond, dtype=F32) * (-math.log(10000.0) / half_cond))
    angles = steps_row.astype(F32)[:, None] * frequency[None, :]
    return jax.nn.silu(jnp.concatenate([jnp.cos(angles), jnp.sin(angles)], axis=1))


def normalize(values):
    average = jnp.mean(values, axis=-1, keepdims=True)
    centered = values - average
    root = lax.rsqrt(jnp.mean(centered * centered, axis=-1, keepdims=True) + 1e-05)
    return (centered * root, root)


def normalize_back(grad, normal, root, gain):
    scaled = grad * gain
    inner = jnp.mean(scaled * normal, axis=-1, keepdims=True)
    return root * (scaled - jnp.mean(scaled, axis=-1, keepdims=True) - normal * inner)


def gelu_slope(values):
    factor = math.sqrt(2.0 / math.pi)
    square = values * values
    bent = jnp.tanh(factor * values * (1.0 + 0.044715 * square))
    return 0.5 * (1.0 + bent) + 0.5 * values * (1.0 - bent * bent) * factor * (1.0 + 3 * 0.044715 * square)


def tiled(values):
    return values.reshape(BLOCKS, TILE, values.shape[-1])


def flat(values):
    return values.reshape(SLOTS, values.shape[-1])


def adam_direction(weight, first_old, second_old, gradient, decay_rate):
    first_new = BETA_ONE * first_old + (1.0 - BETA_ONE) * gradient
    second_new = BETA_TWO * second_old + (1.0 - BETA_TWO) * gradient * gradient
    direction = (
        first_new
        / (1.0 - BETA_ONE**STEP)
        / (jnp.sqrt(second_new / (1.0 - BETA_TWO**STEP)) + EPSILON)
        + decay_rate * weight
    )
    return (first_new, second_new, direction)


GROUPS = 6


def on_device(
    inputs, cotangent, seg_sizes, seq_lengths, timesteps, absorbed,
    qkv_weight, out_weight, up_weight, down_weight, mod_weight,
    qkv_first, out_first, up_first, down_first, mod_first,
    qkv_second, out_second, up_second, down_second, mod_second,
    vectors, vectors_first, vectors_second,
):
    chip = lax.axis_index("fsdp")
    core = lax.axis_index("rep")
    matrices = (qkv_weight, out_weight, up_weight, down_weight, mod_weight)
    weight_squares = jnp.stack([jnp.sum(matrix * matrix) for matrix in matrices])
    low = [matrix.astype(BF) for matrix in matrices]
    qkv_low, mod_turned, vector_low = gather_first(low[0], low[4], vectors.astype(BF), chip, core)
    low[1:4], (qkv_low, mod_turned, vector_low) = hold_back(low[1:4], (qkv_low, mod_turned, vector_low))
    out_low, up_low, down_low = gather_second(low[1], low[2], low[3], chip, core)

    vector_all = vector_low.astype(F32)
    gain_one, gain_two = vector_all[:D], vector_all[D : 2 * D]
    bias_up = vector_all[2 * D : 2 * D + FF]
    bias_down = vector_all[2 * D + FF : 3 * D + FF]
    bias_mod = vector_all[3 * D + FF :]

    segment, member, position, valid_slot = layout_tables(seg_sizes[0], seq_lengths[0])
    member_tile = member.reshape(BLOCKS, TILE, NSEG)[:, 0].astype(F32)
    condition_low = condition(timesteps[0]).astype(BF)
    modulation = linear(condition_low, mod_turned, NT) + bias_mod
    per_tile = precise(member_tile, modulation)[:, None, :]
    shift_one, scale_one, gate_one, shift_two, scale_two, gate_two = jnp.split(per_tile, 6, axis=2)
    cos, sin, feature_query, feature_key = attention_tables(segment, position, valid_slot)

    wide = tiled(inputs[0].astype(F32))
    normal_one, root_one = normalize(wide)
    first_low = flat(normal_one * gain_one * (1.0 + scale_one) + shift_one).astype(BF)
    mixed = linear(first_low, qkv_low)
    per_call = HEADS // 2 // GROUPS
    forward = [
        attention_forward(mixed, cos, sin, feature_query, feature_key, number * per_call, per_call)
        for number in range(GROUPS)
    ]
    attended_low = jnp.concatenate([part[0] for part in forward], axis=1)
    branch = tiled(linear(attended_low, out_low))
    middle = wide + gate_one * branch
    normal_two, root_two = normalize(middle)
    second_low = flat(normal_two * gain_two * (1.0 + scale_two) + shift_two).astype(BF)
    up_values = linear(second_low, up_low) + bias_up
    hidden_low = jax.nn.gelu(up_values, approximate=True).astype(BF)
    feed_out = tiled(linear(hidden_low, down_low) + bias_down)
    out_hidden = flat(middle + gate_two * feed_out).astype(BF)

    weight_mask = (absorbed[0] * valid_slot.astype(jnp.int32)).astype(F32)
    grad_out = tiled(cotangent[0].astype(F32) * weight_mask[:, None])
    grad_mlp = flat(grad_out * gate_two).astype(BF)
    grad_gate_two = jnp.sum(grad_out * feed_out, axis=1)
    grad_down = linear(hidden_low, grad_mlp, TN).astype(BF)
    grad_up = (linear(grad_mlp, down_low, NT) * gelu_slope(up_values)).astype(BF)
    grad_up_weight = linear(second_low, grad_up, TN).astype(BF)
    grad_second = tiled(linear(grad_up, up_low, NT))
    sum_two = jnp.sum(grad_second, axis=1)
    inner_two = jnp.sum(grad_second * normal_two, axis=1)
    grad_middle = grad_out + normalize_back(grad_second, normal_two, root_two, gain_two * (1.0 + scale_two))
    grad_gate_one = jnp.sum(grad_middle * branch, axis=1)
    grad_branch = flat(grad_middle * gate_one).astype(BF)
    grad_attn_out = linear(attended_low, grad_branch, TN).astype(BF)
    grad_attended = linear(grad_branch, out_low, NT).astype(BF)
    backward = []

    def backward_part(number, came):
        part, query, key, value, feature = forward[number]
        width = per_call * PAIR
        grad_part = grad_attended[:, number * width : (number + 1) * width]
        if came is not None:
            grad_part, _ = hold_back(grad_part, came)
        backward.append(attention_backward(query, key, value, feature, feature_key, grad_part, part, cos, sin, per_call))

    later = reduce_second(
        grad_attn_out, grad_up_weight, grad_down, chip, core,
        [functools.partial(backward_part, number) for number in range(GROUPS)],
    )
    grad_mixed = jnp.concatenate([part[kind] for kind in range(3) for part in backward], axis=1)
    grad_qkv = linear(first_low, grad_mixed, TN).astype(BF)
    grad_first = tiled(linear(grad_mixed, qkv_low, NT))
    sum_one = jnp.sum(grad_first, axis=1)
    inner_one = jnp.sum(grad_first * normal_one, axis=1)
    grad_in = flat(grad_middle + normalize_back(grad_first, normal_one, root_one, gain_one * (1.0 + scale_one)))

    tile_grads = jnp.concatenate(
        [sum_one, inner_one * gain_one, grad_gate_one, sum_two, inner_two * gain_two, grad_gate_two], axis=1
    )
    grad_modulation = precise(member_tile, tile_grads, TN)
    grad_mod = precise(grad_modulation, condition_low.astype(F32), TN).astype(BF)
    grad_vectors = jnp.concatenate(
        [
            jnp.sum(inner_one * (1.0 + scale_one[:, 0]), axis=0),
            jnp.sum(inner_two * (1.0 + scale_two[:, 0]), axis=0),
            jnp.sum(grad_up.astype(F32), axis=0),
            jnp.sum(grad_mlp.astype(F32), axis=0),
            jnp.sum(grad_modulation, axis=0),
        ]
    )
    sooner = reduce_first(grad_qkv, grad_mod, grad_vectors, chip, core)

    grads = (sooner[0], later[0], later[1], later[2], sooner[1])
    firsts = (qkv_first, out_first, up_first, down_first, mod_first)
    seconds = (qkv_second, out_second, up_second, down_second, mod_second)
    results = [
        adam_direction(matrices[number], firsts[number], seconds[number], grads[number], DECAY_RATE)
        for number in range(5)
    ]
    update_squares = jnp.stack([jnp.sum(record[2] * record[2]) for record in results])
    norm_roots = jnp.sqrt(sum_over_chips(jnp.stack([weight_squares, update_squares])))
    trust = norm_roots[0] / (norm_roots[1] + EPSILON)
    renewed = [
        matrices[number] - MATRIX_RATE * trust[number] * results[number][2] for number in range(5)
    ]
    vector_record = adam_direction(vectors, vectors_first, vectors_second, sooner[2], 0.0)
    return (
        out_hidden[None],
        grad_in[None],
        *renewed,
        *[record[0] for record in results],
        *[record[1] for record in results],
        vectors - VECTOR_RATE * vector_record[2],
        vector_record[0],
        vector_record[1],
        norm_roots,
    )


def solution(mesh):
    rows = P(("rep", "fsdp"))
    matrix, turned, vector = P("fsdp", None), P(None, "fsdp"), P("fsdp")
    five = (matrix, matrix, matrix, matrix, turned)
    return jax.shard_map(
        on_device,
        mesh=mesh,
        in_specs=(rows,) * 6 + five * 3 + (vector,) * 3,
        out_specs=(rows, rows) + five * 3 + (vector,) * 3 + (P(),),
        check_vma=False,
    )
```

```python
import functools
import math

import jax
import jax.numpy as jnp
import numpy as np
from jax import lax
from jax.experimental import pallas as pl
from jax.experimental.pallas import tpu as pltpu
from jax.sharding import PartitionSpec as P

D = 768
HEADS = 12
HDIM = 64
FF = 3072
COND = 128
SLOTS = 1024
NSEG = 8
STEP = 10
TILE = 128
BLOCKS = SLOTS // TILE

BETA_ONE = 0.9
BETA_TWO = 0.999
EPSILON = 1e-06
DECAY_RATE = 0.01
MATRIX_RATE = 0.3
VECTOR_RATE = 1.0

PAIR = 128
NT = (((1,), (1,)), ((), ()))
NN = (((1,), (0,)), ((), ()))
TN = (((0,), (0,)), ((), ()))
BF = jnp.bfloat16
F32 = jnp.float32


def mm(a, b, dims=NN):
    return lax.dot_general(a, b, dims, preferred_element_type=F32)


def swap_halves(v):
    lane = lax.broadcasted_iota(jnp.int32, v.shape, 1)
    return jnp.where(lane % 64 < 32, pltpu.roll(v, PAIR - 32, 1), pltpu.roll(v, 32, 1))


def attention_forward_kernel(block, q_ref, k_ref, v_ref, fq_ref, fk_ref, *refs):
    o_ref, fo_ref, ka, kb, va, vb = refs[-6:]
    slots = q_ref.shape[0]
    low_all = lax.broadcasted_iota(jnp.int32, (slots, PAIR), 1) < 64
    k_low = k_ref[...]
    v_low = v_ref[...]
    fk = fk_ref[...]
    one = jnp.ones((slots, PAIR), BF)
    ka[...] = jnp.where(low_all, k_low, fk)
    kb[...] = jnp.where(low_all, fk, k_low)
    va[...] = jnp.where(low_all, v_low, one)
    vb[...] = jnp.where(low_all, one, v_low)
    lane = lax.broadcasted_iota(jnp.int32, (block, PAIR), 1)
    low = lane < 64
    spot = lane % 64

    def step(i, carry):
        at = pl.ds(pl.multiple_of(i * block, block), block)
        q = q_ref[at, :]
        fq = fq_ref[at, :]
        sa = mm(jnp.where(low, q, fq), ka[...], NT)
        sb = mm(jnp.where(low, fq, q), kb[...], NT)
        ma = jnp.max(sa, axis=1, keepdims=True)
        mb = jnp.max(sb, axis=1, keepdims=True)
        pa = jnp.exp(sa - ma).astype(BF)
        pb = jnp.exp(sb - mb).astype(BF)
        oa = mm(pa, va[...])
        ob = mm(pb, vb[...])
        o = jnp.where(low, oa / pltpu.roll(oa, 64, 1), ob / pltpu.roll(ob, 64, 1))
        o_ref[at, :] = o.astype(o_ref.dtype)
        neg = jnp.where(low, -(mb + jnp.log(ob)), -(ma + jnp.log(oa)))
        hi = neg.astype(BF)
        rest = neg - hi.astype(F32)
        mid = rest.astype(BF)
        last = (rest - mid.astype(F32)).astype(BF)
        fo_ref[at, :] = jnp.where(spot == 8, hi, jnp.where(spot == 9, mid, jnp.where(spot == 10, last, fq)))
        return carry

    lax.fori_loop(0, slots // block, step, 0)


def attention_forward(qkv, fq, fk, before, first, count, block=256):
    slots, width = qkv.shape
    pairs = width // 3 // PAIR
    blk = lambda off: pl.BlockSpec((slots, PAIR), lambda p: (0, off + p))
    fixed = pl.BlockSpec((slots, PAIR), lambda p: (0, 0))
    anywhere = pl.BlockSpec(memory_space=pl.ANY)
    shape = jax.ShapeDtypeStruct((slots, pairs * PAIR), BF)
    extra = () if before is None else before
    elements = 2 * count * slots * slots
    return pl.pallas_call(
        functools.partial(attention_forward_kernel, block),
        grid=(count,),
        in_specs=[blk(first), blk(pairs + first), blk(2 * pairs + first), fixed, fixed] + [anywhere] * len(extra),
        out_specs=[blk(first)] * 2,
        out_shape=[shape, shape],
        scratch_shapes=[pltpu.VMEM((slots, PAIR), BF)] * 4,
        input_output_aliases={5: 0, 6: 1} if extra else {},
        cost_estimate=pl.CostEstimate(flops=elements * 1000, bytes_accessed=10 * slots * count * PAIR, transcendentals=elements),
        compiler_params=pltpu.CompilerParams(vmem_limit_bytes=48 * 2**20),
    )(qkv, qkv, qkv, fq, fk, *extra)


def attention_backward_kernel(block, q_ref, k_ref, v_ref, fo_ref, fk_ref, do_ref, o_ref, cos_ref, sin_ref, *refs):
    g_ref, ka, kb, va, vb, kt, dka, dkb, dva, dvb = refs[-10:]
    slots = q_ref.shape[0]
    lane_all = lax.broadcasted_iota(jnp.int32, (slots, PAIR), 1)
    low_all = lane_all < 64
    fk = fk_ref[...]
    k_low = k_ref[...]
    v_low = v_ref[...]
    one = jnp.where(lane_all % 64 < 2, 1.0, 0.0).astype(BF)
    ka[...] = jnp.where(low_all, k_low, fk)
    kb[...] = jnp.where(low_all, fk, k_low)
    va[...] = jnp.where(low_all, v_low, one)
    vb[...] = jnp.where(low_all, one, v_low)
    kt[...] = k_low.T
    dka[...] = jnp.zeros_like(dka)
    dkb[...] = jnp.zeros_like(dkb)
    dva[...] = jnp.zeros_like(dva)
    dvb[...] = jnp.zeros_like(dvb)
    lane = lax.broadcasted_iota(jnp.int32, (block, PAIR), 1)
    low = lane < 64
    spot = lane % 64
    top = lax.broadcasted_iota(jnp.int32, (PAIR, block), 0) < 64

    def step(i, carry):
        at = pl.ds(pl.multiple_of(i * block, block), block)
        q = q_ref[at, :]
        fq = fo_ref[at, :]
        do = do_ref[at, :]
        both = do.astype(F32) * o_ref[at, :].astype(F32)
        da = jnp.sum(jnp.where(low, both, 0.0), axis=1, keepdims=True)
        db = jnp.sum(jnp.where(low, 0.0, both), axis=1, keepdims=True)
        neg = jnp.where(low, -db, -da)
        hi = neg.astype(BF)
        rest = (neg - hi.astype(F32)).astype(BF)
        fd = jnp.where(spot == 0, hi, jnp.where(spot == 1, rest, jnp.zeros_like(hi)))
        sa = mm(ka[...], jnp.where(low, q, fq), NT)
        sb = mm(kb[...], jnp.where(low, fq, q), NT)
        ea = mm(va[...], jnp.where(low, do, fd), NT)
        eb = mm(vb[...], jnp.where(low, fd, do), NT)
        pa = jnp.exp(sa)
        pb = jnp.exp(sb)
        dsa = (pa * ea).astype(BF)
        dsb = (pb * eb).astype(BF)
        dva[...] += mm(pa.astype(BF), do)
        dvb[...] += mm(pb.astype(BF), do)
        dka[...] += mm(dsa, q)
        dkb[...] += mm(dsb, q)
        dqt = jnp.where(top, mm(kt[...], dsa), mm(kt[...], dsb))
        dq = dqt.T * 0.125
        g_ref[0, at, :] = (dq * cos_ref[at, :] - swap_halves(dq) * sin_ref[at, :]).astype(BF)
        return carry

    lax.fori_loop(0, slots // block, step, 0)
    dk = jnp.where(low_all, dka[...], dkb[...])
    g_ref[1] = (dk * cos_ref[...] - swap_halves(dk) * sin_ref[...]).astype(BF)
    g_ref[2] = jnp.where(low_all, dva[...], dvb[...]).astype(BF)


def attention_backward(qkv, fo, fk, do, o, cos, sin, before, first, count, block=256):
    slots, width = qkv.shape
    pairs = width // 3 // PAIR
    blk = lambda off: pl.BlockSpec((slots, PAIR), lambda p: (0, off + p))
    fixed = pl.BlockSpec((slots, PAIR), lambda p: (0, 0))
    extra = () if before is None else (before,)
    elements = 2 * count * slots * slots
    return pl.pallas_call(
        functools.partial(attention_backward_kernel, block),
        grid=(count,),
        in_specs=[blk(first), blk(pairs + first), blk(2 * pairs + first), blk(first), fixed, blk(first), blk(first),
                  fixed, fixed] + [pl.BlockSpec(memory_space=pl.ANY)] * len(extra),
        out_specs=pl.BlockSpec((3, slots, PAIR), lambda p: (0, 0, first + p)),
        out_shape=jax.ShapeDtypeStruct((3, slots, pairs * PAIR), BF),
        scratch_shapes=[pltpu.VMEM((slots, PAIR), BF)] * 4 + [pltpu.VMEM((PAIR, slots), BF)]
        + [pltpu.VMEM((slots, PAIR), F32)] * 4,
        input_output_aliases={9: 0} if extra else {},
        cost_estimate=pl.CostEstimate(flops=elements * 2000, bytes_accessed=20 * slots * count * PAIR, transcendentals=elements),
        compiler_params=pltpu.CompilerParams(vmem_limit_bytes=48 * 2**20),
    )(qkv, qkv, qkv, fo, fk, do, o, cos, sin, *extra)


def attention_tables(segment, position, valid_slot):
    inverse = jnp.exp(jnp.arange(32, dtype=F32) * (-math.log(10000.0) / 32))
    angles = position.astype(F32)[:, None] * inverse[None, :]
    c, s = jnp.cos(angles), jnp.sin(angles)
    cos = jnp.concatenate([c, c, c, c], axis=1)
    sin = jnp.concatenate([-s, s, -s, s], axis=1)
    spot = jnp.arange(PAIR) % 64
    same = segment[:, None] == spot[None, :]
    fq = same.astype(BF)
    fk = jnp.where((spot < 8)[None, :], jnp.where(same & valid_slot[:, None], 0.0, -1e30),
                   jnp.where((spot < 11)[None, :], 1.0, 0.0)).astype(BF)
    return cos, sin, fq, fk


UNITS = 16
QKV_HALF = 3 * D // 2
FIRST_WIDE = QKV_HALF + 3 * COND + 128
UP_AT, DOWN_AT, OUT_AT, SECOND_WIDE = 0, FF // 2, FF // 2 + 2 * D, FF // 2 + 2 * D + D // 2
VECTOR_PART = (9 * D + FF) // UNITS
FLAT_ROWS = 80
HBM = pltpu.HBM
SMALL_VMEM = pl.BlockSpec(memory_space=pltpu.SMEM)


def whole(shape):
    return pl.BlockSpec(shape, lambda *_: (0,) * len(shape))


def line(flat_ref, start, count):
    return jnp.concatenate([flat_ref[start + i : start + i + 1, :] for i in range(count)], axis=1)


def unit_copies(units, order, core, sems, plan, first_sem):
    copies = []
    for half in range(2):
        side = core if half == 0 else 1 - core
        for place in range(UNITS):
            origin = order[place]
            for target, rows, column, width, by_origin, by_side, row, column_side, both in plan:
                if half == 1 and not both:
                    continue
                to_row = pl.multiple_of(origin * by_origin + side * by_side + row, 16)
                to_column = pl.multiple_of(side * column_side, 128) if column_side else 0
                copies.append(
                    pltpu.make_async_copy(
                        units[half * UNITS + place].at[pl.ds(0, rows), pl.ds(column, width)],
                        target.at[pl.ds(to_row, rows), pl.ds(to_column, width)],
                        sems.at[first_sem + len(copies)],
                    )
                )
    return copies


def layer_norm(values):
    average = jnp.mean(values, axis=-1, keepdims=True)
    centered = values - average
    root = lax.rsqrt(jnp.mean(centered * centered, axis=-1, keepdims=True) + 1e-05)
    return (centered * root, root)


def layer_norm_back(grad, normal, root, gain):
    scaled = grad * gain
    inner = jnp.mean(scaled * normal, axis=-1, keepdims=True)
    return root * (scaled - jnp.mean(scaled, axis=-1, keepdims=True) - normal * inner)


def first_kernel(rows, order_ref, core_ref, tiles_ref, *refs):
    units = refs[: 2 * UNITS]
    x_ref, cond_ref, cos_ref, sin_ref, qkv_ref, first_ref, w_ref, mod_ref, flat_ref, modt, vecs, sems = refs[2 * UNITS :]
    step = pl.program_id(0)

    @pl.when(step == 0)
    def _():
        core = core_ref[0]
        small = unit_copies(units, order_ref, core, sems, (
            (vecs, 16, QKV_HALF + 3 * COND, 128, 16, 0, 0, 0, False),
            (modt, 48, QKV_HALF, 128, 288, 144, 0, 0, True),
            (modt, 48, QKV_HALF + 128, 128, 288, 144, 48, 0, True),
            (modt, 48, QKV_HALF + 256, 128, 288, 144, 96, 0, True),
        ), 0)
        large = unit_copies(units, order_ref, core, sems, (
            (w_ref, 48, 0, QKV_HALF, 48, 0, 0, QKV_HALF, True),
        ), len(small))
        for copy in small + large:
            copy.start()
        for copy in small:
            copy.wait()
        flat_ref[...] = jnp.zeros_like(flat_ref)
        lane = lax.broadcasted_iota(jnp.int32, (8, 128), 1)
        for part in range(UNITS):
            row, turn = divmod(VECTOR_PART * part, 128)
            piece = vecs[16 * part : 16 * part + 16, :].astype(F32)[:8]
            if turn:
                piece = pltpu.roll(piece, turn, 1)
                flat_ref[row + 1 : row + 6, :] += jnp.where(lane < turn, piece, 0.0)[:5]
                piece = jnp.where(lane >= turn, piece, 0.0)
            flat_ref[row : row + 5, :] += piece[:5]
        mod_ref[...] = mm(cond_ref[...], modt[...], NT) + line(flat_ref, (3 * D + FF) // 128, 6 * D // 128)
        for copy in large:
            copy.wait()

    gain = line(flat_ref, 0, D // 128)
    for part in range(rows // TILE):
        at = pl.ds(part * TILE, TILE)
        segment = tiles_ref[step * (rows // TILE) + part]
        normal, _ = layer_norm(x_ref[at, :].astype(F32))
        shift = mod_ref[pl.ds(segment, 1), 0:D]
        scale = mod_ref[pl.ds(segment, 1), D : 2 * D]
        first_ref[at, :] = (normal * (gain * (1.0 + scale)) + shift).astype(BF)
    first = first_ref[...]
    cos, sin = cos_ref[...], sin_ref[...]
    for kind in range(3):
        mixed = mm(first, w_ref[:, kind * D : (kind + 1) * D])
        if kind < 2:
            for pair in range(D // PAIR):
                part = mixed[:, pair * PAIR : (pair + 1) * PAIR]
                turned = part * cos + swap_halves(part) * sin
                if kind == 0:
                    turned = turned * HDIM ** (-0.5)
                qkv_ref[:, kind * D + pair * PAIR : kind * D + (pair + 1) * PAIR] = turned.astype(BF)
        else:
            qkv_ref[:, 2 * D :] = mixed.astype(BF)


def first_part(units, order, core, tiles, x, cond, cos, sin, rows=256):
    count = UNITS * (1 + 2 * 3 + 2)
    row = lambda width: pl.BlockSpec((rows, width), lambda i: (i, 0))
    shape = lambda s, t: jax.ShapeDtypeStruct(s, t)
    return pl.pallas_call(
        functools.partial(first_kernel, rows),
        grid=(SLOTS // rows,),
        in_specs=[SMALL_VMEM] * 3 + [pl.BlockSpec(memory_space=HBM)] * (2 * UNITS)
        + [row(D), whole((NSEG, COND)), row(PAIR), row(PAIR)],
        out_specs=[row(3 * D), row(D), whole((D, 3 * D)), whole((NSEG, 6 * D)), whole((FLAT_ROWS, 128))],
        out_shape=[shape((SLOTS, 3 * D), BF), shape((SLOTS, D), BF), shape((D, 3 * D), BF),
                   shape((NSEG, 6 * D), F32), shape((FLAT_ROWS, 128), F32)],
        scratch_shapes=[pltpu.VMEM((6 * D, COND), BF), pltpu.VMEM((16 * UNITS, 128), BF), pltpu.SemaphoreType.DMA((count,))],
        cost_estimate=pl.CostEstimate(flops=2 * SLOTS * D * 3 * D, bytes_accessed=20 * 2**20, transcendentals=SLOTS),
        compiler_params=pltpu.CompilerParams(vmem_limit_bytes=56 * 2**20),
    )(order, core, tiles, *units, x, cond, cos, sin)


def middle_kernel(rows, order_ref, core_ref, tiles_ref, *refs):
    units = refs[: 2 * UNITS]
    (att_ref, x_ref, cot_ref, mask_ref, mod_ref, flat_ref,
     out_ref, left_ref, right_ref, gmid_ref, gatt_ref, sums_ref, bias_ref,
     wo, wu, wd, slope, branch_s, middle_s, sems) = refs[2 * UNITS :]
    step = pl.program_id(0)
    core = core_ref[0]
    chunks = FF // D
    tiles = rows // TILE
    each = 2 * UNITS
    copies = [
        unit_copies(units, order_ref, core, sems, ((wo, 48, OUT_AT, D // 2, 48, 0, 0, D // 2, True),), 0),
        unit_copies(units, order_ref, core, sems, ((wu, 48, UP_AT, FF // 2, 48, 0, 0, FF // 2, True),), each),
        unit_copies(units, order_ref, core, sems, (
            (wd, 48, DOWN_AT, D, 192, 96, 0, 0, True),
            (wd, 48, DOWN_AT + D, D, 192, 96, 48, 0, True),
        ), 2 * each),
    ]

    @pl.when(step == 0)
    def _():
        for group in copies:
            for copy in group:
                copy.start()
        bias_ref[...] = jnp.zeros_like(bias_ref)
        for copy in copies[0]:
            copy.wait()

    def table(part, kind):
        return mod_ref[pl.ds(tiles_ref[step * tiles + part], 1), kind * D : (kind + 1) * D]

    att = att_ref[...]
    left_ref[:, FF + D :] = att
    branch_s[...] = mm(att, wo[...])
    gain = line(flat_ref, D // 128, D // 128)
    for part in range(tiles):
        at = pl.ds(part * TILE, TILE)
        middle = x_ref[at, :].astype(F32) + table(part, 2) * branch_s[at, :]
        middle_s[at, :] = middle
        normal, _ = layer_norm(middle)
        left_ref[at, FF : FF + D] = (normal * (gain * (1.0 + table(part, 4))) + table(part, 3)).astype(BF)

    @pl.when(step == 0)
    def _():
        for group in copies[1:]:
            for copy in group:
                copy.wait()

    second = left_ref[:, FF : FF + D]
    factor = math.sqrt(2.0 / math.pi)
    feed = None
    for j in range(chunks):
        at = pl.ds(j * D, D)
        u = mm(second, wu[:, at]) + line(flat_ref, 2 * D // 128 + j * (D // 128), D // 128)
        square = u * u
        bent = jnp.tanh(u * (factor + (factor * 0.044715) * square))
        half = 0.5 * u
        bow = half * bent
        hidden = (half + bow).astype(BF)
        left_ref[:, at] = hidden
        slope[:, at] = (0.5 + 0.5 * bent) + (half - bow * bent) * (factor + (3 * factor * 0.044715) * square)
        share = mm(hidden, wd[at, :])
        feed = share if feed is None else feed + share
    bias_down = line(flat_ref, (2 * D + FF) // 128, D // 128)
    for part in range(tiles):
        at = pl.ds(part * TILE, TILE)
        gate = table(part, 5)
        feed_out = feed[part * TILE : (part + 1) * TILE] + bias_down
        out_ref[at, :] = (middle_s[at, :] + gate * feed_out).astype(BF)
        grad_out = cot_ref[at, :].astype(F32) * mask_ref[at, :]
        sums_ref[part, 3:4, :] = jnp.sum(grad_out * feed_out, axis=0, keepdims=True)
        grad_mlp = (grad_out * gate).astype(BF)
        right_ref[at, 0:D] = grad_mlp
        bias_ref[0:1, FF:] += jnp.sum(grad_mlp.astype(F32), axis=0, keepdims=True)
    grad_mlp = right_ref[:, 0:D]
    grad_second = None
    for j in range(chunks):
        at = pl.ds(j * D, D)
        grad_up = (mm(grad_mlp, wd[at, :], NT) * slope[:, at]).astype(BF)
        right_ref[:, D + j * D : 2 * D + j * D] = grad_up
        bias_ref[0:1, at] += jnp.sum(grad_up.astype(F32), axis=0, keepdims=True)
        share = mm(grad_up, wu[:, at], NT)
        grad_second = share if grad_second is None else grad_second + share
    for part in range(tiles):
        at = pl.ds(part * TILE, TILE)
        normal, root = layer_norm(middle_s[at, :])
        grad = grad_second[part * TILE : (part + 1) * TILE]
        sums_ref[part, 1:2, :] = jnp.sum(grad, axis=0, keepdims=True)
        sums_ref[part, 2:3, :] = jnp.sum(grad * normal, axis=0, keepdims=True)
        grad_middle = cot_ref[at, :].astype(F32) * mask_ref[at, :] + layer_norm_back(
            grad, normal, root, gain * (1.0 + table(part, 4))
        )
        gmid_ref[at, :] = grad_middle
        sums_ref[part, 0:1, :] = jnp.sum(grad_middle * branch_s[at, :], axis=0, keepdims=True)
        right_ref[at, FF + D :] = (grad_middle * table(part, 2)).astype(BF)
    gatt_ref[...] = mm(right_ref[:, FF + D :], wo[...], NT).astype(BF)


def middle_part(units, order, core, tiles, att, x, cot, mask, modulation, flat, rows=256):
    row = lambda width: pl.BlockSpec((rows, width), lambda i: (i, 0))
    shape = lambda s, t: jax.ShapeDtypeStruct(s, t)
    return pl.pallas_call(
        functools.partial(middle_kernel, rows),
        grid=(SLOTS // rows,),
        in_specs=[SMALL_VMEM] * 3 + [pl.BlockSpec(memory_space=HBM)] * (2 * UNITS)
        + [row(D), row(D), row(D), row(1), whole((NSEG, 6 * D)), whole((FLAT_ROWS, 128))],
        out_specs=[row(D), row(FF + 2 * D), row(FF + 2 * D), row(D), row(D),
                   pl.BlockSpec((rows // TILE, 8, D), lambda i: (i, 0, 0)), whole((8, FF + D))],
        out_shape=[shape((SLOTS, D), BF), shape((SLOTS, FF + 2 * D), BF), shape((SLOTS, FF + 2 * D), BF),
                   shape((SLOTS, D), F32), shape((SLOTS, D), BF), shape((BLOCKS, 8, D), F32), shape((8, FF + D), F32)],
        scratch_shapes=[pltpu.VMEM((D, D), BF), pltpu.VMEM((D, FF), BF), pltpu.VMEM((FF, D), BF),
                        pltpu.VMEM((rows, FF), F32), pltpu.VMEM((rows, D), F32), pltpu.VMEM((rows, D), F32),
                        pltpu.SemaphoreType.DMA((8 * UNITS,))],
        cost_estimate=pl.CostEstimate(flops=4 * SLOTS * D * (D + 2 * FF), bytes_accessed=50 * 2**20, transcendentals=SLOTS * FF),
        compiler_params=pltpu.CompilerParams(vmem_limit_bytes=60 * 2**20),
    )(order, core, tiles, *units, att, x, cot, mask, modulation, flat)


def later_grads_kernel(core_ref, left_ref, right_ref, mine_ref, give_ref, buffer, sems):
    step = pl.program_id(0)
    steps = 2 * (FF // D) + 1
    slot = step % 2
    down_steps = FF // D
    core = core_ref[0]

    def wait(at_slot):
        for number in range(16):
            pltpu.make_async_copy(buffer.at[at_slot, number], buffer.at[at_slot, number], sems.at[at_slot, number]).wait()

    @pl.when(step >= 2)
    def _():
        wait(slot)

    product = mm(left_ref[...], right_ref[...], TN).astype(BF)
    buffer[slot] = product.reshape(16, 48, D)

    @pl.when(step < down_steps)
    def _():
        for number in range(16):
            local, side, block = number // 4, (number // 2) % 2, number % 2
            for ref, wanted in ((mine_ref, 0), (give_ref, 1)):
                @pl.when((core ^ side) == wanted)
                def _(ref=ref):
                    pltpu.make_async_copy(
                        buffer.at[slot, number],
                        ref.at[4 * step + local, :, pl.ds(DOWN_AT + block * D, D)],
                        sems.at[slot, number],
                    ).start()

    for j in range(down_steps):
        @pl.when(step == down_steps + j)
        def _():
            for number in range(16):
                for ref, wanted in ((mine_ref, 0), (give_ref, 1)):
                    @pl.when((core ^ (j // 2)) == wanted)
                    def _(ref=ref):
                        pltpu.make_async_copy(
                            buffer.at[slot, number],
                            ref.at[number, :, pl.ds(UP_AT + (j % 2) * D, D)],
                            sems.at[slot, number],
                        ).start()

    @pl.when(step == steps - 1)
    def _():
        for number in range(16):
            for side in range(2):
                for ref, wanted in ((mine_ref, 0), (give_ref, 1)):
                    @pl.when((core ^ side) == wanted)
                    def _(ref=ref):
                        pltpu.make_async_copy(
                            buffer.at[slot, number, :, pl.ds(side * (D // 2), D // 2)],
                            ref.at[number, :, pl.ds(OUT_AT, D // 2)],
                            sems.at[slot, number],
                        ).start()
        wait(1 - slot)
        wait(slot)


def later_grads(core, left, right):
    chunks = FF // D
    left_at = lambda i: (0, jnp.minimum(i, chunks) + jnp.maximum(i - 2 * chunks + 1, 0))
    right_at = lambda i: (0, jnp.maximum(i - chunks + 1, 0))
    shape = jax.ShapeDtypeStruct((UNITS, 48, SECOND_WIDE), BF)
    return pl.pallas_call(
        later_grads_kernel,
        grid=(2 * chunks + 1,),
        in_specs=[SMALL_VMEM, pl.BlockSpec((SLOTS, D), left_at), pl.BlockSpec((SLOTS, D), right_at)],
        out_specs=[pl.BlockSpec(memory_space=HBM)] * 2,
        out_shape=[shape, shape],
        scratch_shapes=[pltpu.VMEM((2, 16, 48, D), BF), pltpu.SemaphoreType.DMA((2, 16))],
        cost_estimate=pl.CostEstimate(flops=2 * SLOTS * D * (2 * FF + D), bytes_accessed=40 * 2**20, transcendentals=0),
        compiler_params=pltpu.CompilerParams(vmem_limit_bytes=48 * 2**20),
    )(core, left, right)


def last_kernel(rows, core_ref, tiles_ref, member_ref, first_ref, g_ref, w_ref, x_ref, gmid_ref, mod_ref, flat_ref, cond_ref,
                sums_in, bias_in, gin_ref, mine_ref, give_ref, sums, units, sems):
    step = pl.program_id(0)
    tiles = rows // TILE
    steps = SLOTS // rows
    core = core_ref[0]
    gain = line(flat_ref, 0, D // 128)

    at_rows = pl.ds(pl.multiple_of(step * rows, rows), rows)
    grad = None
    for kind in range(3):
        share = mm(g_ref[kind, at_rows, :], w_ref[:, kind * D : (kind + 1) * D], NT)
        grad = share if grad is None else grad + share
    for part in range(tiles):
        at = pl.ds(part * TILE, TILE)
        tile = step * tiles + part
        segment = tiles_ref[tile]
        normal, root = layer_norm(x_ref[at, :].astype(F32))
        piece = grad[part * TILE : (part + 1) * TILE]
        scale = mod_ref[pl.ds(segment, 1), D : 2 * D]
        sums[pl.ds(tile, 1), 0:D] = jnp.sum(piece, axis=0, keepdims=True)
        sums[pl.ds(tile, 1), D : 2 * D] = jnp.sum(piece * normal, axis=0, keepdims=True)
        gin_ref[at, :] = gmid_ref[at, :] + layer_norm_back(piece, normal, root, gain * (1.0 + scale))

    @pl.when(step < 3)
    def _():
        kind = step
        product = mm(first_ref[...], g_ref[pl.ds(kind, 1)][0], TN).astype(BF).reshape(UNITS, 48, D)
        for number in range(3):
            @pl.when(kind == number)
            def _():
                if number == 0:
                    units[0, :, :, 0:D] = product
                elif number == 1:
                    units[0, :, :, D:QKV_HALF] = product[:, :, : D // 2]
                    units[1, :, :, 0 : D // 2] = product[:, :, D // 2 :]
                else:
                    units[1, :, :, D // 2 : QKV_HALF] = product

    @pl.when(step == steps - 1)
    def _():
        gain_two = line(flat_ref, D // 128, D // 128)
        for tile in range(BLOCKS):
            at = pl.ds(tile, 1)
            sums[at, 2 * D : 3 * D] = sums_in[tile, 0:1, :]
            sums[at, 3 * D : 4 * D] = sums_in[tile, 1:2, :]
            sums[at, 4 * D : 5 * D] = sums_in[tile, 2:3, :]
            sums[at, 5 * D : 6 * D] = sums_in[tile, 3:4, :]
        member = member_ref[...]
        scale_one = lax.dot_general(member, mod_ref[:, D : 2 * D], NN, precision=lax.Precision.HIGHEST, preferred_element_type=F32)
        scale_two = lax.dot_general(member, mod_ref[:, 4 * D : 5 * D], NN, precision=lax.Precision.HIGHEST, preferred_element_type=F32)
        grad_gain_one = jnp.sum(sums[:, D : 2 * D] * (1.0 + scale_one), axis=0, keepdims=True)
        grad_gain_two = jnp.sum(sums[:, 4 * D : 5 * D] * (1.0 + scale_two), axis=0, keepdims=True)
        sums[:, D : 2 * D] = sums[:, D : 2 * D] * gain
        sums[:, 4 * D : 5 * D] = sums[:, 4 * D : 5 * D] * gain_two
        by_segment = lax.dot_general(member, sums[...], TN, precision=lax.Precision.HIGHEST, preferred_element_type=F32)
        grad_mod = lax.dot_general(
            by_segment, cond_ref[...].astype(F32), TN, precision=lax.Precision.HIGHEST, preferred_element_type=F32
        ).astype(BF).reshape(UNITS, 2, 3, 48, COND)
        for side in range(2):
            for block in range(3):
                units[side, :, :, QKV_HALF + block * COND : QKV_HALF + (block + 1) * COND] = grad_mod[:, side, block]
        row = jnp.concatenate(
            [grad_gain_one, grad_gain_two, bias_in[0:1, :], jnp.sum(by_segment, axis=0, keepdims=True)], axis=1
        )
        lane = lax.broadcasted_iota(jnp.int32, (1, 128), 1)
        blank = jnp.zeros((43, 128), F32)
        for part in range(UNITS):
            start = VECTOR_PART * part
            pieces = []
            for number in range(5):
                first_row, turn = divmod(start + 128 * number, 128)
                piece = row[:, first_row * 128 : (first_row + 1) * 128]
                if turn:
                    following = (
                        row[:, (first_row + 1) * 128 : (first_row + 2) * 128]
                        if (first_row + 2) * 128 <= row.shape[1]
                        else jnp.zeros((1, 128), F32)
                    )
                    piece = jnp.where(
                        lane < 128 - turn, pltpu.roll(piece, 128 - turn, 1), pltpu.roll(following, 128 - turn, 1)
                    )
                if number == 4:
                    piece = jnp.where(lane < VECTOR_PART - 512, piece, 0.0)
                pieces.append(piece)
            stack = jnp.concatenate(pieces + [blank], axis=0).astype(BF)
            for side in range(2):
                units[side, part, :, QKV_HALF + 3 * COND :] = stack
        copies = [
            pltpu.make_async_copy(units.at[core], mine_ref, sems.at[0]),
            pltpu.make_async_copy(units.at[1 - core], give_ref, sems.at[1]),
        ]
        for copy in copies:
            copy.start()
        for copy in copies:
            copy.wait()


def last_part(core, tiles, member, first, g, w, x, gmid, modulation, flat, cond, sums, bias, rows=256):
    row = lambda width: pl.BlockSpec((rows, width), lambda i: (i, 0))
    shape = jax.ShapeDtypeStruct((UNITS, 48, FIRST_WIDE), BF)
    return pl.pallas_call(
        functools.partial(last_kernel, rows),
        grid=(SLOTS // rows,),
        in_specs=[SMALL_VMEM, SMALL_VMEM, whole((BLOCKS, NSEG)), whole((SLOTS, D)), whole((3, SLOTS, D)), whole((D, 3 * D)),
                  row(D), row(D), whole((NSEG, 6 * D)), whole((FLAT_ROWS, 128)), whole((NSEG, COND)),
                  whole((BLOCKS, 8, D)), whole((8, FF + D))],
        out_specs=[row(D)] + [pl.BlockSpec(memory_space=HBM)] * 2,
        out_shape=[jax.ShapeDtypeStruct((SLOTS, D), F32), shape, shape],
        scratch_shapes=[pltpu.VMEM((BLOCKS, 6 * D), F32), pltpu.VMEM((2, UNITS, 48, FIRST_WIDE), BF),
                        pltpu.SemaphoreType.DMA((2,))],
        cost_estimate=pl.CostEstimate(flops=4 * SLOTS * D * 3 * D, bytes_accessed=30 * 2**20, transcendentals=SLOTS),
        compiler_params=pltpu.CompilerParams(vmem_limit_bytes=60 * 2**20),
    )(core, tiles, member, first, g, w, x, gmid, modulation, flat, cond, sums, bias)


ALONG_X, ALONG_Y, ALONG_Z = (1, 0, 0), (0, 1, 0), (0, 0, 1)
ROUNDS = (
    (((0, 0, 0), ALONG_X), ((0, 0, 0), ALONG_Y), ((0, 0, 0), ALONG_Z)),
    (((0, 1, 0), ALONG_X), ((0, 0, 1), ALONG_Y), ((0, 0, 1), ALONG_Z)),
    (((0, 1, 1), ALONG_X), ((0, 0, 2), ALONG_Y), ((0, 0, 2), ALONG_Z)),
    (((0, 0, 1), ALONG_X), ((0, 0, 3), ALONG_Y), ((1, 1, 1), ALONG_Z)),
    (((0, 0, 3), ALONG_X), ((1, 1, 2), ALONG_Y), ((1, 1, 2), ALONG_Z)),
)
OFFSETS = tuple((a, b, c) for c in range(4) for b in range(2) for a in range(2))


def moved(chip, step, sign=1):
    return ((chip & 1) ^ step[0]) + 2 * (((chip >> 1) & 1) ^ step[1]) + 4 * (((chip >> 2) + sign * step[2]) % 4)


def added(offset, step):
    return (offset[0] ^ step[0], offset[1] ^ step[1], (offset[2] + step[2]) % 4)


ORIGIN = np.array([[moved(chip, offset, -1) for offset in OFFSETS] for chip in range(UNITS)], np.int32)


def pass_on(values, step, sign=1):
    return lax.ppermute(values, "fsdp", [(chip, moved(chip, step, sign)) for chip in range(UNITS)])


def swap_core(values):
    return lax.ppermute(values, "rep", [(0, 1), (1, 0)])


def hold_back(later, sooner):
    return lax.optimization_barrier((later, sooner))[0]


def by_rounds():
    return lax.axis_size("fsdp") == UNITS


def gather_units(unit):
    held = {OFFSETS[0]: unit}
    for round_steps in ROUNDS:
        held.update([(added(offset, step), pass_on(held[offset], step)) for offset, step in round_steps])
    own = [held[offset] for offset in OFFSETS]
    return own + [swap_core(one) for one in own]


def sums_kernel(counts, order_ref, *refs):
    outs = refs[len(refs) - len(counts) :]
    at = 0
    for out_ref, count in zip(outs, counts):
        total = refs[at][0].astype(F32) + refs[at + 1][0].astype(F32)
        for arrived in refs[at + 2 : at + 2 + count]:
            total = total + arrived[...].astype(F32)
        out_ref[...] = total.astype(BF)
        at += 2 + count


def unit_sums(order, mine, given, offsets, arrived):
    block = mine.shape[1:]
    specs, operands = [], []
    for offset in offsets:
        pick = pl.BlockSpec((1,) + block, lambda i, s, place=OFFSETS.index(offset): (s[place], 0, 0))
        came = arrived.get(offset, [])
        specs += [pick, pick] + [pl.BlockSpec(block, lambda i, s: (0, 0))] * len(came)
        operands += [mine, given] + came
    return pl.pallas_call(
        functools.partial(sums_kernel, [len(arrived.get(offset, [])) for offset in offsets]),
        grid_spec=pltpu.PrefetchScalarGridSpec(
            num_scalar_prefetch=1,
            grid=(1,),
            in_specs=specs,
            out_specs=[pl.BlockSpec(block, lambda i, s: (0, 0))] * len(offsets),
        ),
        out_shape=[jax.ShapeDtypeStruct(block, BF)] * len(offsets),
        compiler_params=pltpu.CompilerParams(vmem_limit_bytes=48 * 2**20),
    )(order, *operands)


def scatter_sums(mine, give, order, waiting=()):
    given = swap_core(give)
    arrived = {}
    came = None
    for number in range(5):
        round_steps = ROUNDS[4 - number]
        sums = unit_sums(order, mine, given, [added(offset, step) for offset, step in round_steps], arrived)
        sent = [(offset, pass_on(values, step, -1)) for (offset, step), values in zip(round_steps, sums)]
        if number < len(waiting):
            waiting[number](came)
        came = [values for _, values in sent]
        for offset, values in sent:
            arrived.setdefault(offset, []).append(values)
    for rest in waiting[5:]:
        rest(came)
        came = None
    (own,) = unit_sums(order, mine, given, [OFFSETS[0]], arrived)
    other = swap_core(own)
    first = lax.axis_index("rep") == 0
    return (jnp.where(first, own, other).astype(F32), jnp.where(first, other, own).astype(F32))


def sum_small(values):
    for step in (ALONG_X, ALONG_Y, (0, 0, 2)):
        values = values + pass_on(values, step)
    return values + lax.ppermute(values, "fsdp", [(chip, chip ^ 4) for chip in range(UNITS)])


def sum_over_chips(values):
    return sum_small(values) if by_rounds() else lax.psum(values, "fsdp")


def side_columns(matrix, core, width):
    return lax.dynamic_slice_in_dim(matrix, core * width, width, axis=1)


def side_rows(blocks, core):
    return lax.dynamic_index_in_dim(blocks, core, 1, keepdims=False)


def pack_first(qkv, mod_turned, vectors, core):
    count = vectors.shape[0]
    mod_blocks = side_rows(mod_turned.reshape(count, 2, 3, 48, COND), core)
    padded = jnp.pad(vectors, ((0, 0), (0, 640 - VECTOR_PART))).reshape(count, 5, 128)
    return jnp.concatenate(
        [
            side_columns(qkv, core, QKV_HALF).reshape(count, 48, QKV_HALF),
            mod_blocks.transpose(0, 2, 1, 3).reshape(count, 48, 3 * COND),
            jnp.pad(padded, ((0, 0), (0, 43), (0, 0))),
        ],
        axis=2,
    )


def pack_second(out, up, down, core):
    count = out.shape[0] // 48
    down_blocks = side_rows(down.reshape(count, 2, 2, 48, D), core)
    return jnp.concatenate(
        [
            side_columns(up, core, FF // 2).reshape(count, 48, FF // 2),
            down_blocks.transpose(0, 2, 1, 3).reshape(count, 48, 2 * D),
            side_columns(out, core, D // 2).reshape(count, 48, D // 2),
        ],
        axis=2,
    )


def unpack_first(sides):
    count = sides[0].shape[0]
    qkv = jnp.concatenate([side[:, :, :QKV_HALF] for side in sides], axis=2).reshape(count * 48, 3 * D)
    turned = jnp.stack([side[:, :, QKV_HALF : QKV_HALF + 3 * COND] for side in sides], axis=1)
    turned = turned.reshape(count, 2, 48, 3, COND).transpose(0, 1, 3, 2, 4).reshape(count * 288, COND)
    vectors = sides[0][:, :5, QKV_HALF + 3 * COND :].reshape(count, 640)[:, :VECTOR_PART]
    return (qkv, turned.T, vectors.reshape(-1))


def unpack_second(sides):
    count = sides[0].shape[0]
    up = jnp.concatenate([side[:, :, UP_AT : UP_AT + FF // 2] for side in sides], axis=2).reshape(count * 48, FF)
    out = jnp.concatenate([side[:, :, OUT_AT:] for side in sides], axis=2).reshape(count * 48, D)
    down = jnp.stack([side[:, :, DOWN_AT : DOWN_AT + 2 * D] for side in sides], axis=1)
    down = down.reshape(count, 2, 48, 2, D).transpose(0, 1, 3, 2, 4).reshape(count * 192, D)
    return (out, up, down)


def gather_plain(parts, axes):
    return [lax.all_gather(part, "fsdp", axis=axis, tiled=True) for part, axis in zip(parts, axes)]


def virtual_units(pack):
    return [packed[number] for packed in (pack(0), pack(1)) for number in range(UNITS)]


def reduce_plain(grads, axes):
    parts = [
        lax.psum_scatter(grad.astype(F32), "fsdp", scatter_dimension=axis, tiled=True) for grad, axis in zip(grads, axes)
    ]
    return tuple(lax.psum(part.astype(BF), "rep").astype(F32) for part in parts)


def adam_direction(weight, first_old, second_old, gradient, decay_rate):
    first_new = BETA_ONE * first_old + (1.0 - BETA_ONE) * gradient
    second_new = BETA_TWO * second_old + (1.0 - BETA_TWO) * gradient * gradient
    direction = (
        first_new
        / (1.0 - BETA_ONE**STEP)
        / (jnp.sqrt(second_new / (1.0 - BETA_TWO**STEP)) + EPSILON)
        + decay_rate * weight
    )
    return (first_new, second_new, direction)


def layout_tables(sizes_row, lengths_row):
    slot_ids = jnp.arange(SLOTS, dtype=jnp.int32)
    seg_ends = jnp.cumsum(sizes_row)
    starts = seg_ends - sizes_row
    segment = jnp.sum((slot_ids[:, None] >= seg_ends[None, :]).astype(jnp.int32), axis=1)
    member = segment[:, None] == jnp.arange(NSEG, dtype=jnp.int32)[None, :]
    offset = jnp.sum(jnp.where(member, starts[None, :], 0), axis=1)
    length_of = jnp.sum(jnp.where(member, lengths_row[None, :], 0), axis=1)
    position = slot_ids - offset
    return (segment, member, position, position < length_of)


def condition(steps_row):
    half_cond = COND // 2
    frequency = jnp.exp(jnp.arange(half_cond, dtype=F32) * (-math.log(10000.0) / half_cond))
    angles = steps_row.astype(F32)[:, None] * frequency[None, :]
    return jax.nn.silu(jnp.concatenate([jnp.cos(angles), jnp.sin(angles)], axis=1))


GROUPS = 6


def on_device(
    inputs, cotangent, seg_sizes, seq_lengths, timesteps, absorbed,
    qkv_weight, out_weight, up_weight, down_weight, mod_weight,
    qkv_first, out_first, up_first, down_first, mod_first,
    qkv_second, out_second, up_second, down_second, mod_second,
    vectors, vectors_first, vectors_second,
):
    rounds = by_rounds()
    chip = lax.axis_index("fsdp")
    core = lax.axis_index("rep")
    matrices = (qkv_weight, out_weight, up_weight, down_weight, mod_weight)
    qkv_low, out_low, up_low, down_low, mod_low = [matrix.astype(BF) for matrix in matrices]
    vector_low = vectors.astype(BF)
    if rounds:
        order = jnp.asarray(ORIGIN)[chip]
        side = core[None].astype(jnp.int32)
        units_first = gather_units(pack_first(qkv_low, mod_low.T, vector_low[None], core)[0])
        units_second = gather_units(hold_back(pack_second(out_low, up_low, down_low, core)[0], units_first[:UNITS]))
    else:
        order = jnp.arange(UNITS, dtype=jnp.int32)
        side = jnp.zeros((1,), jnp.int32)
        qkv_all, mod_all, vector_all = gather_plain((qkv_low, mod_low, vector_low), (0, 1, 0))
        out_all, up_all, down_all = gather_plain((out_low, up_low, down_low), (0, 0, 0))
        units_first = virtual_units(lambda s: pack_first(qkv_all, mod_all.T, vector_all.reshape(UNITS, -1), s))
        units_second = virtual_units(lambda s: pack_second(out_all, up_all, down_all, s))

    segment, member, position, valid_slot = layout_tables(seg_sizes[0], seq_lengths[0])
    tiles = segment.reshape(BLOCKS, TILE)[:, 0]
    member_tile = member.reshape(BLOCKS, TILE, NSEG)[:, 0].astype(F32)
    condition_low = condition(timesteps[0]).astype(BF)
    cos, sin, feature_query, feature_key = attention_tables(segment, position, valid_slot)
    weight_mask = (absorbed[0] * valid_slot.astype(jnp.int32)).astype(F32)[:, None]
    row_in, row_cot = inputs[0], cotangent[0]

    mixed, first_low, qkv_full, modulation, flat = first_part(
        units_first, order, side, tiles, row_in, condition_low, cos, sin
    )
    per_call = HEADS // 2 // GROUPS
    forward = None
    for number in range(GROUPS):
        forward = attention_forward(mixed, feature_query, feature_key, forward, number * per_call, per_call)
    attended_low, feature = forward
    out_hidden, left, right, grad_middle, grad_attended, sums, bias_sums = middle_part(
        units_second, order, side, tiles, attended_low, row_in, row_cot, weight_mask, modulation, flat
    )
    mine_later, give_later = later_grads(side, left, right)

    state = [None]

    def backward_part(number, came):
        grad_here = grad_attended if came is None else hold_back(grad_attended, came)
        state[0] = attention_backward(
            mixed, feature, feature_key, grad_here, attended_low, cos, sin, state[0], number * per_call, per_call
        )

    waiting = [functools.partial(backward_part, number) for number in range(GROUPS)]
    if rounds:
        later = scatter_sums(mine_later, give_later, order, waiting)
        grad_out, grad_up, grad_down = unpack_second([part[None] for part in later])
    else:
        for one in waiting:
            one(None)
        grad_out, grad_up, grad_down = reduce_plain(unpack_second((mine_later, give_later)), (0, 0, 0))
    grad_in, mine_sooner, give_sooner = last_part(
        side, tiles, member_tile, first_low, state[0], qkv_full, row_in, grad_middle, modulation, flat, condition_low,
        sums, bias_sums,
    )
    if rounds:
        sooner = scatter_sums(mine_sooner, give_sooner, order)
        grad_qkv, grad_mod, grad_vectors = unpack_first([part[None] for part in sooner])
    else:
        grad_qkv, grad_mod, grad_vectors = reduce_plain(unpack_first((mine_sooner, give_sooner)), (0, 1, 0))

    grads = (grad_qkv, grad_out, grad_up, grad_down, grad_mod)
    firsts = (qkv_first, out_first, up_first, down_first, mod_first)
    seconds = (qkv_second, out_second, up_second, down_second, mod_second)
    results = [
        adam_direction(matrices[number], firsts[number], seconds[number], grads[number], DECAY_RATE)
        for number in range(5)
    ]
    squares = jnp.zeros((2, 5), F32)
    for number in range(5):
        column = (jnp.arange(5) == number)[None, :]
        pair = jnp.stack([jnp.sum(matrices[number] * matrices[number]), jnp.sum(results[number][2] * results[number][2])])
        squares = squares + jnp.where(column, pair[:, None], 0.0)
    norm_roots = jnp.sqrt(sum_over_chips(squares))
    trust = norm_roots[0] / (norm_roots[1] + EPSILON)
    renewed = [
        matrices[number] - MATRIX_RATE * trust[number] * results[number][2] for number in range(5)
    ]
    vector_record = adam_direction(vectors, vectors_first, vectors_second, grad_vectors, 0.0)
    return (
        out_hidden[None],
        grad_in[None],
        *renewed,
        *[record[0] for record in results],
        *[record[1] for record in results],
        vectors - VECTOR_RATE * vector_record[2],
        vector_record[0],
        vector_record[1],
        norm_roots,
    )


def solution(mesh):
    rows = P(("rep", "fsdp"))
    matrix, turned, vector = P("fsdp", None), P(None, "fsdp"), P("fsdp")
    five = (matrix, matrix, matrix, matrix, turned)
    return jax.shard_map(
        on_device,
        mesh=mesh,
        in_specs=(rows,) * 6 + five * 3 + (vector,) * 3,
        out_specs=(rows, rows) + five * 3 + (vector,) * 3 + (P(),),
        check_vma=False,
    )
```

```python
import functools
import math

import jax
import jax.numpy as jnp
import numpy as np
from jax import lax
from jax.experimental import pallas as pl
from jax.experimental.pallas import tpu as pltpu
from jax.sharding import PartitionSpec as P

D = 768
HEADS = 12
HDIM = 64
FF = 3072
COND = 128
SLOTS = 1024
NSEG = 8
STEP = 10
TILE = 128
BLOCKS = SLOTS // TILE

BETA_ONE = 0.9
BETA_TWO = 0.999
EPSILON = 1e-06
DECAY_RATE = 0.01
MATRIX_RATE = 0.3
VECTOR_RATE = 1.0

PAIR = 128
NT = (((1,), (1,)), ((), ()))
NN = (((1,), (0,)), ((), ()))
TN = (((0,), (0,)), ((), ()))
BF = jnp.bfloat16
F32 = jnp.float32


def mm(a, b, dims=NN):
    return lax.dot_general(a, b, dims, preferred_element_type=F32)


def swap_halves(v):
    lane = lax.broadcasted_iota(jnp.int32, v.shape, 1)
    return jnp.where(lane % 64 < 32, pltpu.roll(v, PAIR - 32, 1), pltpu.roll(v, 32, 1))


def attention_forward_kernel(block, q_ref, k_ref, v_ref, fq_ref, fk_ref, *refs):
    o_ref, fo_ref, ka, kb, va, vb = refs[-6:]
    slots = q_ref.shape[0]
    low_all = lax.broadcasted_iota(jnp.int32, (slots, PAIR), 1) < 64
    k_low = k_ref[...]
    v_low = v_ref[...]
    fk = fk_ref[...]
    one = jnp.ones((slots, PAIR), BF)
    ka[...] = jnp.where(low_all, k_low, fk)
    kb[...] = jnp.where(low_all, fk, k_low)
    va[...] = jnp.where(low_all, v_low, one)
    vb[...] = jnp.where(low_all, one, v_low)
    lane = lax.broadcasted_iota(jnp.int32, (block, PAIR), 1)
    low = lane < 64
    spot = lane % 64

    def step(i, carry):
        at = pl.ds(pl.multiple_of(i * block, block), block)
        q = q_ref[at, :]
        fq = fq_ref[at, :]
        sa = mm(jnp.where(low, q, fq), ka[...], NT)
        sb = mm(jnp.where(low, fq, q), kb[...], NT)
        ma = jnp.max(sa, axis=1, keepdims=True)
        mb = jnp.max(sb, axis=1, keepdims=True)
        pa = jnp.exp(sa - ma).astype(BF)
        pb = jnp.exp(sb - mb).astype(BF)
        oa = mm(pa, va[...])
        ob = mm(pb, vb[...])
        o = jnp.where(low, oa / pltpu.roll(oa, 64, 1), ob / pltpu.roll(ob, 64, 1))
        o_ref[at, :] = o.astype(o_ref.dtype)
        neg = jnp.where(low, -(mb + jnp.log(ob)), -(ma + jnp.log(oa)))
        hi = neg.astype(BF)
        rest = neg - hi.astype(F32)
        mid = rest.astype(BF)
        last = (rest - mid.astype(F32)).astype(BF)
        fo_ref[at, :] = jnp.where(spot == 8, hi, jnp.where(spot == 9, mid, jnp.where(spot == 10, last, fq)))
        return carry

    lax.fori_loop(0, slots // block, step, 0)


def attention_forward(qkv, fq, fk, before, first, count, block=1024):
    slots, width = qkv.shape
    pairs = width // 3 // PAIR
    blk = lambda off: pl.BlockSpec((slots, PAIR), lambda p: (0, off + p))
    fixed = pl.BlockSpec((slots, PAIR), lambda p: (0, 0))
    anywhere = pl.BlockSpec(memory_space=pl.ANY)
    shape = jax.ShapeDtypeStruct((slots, pairs * PAIR), BF)
    extra = () if before is None else before
    elements = 2 * count * slots * slots
    return pl.pallas_call(
        functools.partial(attention_forward_kernel, block),
        grid=(count,),
        in_specs=[blk(first), blk(pairs + first), blk(2 * pairs + first), fixed, fixed] + [anywhere] * len(extra),
        out_specs=[blk(first)] * 2,
        out_shape=[shape, shape],
        scratch_shapes=[pltpu.VMEM((slots, PAIR), BF)] * 4,
        input_output_aliases={5: 0, 6: 1} if extra else {},
        cost_estimate=pl.CostEstimate(flops=elements * 3000, bytes_accessed=10 * slots * count * PAIR, transcendentals=elements),
        compiler_params=pltpu.CompilerParams(vmem_limit_bytes=48 * 2**20),
    )(qkv, qkv, qkv, fq, fk, *extra)


def attention_backward_kernel(block, q_ref, k_ref, v_ref, fo_ref, fk_ref, do_ref, o_ref, cos_ref, sin_ref, *refs):
    g_ref, ka, kb, va, vb, kt, dka, dkb, dva, dvb = refs[-10:]
    slots = q_ref.shape[0]
    lane_all = lax.broadcasted_iota(jnp.int32, (slots, PAIR), 1)
    low_all = lane_all < 64
    fk = fk_ref[...]
    k_low = k_ref[...]
    v_low = v_ref[...]
    one = jnp.where(lane_all % 64 < 2, 1.0, 0.0).astype(BF)
    ka[...] = jnp.where(low_all, k_low, fk)
    kb[...] = jnp.where(low_all, fk, k_low)
    va[...] = jnp.where(low_all, v_low, one)
    vb[...] = jnp.where(low_all, one, v_low)
    kt[...] = k_low.T
    dka[...] = jnp.zeros_like(dka)
    dkb[...] = jnp.zeros_like(dkb)
    dva[...] = jnp.zeros_like(dva)
    dvb[...] = jnp.zeros_like(dvb)
    lane = lax.broadcasted_iota(jnp.int32, (block, PAIR), 1)
    low = lane < 64
    spot = lane % 64
    top = lax.broadcasted_iota(jnp.int32, (PAIR, block), 0) < 64

    def step(i, carry):
        at = pl.ds(pl.multiple_of(i * block, block), block)
        q = q_ref[at, :]
        fq = fo_ref[at, :]
        do = do_ref[at, :]
        both = do.astype(F32) * o_ref[at, :].astype(F32)
        da = jnp.sum(jnp.where(low, both, 0.0), axis=1, keepdims=True)
        db = jnp.sum(jnp.where(low, 0.0, both), axis=1, keepdims=True)
        neg = jnp.where(low, -db, -da)
        hi = neg.astype(BF)
        rest = (neg - hi.astype(F32)).astype(BF)
        fd = jnp.where(spot == 0, hi, jnp.where(spot == 1, rest, jnp.zeros_like(hi)))
        sa = mm(ka[...], jnp.where(low, q, fq), NT)
        sb = mm(kb[...], jnp.where(low, fq, q), NT)
        ea = mm(va[...], jnp.where(low, do, fd), NT)
        eb = mm(vb[...], jnp.where(low, fd, do), NT)
        pa = jnp.exp(sa)
        pb = jnp.exp(sb)
        dsa = (pa * ea).astype(BF)
        dsb = (pb * eb).astype(BF)
        dva[...] += mm(pa.astype(BF), do)
        dvb[...] += mm(pb.astype(BF), do)
        dka[...] += mm(dsa, q)
        dkb[...] += mm(dsb, q)
        dqt = jnp.where(top, mm(kt[...], dsa), mm(kt[...], dsb))
        dq = dqt.T * 0.125
        g_ref[0, at, :] = (dq * cos_ref[at, :] - swap_halves(dq) * sin_ref[at, :]).astype(BF)
        return carry

    lax.fori_loop(0, slots // block, step, 0)
    dk = jnp.where(low_all, dka[...], dkb[...])
    g_ref[1] = (dk * cos_ref[...] - swap_halves(dk) * sin_ref[...]).astype(BF)
    g_ref[2] = jnp.where(low_all, dva[...], dvb[...]).astype(BF)


def attention_backward(qkv, fo, fk, do, o, cos, sin, before, first, count, block=512):
    slots, width = qkv.shape
    pairs = width // 3 // PAIR
    blk = lambda off: pl.BlockSpec((slots, PAIR), lambda p: (0, off + p))
    fixed = pl.BlockSpec((slots, PAIR), lambda p: (0, 0))
    extra = () if before is None else (before,)
    elements = 2 * count * slots * slots
    return pl.pallas_call(
        functools.partial(attention_backward_kernel, block),
        grid=(count,),
        in_specs=[blk(first), blk(pairs + first), blk(2 * pairs + first), blk(first), fixed, blk(first), blk(first),
                  fixed, fixed] + [pl.BlockSpec(memory_space=pl.ANY)] * len(extra),
        out_specs=pl.BlockSpec((3, slots, PAIR), lambda p: (0, 0, first + p)),
        out_shape=jax.ShapeDtypeStruct((3, slots, pairs * PAIR), BF),
        scratch_shapes=[pltpu.VMEM((slots, PAIR), BF)] * 4 + [pltpu.VMEM((PAIR, slots), BF)]
        + [pltpu.VMEM((slots, PAIR), F32)] * 4,
        input_output_aliases={9: 0} if extra else {},
        cost_estimate=pl.CostEstimate(flops=elements * 2000, bytes_accessed=20 * slots * count * PAIR, transcendentals=elements),
        compiler_params=pltpu.CompilerParams(vmem_limit_bytes=48 * 2**20),
    )(qkv, qkv, qkv, fo, fk, do, o, cos, sin, *extra)


def attention_tables(segment, position, valid_slot):
    inverse = jnp.exp(jnp.arange(32, dtype=F32) * (-math.log(10000.0) / 32))
    angles = position.astype(F32)[:, None] * inverse[None, :]
    c, s = jnp.cos(angles), jnp.sin(angles)
    cos = jnp.concatenate([c, c, c, c], axis=1)
    sin = jnp.concatenate([-s, s, -s, s], axis=1)
    spot = jnp.arange(PAIR) % 64
    same = segment[:, None] == spot[None, :]
    fq = same.astype(BF)
    fk = jnp.where((spot < 8)[None, :], jnp.where(same & valid_slot[:, None], 0.0, -1e30),
                   jnp.where((spot < 11)[None, :], 1.0, 0.0)).astype(BF)
    return cos, sin, fq, fk


UNITS = 16
QKV_HALF = 3 * D // 2
SMALL_WIDE = 6 * COND + 128
FIRST_WIDE = QKV_HALF + 3 * COND + 128
UP_AT, DOWN_AT, OUT_AT, SECOND_WIDE = 0, FF // 2, FF // 2 + 2 * D, FF // 2 + 2 * D + D // 2
VECTOR_PART = (9 * D + FF) // UNITS
FLAT_ROWS = 80
HBM = pltpu.HBM
SMALL_VMEM = pl.BlockSpec(memory_space=pltpu.SMEM)


def whole(shape):
    return pl.BlockSpec(shape, lambda *_: (0,) * len(shape))


def line(flat_ref, start, count):
    return jnp.concatenate([flat_ref[start + i : start + i + 1, :] for i in range(count)], axis=1)


def unit_of(units, half, place):
    if len(units) == 8:
        return units[half * 4 + place // 4].at[place % 4]
    return units[half * 8 + place // 4 * 2 + min(place % 4, 1)].at[max(place % 4 - 1, 0)]


def unit_copies(units, order, core, sems, plan, first_sem):
    copies = []
    for half in range(2):
        side = core if half == 0 else 1 - core
        for place in range(UNITS):
            origin = order[half * UNITS + place]
            for target, rows, column, width, by_origin, by_side, row, column_side, both in plan:
                if half == 1 and not both:
                    continue
                to_row = pl.multiple_of(origin * by_origin + side * by_side + row, 16)
                to_column = pl.multiple_of(side * column_side, 128) if column_side else 0
                copies.append(
                    pltpu.make_async_copy(
                        unit_of(units, half, place).at[pl.ds(0, rows), pl.ds(column, width)],
                        target.at[pl.ds(to_row, rows), pl.ds(to_column, width)],
                        sems.at[first_sem + len(copies)],
                    )
                )
    return copies


def layer_norm(values):
    average = jnp.mean(values, axis=-1, keepdims=True)
    centered = values - average
    root = lax.rsqrt(jnp.mean(centered * centered, axis=-1, keepdims=True) + 1e-05)
    return (centered * root, root)


def layer_norm_back(grad, normal, root, gain):
    scaled = grad * gain
    inner = jnp.mean(scaled * normal, axis=-1, keepdims=True)
    return root * (scaled - jnp.mean(scaled, axis=-1, keepdims=True) - normal * inner)


def first_kernel(rows, order_ref, core_ref, tiles_ref, *refs):
    units = refs[:8]
    x_ref, cond_ref, cos_ref, sin_ref, qkv_ref, first_ref, w_ref, mod_ref, flat_ref, modt, vecs, sems = refs[8:]
    step = pl.program_id(0)

    @pl.when(step == 0)
    def _():
        core = core_ref[0]
        small = unit_copies(units, order_ref, core, sems, (
            (vecs, 16, QKV_HALF + 3 * COND, 128, 16, 0, 0, 0, False),
            (modt, 48, QKV_HALF, 128, 288, 144, 0, 0, True),
            (modt, 48, QKV_HALF + 128, 128, 288, 144, 48, 0, True),
            (modt, 48, QKV_HALF + 256, 128, 288, 144, 96, 0, True),
        ), 0)
        large = unit_copies(units, order_ref, core, sems, (
            (w_ref, 48, 0, QKV_HALF, 48, 0, 0, QKV_HALF, True),
        ), len(small))
        for copy in small + large:
            copy.start()
        for copy in small:
            copy.wait()
        flat_ref[...] = jnp.zeros_like(flat_ref)
        lane = lax.broadcasted_iota(jnp.int32, (8, 128), 1)
        for part in range(UNITS):
            row, turn = divmod(VECTOR_PART * part, 128)
            piece = vecs[16 * part : 16 * part + 16, :].astype(F32)[:8]
            if turn:
                piece = pltpu.roll(piece, turn, 1)
                flat_ref[row + 1 : row + 6, :] += jnp.where(lane < turn, piece, 0.0)[:5]
                piece = jnp.where(lane >= turn, piece, 0.0)
            flat_ref[row : row + 5, :] += piece[:5]
        mod_ref[...] = mm(cond_ref[...], modt[...], NT) + line(flat_ref, (3 * D + FF) // 128, 6 * D // 128)
        for copy in large:
            copy.wait()

    gain = line(flat_ref, 0, D // 128)
    for part in range(rows // TILE):
        at = pl.ds(part * TILE, TILE)
        segment = tiles_ref[step * (rows // TILE) + part]
        normal, _ = layer_norm(x_ref[at, :].astype(F32))
        shift = mod_ref[pl.ds(segment, 1), 0:D]
        scale = mod_ref[pl.ds(segment, 1), D : 2 * D]
        first_ref[at, :] = (normal * (gain * (1.0 + scale)) + shift).astype(BF)
    first = first_ref[...]
    cos, sin = cos_ref[...], sin_ref[...]
    for kind in range(3):
        mixed = mm(first, w_ref[:, kind * D : (kind + 1) * D])
        if kind < 2:
            for pair in range(D // PAIR):
                part = mixed[:, pair * PAIR : (pair + 1) * PAIR]
                turned = part * cos + swap_halves(part) * sin
                if kind == 0:
                    turned = turned * HDIM ** (-0.5)
                qkv_ref[:, kind * D + pair * PAIR : kind * D + (pair + 1) * PAIR] = turned.astype(BF)
        else:
            qkv_ref[:, 2 * D :] = mixed.astype(BF)


def first_part(units, order, core, tiles, x, cond, cos, sin, rows=256):
    count = UNITS * (1 + 2 * 3 + 2)
    row = lambda width: pl.BlockSpec((rows, width), lambda i: (i, 0))
    shape = lambda s, t: jax.ShapeDtypeStruct(s, t)
    return pl.pallas_call(
        functools.partial(first_kernel, rows),
        grid=(SLOTS // rows,),
        in_specs=[SMALL_VMEM] * 3 + [pl.BlockSpec(memory_space=HBM)] * 8
        + [row(D), whole((NSEG, COND)), row(PAIR), row(PAIR)],
        out_specs=[row(3 * D), row(D), whole((D, 3 * D)), whole((NSEG, 6 * D)), whole((FLAT_ROWS, 128))],
        out_shape=[shape((SLOTS, 3 * D), BF), shape((SLOTS, D), BF), shape((D, 3 * D), BF),
                   shape((NSEG, 6 * D), F32), shape((FLAT_ROWS, 128), F32)],
        scratch_shapes=[pltpu.VMEM((6 * D, COND), BF), pltpu.VMEM((16 * UNITS, 128), BF), pltpu.SemaphoreType.DMA((count,))],
        cost_estimate=pl.CostEstimate(flops=2 * SLOTS * D * 3 * D, bytes_accessed=20 * 2**20, transcendentals=SLOTS),
        compiler_params=pltpu.CompilerParams(vmem_limit_bytes=56 * 2**20),
    )(order, core, tiles, *units, x, cond, cos, sin)


def middle_kernel(rows, order_ref, core_ref, tiles_ref, *refs):
    units = refs[:16]
    (att_ref, x_ref, cot_ref, mask_ref, mod_ref, flat_ref,
     out_ref, left_ref, right_ref, gmid_ref, gatt_ref, sums_ref, bias_ref,
     wo, wu, wd, slope, branch_s, middle_s, sems) = refs[16:]
    step = pl.program_id(0)
    core = core_ref[0]
    chunks = FF // D
    tiles = rows // TILE
    each = 2 * UNITS
    copies = [
        unit_copies(units, order_ref, core, sems, ((wo, 48, OUT_AT, D // 2, 48, 0, 0, D // 2, True),), 0),
        unit_copies(units, order_ref, core, sems, ((wu, 48, UP_AT, FF // 2, 48, 0, 0, FF // 2, True),), each),
        unit_copies(units, order_ref, core, sems, (
            (wd, 48, DOWN_AT, D, 192, 96, 0, 0, True),
            (wd, 48, DOWN_AT + D, D, 192, 96, 48, 0, True),
        ), 2 * each),
    ]

    @pl.when(step == 0)
    def _():
        for group in copies:
            for copy in group:
                copy.start()
        bias_ref[...] = jnp.zeros_like(bias_ref)
        for copy in copies[0]:
            copy.wait()

    def table(part, kind):
        return mod_ref[pl.ds(tiles_ref[step * tiles + part], 1), kind * D : (kind + 1) * D]

    def mask_column(part):
        row = mask_ref[pl.ds(step * tiles + part, 1), :]
        return jnp.broadcast_to(row, (TILE, TILE)).T[:, :1]

    att = att_ref[...]
    left_ref[:, FF + D :] = att
    branch_s[...] = mm(att, wo[...])
    gain = line(flat_ref, D // 128, D // 128)
    for part in range(tiles):
        at = pl.ds(part * TILE, TILE)
        middle = x_ref[at, :].astype(F32) + table(part, 2) * branch_s[at, :]
        middle_s[at, :] = middle
        normal, _ = layer_norm(middle)
        left_ref[at, FF : FF + D] = (normal * (gain * (1.0 + table(part, 4))) + table(part, 3)).astype(BF)

    @pl.when(step == 0)
    def _():
        for group in copies[1:]:
            for copy in group:
                copy.wait()

    second = left_ref[:, FF : FF + D]
    factor = math.sqrt(2.0 / math.pi)
    feed = None
    for j in range(chunks):
        at = pl.ds(j * D, D)
        u = mm(second, wu[:, at]) + line(flat_ref, 2 * D // 128 + j * (D // 128), D // 128)
        square = u * u
        bent = jnp.tanh(u * (factor + (factor * 0.044715) * square))
        half = 0.5 * u
        bow = half * bent
        hidden = (half + bow).astype(BF)
        left_ref[:, at] = hidden
        slope[:, at] = (0.5 + 0.5 * bent) + (half - bow * bent) * (factor + (3 * factor * 0.044715) * square)
        share = mm(hidden, wd[at, :])
        feed = share if feed is None else feed + share
    bias_down = line(flat_ref, (2 * D + FF) // 128, D // 128)
    for part in range(tiles):
        at = pl.ds(part * TILE, TILE)
        gate = table(part, 5)
        feed_out = feed[part * TILE : (part + 1) * TILE] + bias_down
        out_ref[at, :] = (middle_s[at, :] + gate * feed_out).astype(BF)
        grad_out = cot_ref[at, :].astype(F32) * mask_column(part)
        sums_ref[part, 3:4, :] = jnp.sum(grad_out * feed_out, axis=0, keepdims=True)
        grad_mlp = (grad_out * gate).astype(BF)
        right_ref[at, 0:D] = grad_mlp
        bias_ref[0:1, FF:] += jnp.sum(grad_mlp.astype(F32), axis=0, keepdims=True)
    grad_mlp = right_ref[:, 0:D]
    grad_second = None
    for j in range(chunks):
        at = pl.ds(j * D, D)
        grad_up = (mm(grad_mlp, wd[at, :], NT) * slope[:, at]).astype(BF)
        right_ref[:, D + j * D : 2 * D + j * D] = grad_up
        bias_ref[0:1, at] += jnp.sum(grad_up.astype(F32), axis=0, keepdims=True)
        share = mm(grad_up, wu[:, at], NT)
        grad_second = share if grad_second is None else grad_second + share
    for part in range(tiles):
        at = pl.ds(part * TILE, TILE)
        normal, root = layer_norm(middle_s[at, :])
        grad = grad_second[part * TILE : (part + 1) * TILE]
        sums_ref[part, 1:2, :] = jnp.sum(grad, axis=0, keepdims=True)
        sums_ref[part, 2:3, :] = jnp.sum(grad * normal, axis=0, keepdims=True)
        grad_middle = cot_ref[at, :].astype(F32) * mask_column(part) + layer_norm_back(
            grad, normal, root, gain * (1.0 + table(part, 4))
        )
        gmid_ref[at, :] = grad_middle
        sums_ref[part, 0:1, :] = jnp.sum(grad_middle * branch_s[at, :], axis=0, keepdims=True)
        right_ref[at, FF + D :] = (grad_middle * table(part, 2)).astype(BF)
    gatt_ref[...] = mm(right_ref[:, FF + D :], wo[...], NT).astype(BF)


def middle_part(units, order, core, tiles, att, x, cot, mask, modulation, flat, rows=256):
    row = lambda width: pl.BlockSpec((rows, width), lambda i: (i, 0))
    shape = lambda s, t: jax.ShapeDtypeStruct(s, t)
    return pl.pallas_call(
        functools.partial(middle_kernel, rows),
        grid=(SLOTS // rows,),
        in_specs=[SMALL_VMEM] * 3 + [pl.BlockSpec(memory_space=HBM)] * 16
        + [row(D), row(D), row(D), whole((BLOCKS, TILE)), whole((NSEG, 6 * D)), whole((FLAT_ROWS, 128))],
        out_specs=[row(D), row(FF + 2 * D), row(FF + 2 * D), row(D), row(D),
                   pl.BlockSpec((rows // TILE, 8, D), lambda i: (i, 0, 0)), whole((8, FF + D))],
        out_shape=[shape((SLOTS, D), BF), shape((SLOTS, FF + 2 * D), BF), shape((SLOTS, FF + 2 * D), BF),
                   shape((SLOTS, D), F32), shape((SLOTS, D), BF), shape((BLOCKS, 8, D), F32), shape((8, FF + D), F32)],
        scratch_shapes=[pltpu.VMEM((D, D), BF), pltpu.VMEM((D, FF), BF), pltpu.VMEM((FF, D), BF),
                        pltpu.VMEM((rows, FF), F32), pltpu.VMEM((rows, D), F32), pltpu.VMEM((rows, D), F32),
                        pltpu.SemaphoreType.DMA((8 * UNITS,))],
        cost_estimate=pl.CostEstimate(flops=4 * SLOTS * D * (D + 2 * FF), bytes_accessed=50 * 2**20, transcendentals=SLOTS * FF),
        compiler_params=pltpu.CompilerParams(vmem_limit_bytes=60 * 2**20),
    )(order, core, tiles, *units, att, x, cot, mask, modulation, flat)


def later_grads_kernel(core_ref, left_ref, right_ref, mine_ref, give_ref, buffer, sems):
    step = pl.program_id(0)
    steps = 2 * (FF // D) + 1
    slot = step % 2
    down_steps = FF // D
    core = core_ref[0]

    def wait(at_slot):
        for number in range(16):
            pltpu.make_async_copy(buffer.at[at_slot, number], buffer.at[at_slot, number], sems.at[at_slot, number]).wait()

    @pl.when(step >= 2)
    def _():
        wait(slot)

    product = mm(left_ref[...], right_ref[...], TN).astype(BF)
    buffer[slot] = product.reshape(16, 48, D)

    @pl.when(step < down_steps)
    def _():
        for number in range(16):
            local, side, block = number // 4, (number // 2) % 2, number % 2
            for ref, wanted in ((mine_ref, 0), (give_ref, 1)):
                @pl.when((core ^ side) == wanted)
                def _(ref=ref):
                    pltpu.make_async_copy(
                        buffer.at[slot, number],
                        ref.at[4 * step + local, :, pl.ds(DOWN_AT + block * D, D)],
                        sems.at[slot, number],
                    ).start()

    for j in range(down_steps):
        @pl.when(step == down_steps + j)
        def _():
            for number in range(16):
                for ref, wanted in ((mine_ref, 0), (give_ref, 1)):
                    @pl.when((core ^ (j // 2)) == wanted)
                    def _(ref=ref):
                        pltpu.make_async_copy(
                            buffer.at[slot, number],
                            ref.at[number, :, pl.ds(UP_AT + (j % 2) * D, D)],
                            sems.at[slot, number],
                        ).start()

    @pl.when(step == steps - 1)
    def _():
        for number in range(16):
            for side in range(2):
                for ref, wanted in ((mine_ref, 0), (give_ref, 1)):
                    @pl.when((core ^ side) == wanted)
                    def _(ref=ref):
                        pltpu.make_async_copy(
                            buffer.at[slot, number, :, pl.ds(side * (D // 2), D // 2)],
                            ref.at[number, :, pl.ds(OUT_AT, D // 2)],
                            sems.at[slot, number],
                        ).start()
        wait(1 - slot)
        wait(slot)


def later_grads(core, left, right):
    chunks = FF // D
    left_at = lambda i: (0, jnp.minimum(i, chunks) + jnp.maximum(i - 2 * chunks + 1, 0))
    right_at = lambda i: (0, jnp.maximum(i - chunks + 1, 0))
    shape = jax.ShapeDtypeStruct((UNITS, 48, SECOND_WIDE), BF)
    return pl.pallas_call(
        later_grads_kernel,
        grid=(2 * chunks + 1,),
        in_specs=[SMALL_VMEM, pl.BlockSpec((SLOTS, D), left_at), pl.BlockSpec((SLOTS, D), right_at)],
        out_specs=[pl.BlockSpec(memory_space=HBM)] * 2,
        out_shape=[shape, shape],
        scratch_shapes=[pltpu.VMEM((2, 16, 48, D), BF), pltpu.SemaphoreType.DMA((2, 16))],
        cost_estimate=pl.CostEstimate(flops=2 * SLOTS * D * (2 * FF + D), bytes_accessed=40 * 2**20, transcendentals=0),
        compiler_params=pltpu.CompilerParams(vmem_limit_bytes=48 * 2**20),
    )(core, left, right)


def qkv_grads_kernel(core_ref, first_ref, g_ref, mine_ref, give_ref, units, sems):
    step = pl.program_id(0)
    core = core_ref[0]
    product = mm(first_ref[...], g_ref[0], TN).astype(BF).reshape(UNITS, 48, D)

    @pl.when(step == 0)
    def _():
        units[0, :, :, 0:D] = product

    @pl.when(step == 1)
    def _():
        units[0, :, :, D:] = product[:, :, : D // 2]
        units[1, :, :, 0 : D // 2] = product[:, :, D // 2 :]

    @pl.when(step == 2)
    def _():
        units[1, :, :, D // 2 :] = product
        copies = [
            pltpu.make_async_copy(units.at[core], mine_ref, sems.at[0]),
            pltpu.make_async_copy(units.at[1 - core], give_ref, sems.at[1]),
        ]
        for copy in copies:
            copy.start()
        for copy in copies:
            copy.wait()


def qkv_grads(core, first, g):
    shape = jax.ShapeDtypeStruct((UNITS, 48, QKV_HALF), BF)
    return pl.pallas_call(
        qkv_grads_kernel,
        grid=(3,),
        in_specs=[SMALL_VMEM, whole((SLOTS, D)), pl.BlockSpec((1, SLOTS, D), lambda i: (i, 0, 0))],
        out_specs=[pl.BlockSpec(memory_space=HBM)] * 2,
        out_shape=[shape, shape],
        scratch_shapes=[pltpu.VMEM((2, UNITS, 48, QKV_HALF), BF), pltpu.SemaphoreType.DMA((2,))],
        cost_estimate=pl.CostEstimate(flops=SLOTS * D * D, bytes_accessed=2**20, transcendentals=0),
        compiler_params=pltpu.CompilerParams(vmem_limit_bytes=48 * 2**20),
    )(core, first, g)


def last_kernel(rows, places_ref, tiles_ref, member_ref, g_ref, w_ref, x_ref, gmid_ref, mod_ref, flat_ref, cond_ref,
                sums_in, bias_in, gin_ref, own_ref, first_ref, second_ref, far_ref, sums, units, sems):
    step = pl.program_id(0)
    tiles = rows // TILE
    steps = SLOTS // rows
    gain = line(flat_ref, 0, D // 128)

    grad = None
    for kind in range(3):
        share = mm(g_ref[kind], w_ref[:, kind * D : (kind + 1) * D], NT)
        grad = share if grad is None else grad + share
    for part in range(tiles):
        at = pl.ds(part * TILE, TILE)
        tile = step * tiles + part
        segment = tiles_ref[tile]
        normal, root = layer_norm(x_ref[at, :].astype(F32))
        piece = grad[part * TILE : (part + 1) * TILE]
        scale = mod_ref[pl.ds(segment, 1), D : 2 * D]
        sums[pl.ds(tile, 1), 0:D] = jnp.sum(piece, axis=0, keepdims=True)
        sums[pl.ds(tile, 1), D : 2 * D] = jnp.sum(piece * normal, axis=0, keepdims=True)
        gin_ref[at, :] = gmid_ref[at, :] + layer_norm_back(piece, normal, root, gain * (1.0 + scale))

    @pl.when(step == steps - 1)
    def _():
        gain_two = line(flat_ref, D // 128, D // 128)
        for tile in range(BLOCKS):
            at = pl.ds(tile, 1)
            sums[at, 2 * D : 3 * D] = sums_in[tile, 0:1, :]
            sums[at, 3 * D : 4 * D] = sums_in[tile, 1:2, :]
            sums[at, 4 * D : 5 * D] = sums_in[tile, 2:3, :]
            sums[at, 5 * D : 6 * D] = sums_in[tile, 3:4, :]
        member = member_ref[...]
        scale_one = lax.dot_general(member, mod_ref[:, D : 2 * D], NN, precision=lax.Precision.HIGHEST, preferred_element_type=F32)
        scale_two = lax.dot_general(member, mod_ref[:, 4 * D : 5 * D], NN, precision=lax.Precision.HIGHEST, preferred_element_type=F32)
        grad_gain_one = jnp.sum(sums[:, D : 2 * D] * (1.0 + scale_one), axis=0, keepdims=True)
        grad_gain_two = jnp.sum(sums[:, 4 * D : 5 * D] * (1.0 + scale_two), axis=0, keepdims=True)
        sums[:, D : 2 * D] = sums[:, D : 2 * D] * gain
        sums[:, 4 * D : 5 * D] = sums[:, 4 * D : 5 * D] * gain_two
        by_segment = lax.dot_general(member, sums[...], TN, precision=lax.Precision.HIGHEST, preferred_element_type=F32)
        grad_mod = lax.dot_general(
            by_segment, cond_ref[...].astype(F32), TN, precision=lax.Precision.HIGHEST, preferred_element_type=F32
        ).astype(BF).reshape(4, 4, 6, 48, COND)
        for block in range(6):
            units[:, :, :, block * COND : (block + 1) * COND] = grad_mod[:, :, block]
        row = jnp.concatenate(
            [grad_gain_one, grad_gain_two, bias_in[0:1, :], jnp.sum(by_segment, axis=0, keepdims=True)], axis=1
        )
        lane = lax.broadcasted_iota(jnp.int32, (1, 128), 1)
        blank = jnp.zeros((43, 128), F32)
        for part in range(UNITS):
            start = VECTOR_PART * part
            pieces = []
            for number in range(5):
                first_row, turn = divmod(start + 128 * number, 128)
                piece = row[:, first_row * 128 : (first_row + 1) * 128]
                if turn:
                    following = (
                        row[:, (first_row + 1) * 128 : (first_row + 2) * 128]
                        if (first_row + 2) * 128 <= row.shape[1]
                        else jnp.zeros((1, 128), F32)
                    )
                    piece = jnp.where(
                        lane < 128 - turn, pltpu.roll(piece, 128 - turn, 1), pltpu.roll(following, 128 - turn, 1)
                    )
                if number == 4:
                    piece = jnp.where(lane < VECTOR_PART - 512, piece, 0.0)
                pieces.append(piece)
            stack = jnp.concatenate(pieces + [blank], axis=0).astype(BF)
            units[part // 4, part % 4, :, 6 * COND :] = stack
        copies = [
            pltpu.make_async_copy(units.at[:, places_ref[kind]], ref, sems.at[kind])
            for kind, ref in enumerate((own_ref, first_ref, second_ref, far_ref))
        ]
        for copy in copies:
            copy.start()
        for copy in copies:
            copy.wait()


def last_part(places, tiles, member, g, w, x, gmid, modulation, flat, cond, sums, bias, rows=256):
    row = lambda width: pl.BlockSpec((rows, width), lambda i: (i, 0))
    shape = jax.ShapeDtypeStruct((4, 48, SMALL_WIDE), BF)
    return pl.pallas_call(
        functools.partial(last_kernel, rows),
        grid=(SLOTS // rows,),
        in_specs=[SMALL_VMEM, SMALL_VMEM, whole((BLOCKS, NSEG)), pl.BlockSpec((3, rows, D), lambda i: (0, i, 0)), whole((D, 3 * D)),
                  row(D), row(D), whole((NSEG, 6 * D)), whole((FLAT_ROWS, 128)), whole((NSEG, COND)),
                  whole((BLOCKS, 8, D)), whole((8, FF + D))],
        out_specs=[row(D)] + [pl.BlockSpec(memory_space=HBM)] * 4,
        out_shape=[jax.ShapeDtypeStruct((SLOTS, D), F32)] + [shape] * 4,
        scratch_shapes=[pltpu.VMEM((BLOCKS, 6 * D), F32), pltpu.VMEM((4, 4, 48, SMALL_WIDE), BF),
                        pltpu.SemaphoreType.DMA((4,))],
        cost_estimate=pl.CostEstimate(flops=2 * SLOTS * D * 3 * D, bytes_accessed=30 * 2**20, transcendentals=SLOTS),
        compiler_params=pltpu.CompilerParams(vmem_limit_bytes=60 * 2**20),
    )(places, tiles, member, g, w, x, gmid, modulation, flat, cond, sums, bias)


def moments(weight_ref, first_ref, second_ref, gradient, first_out, second_out, direction_out, decay_rate=DECAY_RATE):
    weight = weight_ref[...]
    first_new = BETA_ONE * first_ref[...] + (1.0 - BETA_ONE) * gradient
    second_new = BETA_TWO * second_ref[...] + (1.0 - BETA_TWO) * gradient * gradient
    direction = (
        first_new
        / (1.0 - BETA_ONE**STEP)
        / (jnp.sqrt(second_new / (1.0 - BETA_TWO**STEP)) + EPSILON)
        + decay_rate * weight
    )
    first_out[...] = first_new
    second_out[...] = second_new
    direction_out[...] = direction
    return [jnp.sum(values * values, axis=(0, 1), keepdims=True) for values in (weight, direction)]


def squares_table(pairs):
    row = lax.broadcasted_iota(jnp.int32, (8, 128), 0)
    lane = lax.broadcasted_iota(jnp.int32, (8, 128), 1)
    table = jnp.zeros((8, 128), F32)
    for number, sums in pairs:
        for kind in range(2):
            table = jnp.where((row == kind) & (lane == number), sums[kind], table)
    return table


def update_later_kernel(side_ref, own_ref, other_ref, *refs):
    outs, table_ref = refs[9:18], refs[18]
    zero = side_ref[0] == 0
    own, other = own_ref[...].astype(F32), other_ref[...].astype(F32)
    halves = (jnp.where(zero, own, other), jnp.where(zero, other, own))
    out_grad = jnp.concatenate([half[:, OUT_AT:] for half in halves], axis=1)
    up_grad = jnp.concatenate([half[:, UP_AT : UP_AT + FF // 2] for half in halves], axis=1)
    down_grad = jnp.concatenate(
        [half[:, DOWN_AT + D * part : DOWN_AT + D * (part + 1)] for half in halves for part in range(2)], axis=0
    )
    table_ref[...] = squares_table(
        [
            (1 + place, moments(*refs[3 * place : 3 * place + 3], gradient, *outs[3 * place : 3 * place + 3]))
            for place, gradient in enumerate((out_grad, up_grad, down_grad))
        ]
    )


def update_sooner_kernel(side_ref, own_ref, other_ref, small_ref, *refs):
    outs, table_ref = refs[6:12], refs[12]
    zero = side_ref[0] == 0
    own, other = own_ref[...].astype(F32), other_ref[...].astype(F32)
    qkv_grad = jnp.concatenate([jnp.where(zero, own, other), jnp.where(zero, other, own)], axis=1)
    mod_grad = jnp.concatenate([small_ref[:, COND * part : COND * (part + 1)] for part in range(6)], axis=0)
    table_ref[...] = squares_table(
        [
            (4 * place, moments(*refs[3 * place : 3 * place + 3], gradient, *outs[3 * place : 3 * place + 3]))
            for place, gradient in enumerate((qkv_grad, mod_grad))
        ]
    )


def update_moments(kernel, side, parts, arrays):
    block = pl.BlockSpec(memory_space=pltpu.VMEM)
    shapes = [jax.ShapeDtypeStruct(arrays[3 * (i // 3)].shape, F32) for i in range(len(arrays))]
    *outs, table = pl.pallas_call(
        kernel,
        in_specs=[SMALL_VMEM] + [block] * (len(parts) + len(arrays)),
        out_specs=[block] * (len(arrays) + 1),
        out_shape=shapes + [jax.ShapeDtypeStruct((8, 128), F32)],
        compiler_params=pltpu.CompilerParams(vmem_limit_bytes=48 * 2**20),
    )(side, *parts, *arrays)
    return [outs[i : i + 3] for i in range(0, len(outs), 3)], table


def renew_kernel(table_ref, *refs):
    norms_ref = refs[15]
    roots = jnp.sqrt(table_ref[...])
    norms_ref[...] = roots[:2, :5]
    for number in range(5):
        trust = roots[0:1, number : number + 1] / (roots[1:2, number : number + 1] + EPSILON)
        refs[10 + number][...] = refs[number][...] - (MATRIX_RATE * trust) * refs[5 + number][...]


def renew(table, matrices, turns):
    block = pl.BlockSpec(memory_space=pltpu.VMEM)
    return pl.pallas_call(
        renew_kernel,
        in_specs=[block] * 11,
        out_specs=[block] * 6,
        out_shape=[jax.ShapeDtypeStruct(matrix.shape, F32) for matrix in matrices] + [jax.ShapeDtypeStruct((2, 5), F32)],
        compiler_params=pltpu.CompilerParams(vmem_limit_bytes=48 * 2**20),
    )(table, *matrices, *turns)


ALONG = ((1, 2), (2, 1))


def column_of(core, chip, kind):
    first, second = ALONG[core]
    return (chip % 4) ^ (0, first, second, first ^ second)[kind]


ORIGIN = np.array(
    [
        [[column_of(core, chip, kind) + 4 * ((chip // 4 - back) % 4) for kind in range(4) for back in range(4)]
         for chip in range(UNITS)]
        for core in range(2)
    ],
    np.int32,
)
PLACES = np.array(
    [
        [[column_of(core, chip, kind) for kind in range(4)] + [(chip // 4 + ahead) % 4 for ahead in range(4)]
         for chip in range(UNITS)]
        for core in range(2)
    ],
    np.int32,
)


def along_z(values, ahead):
    return lax.ppermute(values, "fsdp", [(chip, chip % 4 + 4 * ((chip // 4 + ahead) % 4)) for chip in range(UNITS)])


def along_plane(values, direction):
    moves = [
        (core * UNITS + chip, core * UNITS + (chip ^ ALONG[core][direction]))
        for core in range(2)
        for chip in range(UNITS)
    ]
    return lax.ppermute(values, ("rep", "fsdp"), moves)


def across_plane(values):
    return lax.ppermute(values, "fsdp", [(chip, chip ^ 3) for chip in range(UNITS)])


def swap_core(values):
    return lax.ppermute(values, "rep", [(0, 1), (1, 0)])


def hold_back(later, sooner):
    return lax.optimization_barrier((later, sooner))[0]


def by_rounds():
    return lax.axis_size("fsdp") == UNITS


def far_from(near):
    return along_plane(near[0], 1)


def near_of(piece):
    return [along_plane(piece, 0), along_plane(piece, 1)]


def swapped(values):
    return [swap_core(one) for one in values]


def column_sums_kernel(counts, places_ref, *refs):
    outs = refs[len(refs) - len(counts) :]
    at = 0
    for out_ref, count in zip(outs, counts):
        total = refs[at][...].astype(F32) + refs[at + 1][...].astype(F32)
        for arrived in refs[at + 2 : at + 2 + count]:
            total = total + arrived[...].astype(F32).reshape(total.shape)
        out_ref[...] = total.astype(BF).reshape(out_ref.shape)
        at += 2 + count


def column_sums(places, mine, given, parts, apart=False):
    block = mine.shape[1:]
    pair = [values.reshape((4, 4) + block) for values in (mine, given)]
    specs, operands, counts = [], [], []
    for ahead in range(4) if apart else (None,):
        for kind, arrived in parts:
            if apart:
                pick = pl.BlockSpec((1, 1) + block, lambda i, s, kind=kind, ahead=ahead: (s[4 + ahead], s[kind], 0, 0))
                came = pl.BlockSpec((1,) + block, lambda i, s, ahead=ahead: (s[4 + ahead], 0, 0))
            else:
                pick = pl.BlockSpec((1, 1) + block, lambda i, s, kind=kind: (i, s[kind], 0, 0))
                came = pl.BlockSpec((1,) + block, lambda i, s: (i, 0, 0))
            specs += [pick, pick] + [came] * len(arrived)
            operands += pair + arrived
            counts.append(len(arrived))
    if apart:
        out_spec, out_shape = pl.BlockSpec(block, lambda i, s: (0, 0)), jax.ShapeDtypeStruct(block, BF)
    else:
        out_spec, out_shape = pl.BlockSpec((1,) + block, lambda i, s: (i, 0, 0)), jax.ShapeDtypeStruct((4,) + block, BF)
    return pl.pallas_call(
        functools.partial(column_sums_kernel, counts),
        grid_spec=pltpu.PrefetchScalarGridSpec(
            num_scalar_prefetch=1,
            grid=(1 if apart else 4,),
            in_specs=specs,
            out_specs=[out_spec] * len(counts),
        ),
        out_shape=[out_shape] * len(counts),
        cost_estimate=pl.CostEstimate(flops=0, bytes_accessed=(200 if apart else 12) * 2**20, transcendentals=0),
        compiler_params=pltpu.CompilerParams(vmem_limit_bytes=48 * 2**20),
    )(places, *operands)


class Scatter:
    def __init__(self, mine, give, places):
        self.mine, self.places = mine, places
        self.given = swap_core(give)

    def send_plane(self, sooner=None):
        given = self.given if sooner is None else hold_back(self.given, sooner)
        sums = column_sums(self.places, self.mine, given, [(3, []), (1, []), (2, [])])
        self.arrived = [across_plane(sums[0]), along_plane(sums[1], 0), along_plane(sums[2], 1)]
        return sums[0]

    def send_far(self, sooner=None):
        given = self.given if sooner is None else hold_back(self.given, sooner)
        far, second = column_sums(self.places, self.mine, given, [(3, []), (2, [])])
        self.far_came, self.second_came = along_plane(far, 1), along_plane(second, 1)
        return far

    def send_first(self, sooner=None):
        self.far_came, self.second_came = (
            (self.far_came, self.second_came) if sooner is None else hold_back((self.far_came, self.second_came), sooner)
        )
        (first,) = column_sums(self.places, self.mine, self.given, [(1, [self.far_came])])
        self.arrived = [along_plane(first, 0), self.second_came]
        return first

    def send_column(self, sooner=None):
        arrived = self.arrived if sooner is None else hold_back(self.arrived, sooner)
        units = column_sums(self.places, self.mine, self.given, [(0, arrived)], apart=True)
        self.own = units[0]
        self.came = [along_z(units[ahead], ahead) for ahead in range(1, 4)]
        return self.own

    def finish(self, sooner=None):
        came = self.came if sooner is None else hold_back(self.came, sooner)
        total = self.own.astype(F32)
        for part in came:
            total = total + part.astype(F32)
        own = total.astype(BF)
        return (own, swap_core(own))


def arrivals_kernel(*refs):
    inputs, outs = refs[1 : len(refs) - 4], refs[len(refs) - 4 :]
    each = len(inputs) // 4
    for number, out_ref in enumerate(outs):
        total = inputs[number * each][0].astype(F32)
        for part in inputs[number * each + 1 : (number + 1) * each]:
            total = total + part[0].astype(F32)
        out_ref[...] = total.astype(BF)


class SmallScatter:
    def __init__(self, own, first, second, far, places):
        self.places = places
        self.parts = [own, across_plane(far), along_plane(first, 0), along_plane(second, 1)]

    def send_column(self, sooner=None):
        parts = self.parts if sooner is None else hold_back(self.parts, sooner)
        block = parts[0].shape[1:]
        picks = [
            pl.BlockSpec((1,) + block, lambda i, s, ahead=ahead: (s[4 + ahead], 0, 0)) for ahead in range(4) for _ in parts
        ]
        self.own, *units = pl.pallas_call(
            arrivals_kernel,
            grid_spec=pltpu.PrefetchScalarGridSpec(
                num_scalar_prefetch=1, grid=(1,), in_specs=picks, out_specs=[pl.BlockSpec(block, lambda i, s: (0, 0))] * 4
            ),
            out_shape=[jax.ShapeDtypeStruct(block, BF)] * 4,
        )(self.places, *(parts * 4))
        self.came = [along_z(unit, ahead + 1) for ahead, unit in enumerate(units)]
        return self.own

    def finish(self):
        total = self.own.astype(F32)
        for part in self.came:
            total = total + part.astype(F32)
        own = total.astype(BF)
        return own.astype(F32) + swap_core(own).astype(F32)


def sum_small(values):
    for turn in (1, 2, 4, 8):
        values = values + lax.ppermute(values, "fsdp", [(chip, chip ^ turn) for chip in range(UNITS)])
    return values


def side_columns(matrix, core, width):
    return lax.dynamic_slice_in_dim(matrix, core * width, width, axis=1)


def side_rows(blocks, core):
    return lax.dynamic_index_in_dim(blocks, core, 1, keepdims=False)


def pack_first(qkv, mod_turned, vectors, core):
    count = vectors.shape[0]
    mod_blocks = side_rows(mod_turned.reshape(count, 2, 3, 48, COND), core)
    padded = jnp.pad(vectors, ((0, 0), (0, 640 - VECTOR_PART))).reshape(count, 5, 128)
    return jnp.concatenate(
        [
            side_columns(qkv, core, QKV_HALF).reshape(count, 48, QKV_HALF),
            mod_blocks.transpose(0, 2, 1, 3).reshape(count, 48, 3 * COND),
            jnp.pad(padded, ((0, 0), (0, 43), (0, 0))),
        ],
        axis=2,
    )


def pack_second(out, up, down, core):
    count = out.shape[0] // 48
    down_blocks = side_rows(down.reshape(count, 2, 2, 48, D), core)
    return jnp.concatenate(
        [
            side_columns(up, core, FF // 2).reshape(count, 48, FF // 2),
            down_blocks.transpose(0, 2, 1, 3).reshape(count, 48, 2 * D),
            side_columns(out, core, D // 2).reshape(count, 48, D // 2),
        ],
        axis=2,
    )


def unpack_qkv(sides):
    return jnp.concatenate([side for side in sides], axis=2).reshape(-1, 3 * D)


def unpack_small(own, first, second, far):
    units = jnp.stack([own, first, second, far], axis=1).reshape(UNITS, 48, SMALL_WIDE)
    turned = units[:, :, : 6 * COND].reshape(UNITS, 48, 6, COND).transpose(0, 2, 1, 3).reshape(6 * D, COND)
    vectors = units[:, :5, 6 * COND :].reshape(UNITS, 640)[:, :VECTOR_PART]
    return (turned.T, vectors.reshape(-1))


def unpack_second(sides):
    count = sides[0].shape[0]
    up = jnp.concatenate([side[:, :, UP_AT : UP_AT + FF // 2] for side in sides], axis=2).reshape(count * 48, FF)
    out = jnp.concatenate([side[:, :, OUT_AT:] for side in sides], axis=2).reshape(count * 48, D)
    down = jnp.stack([side[:, :, DOWN_AT : DOWN_AT + 2 * D] for side in sides], axis=1)
    down = down.reshape(count, 2, 48, 2, D).transpose(0, 1, 3, 2, 4).reshape(count * 192, D)
    return (out, up, down)


def gather_plain(parts, axes):
    return [lax.all_gather(part, "fsdp", axis=axis, tiled=True) for part, axis in zip(parts, axes)]


def virtual_units(pack, cuts):
    return [
        packed[4 * part + start : 4 * part + stop] for packed in (pack(0), pack(1)) for part in range(4) for start, stop in cuts
    ]


def reduce_plain(grads, axes):
    parts = [
        lax.psum_scatter(grad.astype(F32), "fsdp", scatter_dimension=axis, tiled=True) for grad, axis in zip(grads, axes)
    ]
    return tuple(lax.psum(part.astype(BF), "rep").astype(F32) for part in parts)


def adam_direction(weight, first_old, second_old, gradient, decay_rate):
    first_new = BETA_ONE * first_old + (1.0 - BETA_ONE) * gradient
    second_new = BETA_TWO * second_old + (1.0 - BETA_TWO) * gradient * gradient
    direction = (
        first_new
        / (1.0 - BETA_ONE**STEP)
        / (jnp.sqrt(second_new / (1.0 - BETA_TWO**STEP)) + EPSILON)
        + decay_rate * weight
    )
    return (first_new, second_new, direction)


def layout_tables(sizes_row, lengths_row):
    slot_ids = jnp.arange(SLOTS, dtype=jnp.int32)
    seg_ends = jnp.cumsum(sizes_row)
    starts = seg_ends - sizes_row
    segment = jnp.sum((slot_ids[:, None] >= seg_ends[None, :]).astype(jnp.int32), axis=1)
    member = segment[:, None] == jnp.arange(NSEG, dtype=jnp.int32)[None, :]
    offset = jnp.sum(jnp.where(member, starts[None, :], 0), axis=1)
    length_of = jnp.sum(jnp.where(member, lengths_row[None, :], 0), axis=1)
    position = slot_ids - offset
    return (segment, member, position, position < length_of)


def condition(steps_row):
    half_cond = COND // 2
    frequency = jnp.exp(jnp.arange(half_cond, dtype=F32) * (-math.log(10000.0) / half_cond))
    angles = steps_row.astype(F32)[:, None] * frequency[None, :]
    return jax.nn.silu(jnp.concatenate([jnp.cos(angles), jnp.sin(angles)], axis=1))


FORWARD_CALLS = (2, 3, 1)
BACKWARD_CALLS = (1, 3, 2)


def on_device(
    inputs, cotangent, seg_sizes, seq_lengths, timesteps, absorbed,
    qkv_weight, out_weight, up_weight, down_weight, mod_weight,
    qkv_first, out_first, up_first, down_first, mod_first,
    qkv_second, out_second, up_second, down_second, mod_second,
    vectors, vectors_first, vectors_second,
):
    rounds = by_rounds()
    chip = lax.axis_index("fsdp")
    core = lax.axis_index("rep")
    matrices = (qkv_weight, out_weight, up_weight, down_weight, mod_weight)
    qkv_low, out_low, up_low, down_low, mod_low = [matrix.astype(BF) for matrix in matrices]
    vector_low = vectors.astype(BF)
    if rounds:
        order = jnp.concatenate([jnp.asarray(ORIGIN)[core, chip], jnp.asarray(ORIGIN)[1 - core, chip]])
        places = jnp.asarray(PLACES)[core, chip]
        side = core[None].astype(jnp.int32)
        unit_first = pack_first(qkv_low, mod_low.T, vector_low[None], core)[0]
        unit_second = pack_second(out_low, up_low, down_low, core)[0]
        second_one = unit_second[None]
        first_back = [along_z(unit_first, back) for back in range(1, 4)]
        second_near = near_of(second_one)
        first_column = jnp.stack([unit_first] + first_back)
        first_near = near_of(first_column)
        second_from = hold_back(unit_second, first_column)
        second_back = [along_z(second_from, back) for back in range(1, 4)]
        second_far = far_from(second_near)
        first_near[0] = hold_back(first_near[0], (second_far, second_near, second_back))
        units_first = [first_column] + first_near + [far_from(first_near)]
        units_first = units_first + swapped(units_first)
    else:
        order = jnp.concatenate([jnp.arange(UNITS, dtype=jnp.int32)] * 2)
        places = jnp.asarray(PLACES)[0, 0]
        side = jnp.zeros((1,), jnp.int32)
        qkv_all, mod_all, vector_all = gather_plain((qkv_low, mod_low, vector_low), (0, 1, 0))
        out_all, up_all, down_all = gather_plain((out_low, up_low, down_low), (0, 0, 0))
        units_first = virtual_units(lambda s: pack_first(qkv_all, mod_all.T, vector_all.reshape(UNITS, -1), s), ((0, 4),))
        units_second = virtual_units(lambda s: pack_second(out_all, up_all, down_all, s), ((0, 1), (1, 4)))

    segment, member, position, valid_slot = layout_tables(seg_sizes[0], seq_lengths[0])
    tiles = segment.reshape(BLOCKS, TILE)[:, 0]
    member_tile = member.reshape(BLOCKS, TILE, NSEG)[:, 0].astype(F32)
    condition_low = condition(timesteps[0]).astype(BF)
    cos, sin, feature_query, feature_key = attention_tables(segment, position, valid_slot)
    weight_mask = (absorbed[0] * valid_slot.astype(jnp.int32)).astype(F32).reshape(BLOCKS, TILE)
    row_in, row_cot = inputs[0], cotangent[0]

    mixed, first_low, qkv_full, modulation, flat = first_part(
        units_first, order, side, tiles, row_in, condition_low, cos, sin
    )
    forward, first_pair = None, 0
    if rounds:
        second_rest = jnp.stack(second_back)
        second_rest_near = near_of(second_rest)
    for number, count in enumerate(FORWARD_CALLS):
        if rounds and number == 1:
            second_rest_far = far_from(hold_back(second_rest_near, forward))
            second_own = [second_one, second_rest, second_near[0], second_rest_near[0], second_near[1], second_rest_near[1]]
            second_own.append(second_far)
            second_other = swapped(hold_back(second_own, forward))
        if rounds and number == 2:
            forward, second_rest_far = hold_back((forward, second_rest_far), second_other)
        forward = attention_forward(mixed, feature_query, feature_key, forward, first_pair, count)
        first_pair += count
    if rounds:
        units_second = second_own + [second_rest_far] + second_other + [swap_core(second_rest_far)]
    attended_low, feature = forward
    out_hidden, left, right, grad_middle, grad_attended, sums, bias_sums = middle_part(
        units_second, order, side, tiles, attended_low, row_in, row_cot, weight_mask, modulation, flat
    )
    mine_later, give_later = later_grads(side, left, right)

    state = [None]

    def backward_part(number, came):
        grad_here = grad_attended if came is None else hold_back(grad_attended, came)
        state[0] = attention_backward(
            mixed, feature, feature_key, grad_here, attended_low, cos, sin, state[0],
            sum(BACKWARD_CALLS[:number]), BACKWARD_CALLS[number],
        )
        return state[0]

    def qkv_end(sooner=None):
        follows = state[0] if sooner is None else hold_back(state[0], sooner)
        return qkv_grads(side, first_low, follows)

    def row_end(sooner=None):
        follows = state[0] if sooner is None else hold_back(state[0], sooner)
        return last_part(
            places, tiles, member_tile, follows, qkv_full, row_in, grad_middle, modulation, flat, condition_low,
            sums, bias_sums,
        )

    vector_arrays = (vectors, vectors_first, vectors_second)
    of_qkv, of_out = (qkv_weight, qkv_first, qkv_second), (out_weight, out_first, out_second)
    of_up, of_down = (up_weight, up_first, up_second), (down_weight, down_first, down_second)
    of_mod = (mod_weight, mod_first, mod_second)
    if rounds:
        later = Scatter(mine_later, give_later, places)
        backward_part(0, None)
        sent = later.send_far(state[0])
        backward_part(1, sent)
        sent = later.send_first(state[0])
        backward_part(2, sent)
        sent = later.send_column(state[0])
        qkv_parts = qkv_end(sent)
        sooner = Scatter(*qkv_parts, places)
        sent = sooner.send_plane()
        grad_in, *small_parts = row_end(sent)
        small = SmallScatter(*small_parts, places)
        sent = sooner.send_column(grad_in)
        sent = small.send_column((sent, sooner.came, later.came))
        later_sums = later.finish(sent)
        (out_new, up_new, down_new), later_table = update_moments(
            update_later_kernel, side, later_sums, of_out + of_up + of_down
        )
        qkv_sums = sooner.finish(sent)
        small_sums = small.finish()
        (qkv_new, mod_new), sooner_table = update_moments(
            update_sooner_kernel, side, qkv_sums + (small_sums,), of_qkv + tuple(part.T for part in of_mod)
        )
        results = [qkv_new, out_new, up_new, down_new, mod_new]
        *renewed, norm_roots = renew(
            sum_small(later_table + sooner_table),
            [*matrices[:4], mod_weight.T],
            [record[2] for record in results],
        )
        renewed[4] = renewed[4].T
        results[4] = [part.T for part in mod_new]
        grad_vectors = small_sums[:5, 6 * COND :].reshape(-1)[:VECTOR_PART]
    else:
        for number in range(3):
            backward_part(number, None)
        grad_out, grad_up, grad_down = reduce_plain(unpack_second((mine_later, give_later)), (0, 0, 0))
        grad_in, *small_parts = row_end()
        grad_qkv, grad_mod, grad_vectors = reduce_plain(
            (unpack_qkv(qkv_end()), *unpack_small(*small_parts)), (0, 1, 0)
        )
        grads = (grad_qkv, grad_out, grad_up, grad_down, grad_mod)
        olds = (of_qkv, of_out, of_up, of_down, of_mod)
        results = [adam_direction(*old, grad, DECAY_RATE) for old, grad in zip(olds, grads)]
        squares = [
            jnp.stack([jnp.sum(values[number] * values[number]) for number in range(5)])
            for values in (matrices, [record[2] for record in results])
        ]
        norm_roots = jnp.sqrt(lax.psum(jnp.stack(squares), "fsdp"))
        trust = norm_roots[0] / (norm_roots[1] + EPSILON)
        renewed = [matrices[number] - MATRIX_RATE * trust[number] * results[number][2] for number in range(5)]
    vector_record = adam_direction(*vector_arrays, grad_vectors, 0.0)
    return (
        out_hidden[None],
        grad_in[None],
        *renewed,
        *[record[0] for record in results],
        *[record[1] for record in results],
        vectors - VECTOR_RATE * vector_record[2],
        vector_record[0],
        vector_record[1],
        norm_roots,
    )


def solution(mesh):
    rows = P(("rep", "fsdp"))
    matrix, turned, vector = P("fsdp", None), P(None, "fsdp"), P("fsdp")
    five = (matrix, matrix, matrix, matrix, turned)
    return jax.shard_map(
        on_device,
        mesh=mesh,
        in_specs=(rows,) * 6 + five * 3 + (vector,) * 3,
        out_specs=(rows, rows) + five * 3 + (vector,) * 3 + (P(),),
        check_vma=False,
    )
```

```python
import functools
import math

import jax
import jax.numpy as jnp
import numpy as np
from jax import lax
from jax.experimental import pallas as pl
from jax.experimental.pallas import tpu as pltpu
from jax.sharding import PartitionSpec as P

D = 768
HEADS = 12
HDIM = 64
FF = 3072
COND = 128
SLOTS = 1024
NSEG = 8
STEP = 10
TILE = 128
BLOCKS = SLOTS // TILE

BETA_ONE = 0.9
BETA_TWO = 0.999
EPSILON = 1e-06
DECAY_RATE = 0.01
MATRIX_RATE = 0.3
VECTOR_RATE = 1.0

PAIR = 128
NT = (((1,), (1,)), ((), ()))
NN = (((1,), (0,)), ((), ()))
TN = (((0,), (0,)), ((), ()))
BF = jnp.bfloat16
F32 = jnp.float32


def mm(a, b, dims=NN):
    return lax.dot_general(a, b, dims, preferred_element_type=F32)


def swap_halves(v):
    lane = lax.broadcasted_iota(jnp.int32, v.shape, 1)
    return jnp.where(lane % 64 < 32, pltpu.roll(v, PAIR - 32, 1), pltpu.roll(v, 32, 1))


def attention_forward_kernel(block, q_ref, k_ref, v_ref, fq_ref, fk_ref, *refs):
    o_ref, fo_ref, ka, kb, va, vb = refs[-6:]
    slots = q_ref.shape[0]
    low_all = lax.broadcasted_iota(jnp.int32, (slots, PAIR), 1) < 64
    k_low = k_ref[...]
    v_low = v_ref[...]
    fk = fk_ref[...]
    one = jnp.ones((slots, PAIR), BF)
    ka[...] = jnp.where(low_all, k_low, fk)
    kb[...] = jnp.where(low_all, fk, k_low)
    va[...] = jnp.where(low_all, v_low, one)
    vb[...] = jnp.where(low_all, one, v_low)
    lane = lax.broadcasted_iota(jnp.int32, (block, PAIR), 1)
    low = lane < 64
    spot = lane % 64

    def step(i, carry):
        at = pl.ds(pl.multiple_of(i * block, block), block)
        q = q_ref[at, :]
        fq = fq_ref[at, :]
        sa = mm(jnp.where(low, q, fq), ka[...], NT)
        sb = mm(jnp.where(low, fq, q), kb[...], NT)
        ma = jnp.max(sa, axis=1, keepdims=True)
        mb = jnp.max(sb, axis=1, keepdims=True)
        pa = jnp.exp(sa - ma).astype(BF)
        pb = jnp.exp(sb - mb).astype(BF)
        oa = mm(pa, va[...])
        ob = mm(pb, vb[...])
        o = jnp.where(low, oa / pltpu.roll(oa, 64, 1), ob / pltpu.roll(ob, 64, 1))
        o_ref[at, :] = o.astype(o_ref.dtype)
        neg = jnp.where(low, -(mb + jnp.log(ob)), -(ma + jnp.log(oa)))
        hi = neg.astype(BF)
        rest = neg - hi.astype(F32)
        mid = rest.astype(BF)
        last = (rest - mid.astype(F32)).astype(BF)
        fo_ref[at, :] = jnp.where(spot == 8, hi, jnp.where(spot == 9, mid, jnp.where(spot == 10, last, fq)))
        return carry

    lax.fori_loop(0, slots // block, step, 0)


def attention_forward(qkv, fq, fk, before, first, count, block=1024):
    slots, width = qkv.shape
    pairs = width // 3 // PAIR
    blk = lambda off: pl.BlockSpec((slots, PAIR), lambda p: (0, off + p))
    fixed = pl.BlockSpec((slots, PAIR), lambda p: (0, 0))
    anywhere = pl.BlockSpec(memory_space=pl.ANY)
    shape = jax.ShapeDtypeStruct((slots, pairs * PAIR), BF)
    extra = () if before is None else before
    elements = 2 * count * slots * slots
    return pl.pallas_call(
        functools.partial(attention_forward_kernel, block),
        grid=(count,),
        in_specs=[blk(first), blk(pairs + first), blk(2 * pairs + first), fixed, fixed] + [anywhere] * len(extra),
        out_specs=[blk(first)] * 2,
        out_shape=[shape, shape],
        scratch_shapes=[pltpu.VMEM((slots, PAIR), BF)] * 4,
        input_output_aliases={5: 0, 6: 1} if extra else {},
        cost_estimate=pl.CostEstimate(flops=elements * 3000, bytes_accessed=10 * slots * count * PAIR, transcendentals=elements),
        compiler_params=pltpu.CompilerParams(vmem_limit_bytes=62 * 2**20),
    )(qkv, qkv, qkv, fq, fk, *extra)


def attention_backward_kernel(block, q_ref, k_ref, v_ref, fo_ref, fk_ref, do_ref, o_ref, cos_ref, sin_ref, *refs):
    g_ref, ka, kb, va, vb, kt, dka, dkb, dva, dvb = refs[-10:]
    slots = q_ref.shape[0]
    lane_all = lax.broadcasted_iota(jnp.int32, (slots, PAIR), 1)
    low_all = lane_all < 64
    fk = fk_ref[...]
    k_low = k_ref[...]
    v_low = v_ref[...]
    one = jnp.where(lane_all % 64 < 2, 1.0, 0.0).astype(BF)
    ka[...] = jnp.where(low_all, k_low, fk)
    kb[...] = jnp.where(low_all, fk, k_low)
    va[...] = jnp.where(low_all, v_low, one)
    vb[...] = jnp.where(low_all, one, v_low)
    kt[...] = k_low.T
    dka[...] = jnp.zeros_like(dka)
    dkb[...] = jnp.zeros_like(dkb)
    dva[...] = jnp.zeros_like(dva)
    dvb[...] = jnp.zeros_like(dvb)
    lane = lax.broadcasted_iota(jnp.int32, (block, PAIR), 1)
    low = lane < 64
    spot = lane % 64
    top = lax.broadcasted_iota(jnp.int32, (PAIR, block), 0) < 64

    def step(i, carry):
        at = pl.ds(pl.multiple_of(i * block, block), block)
        q = q_ref[at, :]
        fq = fo_ref[at, :]
        do = do_ref[at, :]
        both = do.astype(F32) * o_ref[at, :].astype(F32)
        da = jnp.sum(jnp.where(low, both, 0.0), axis=1, keepdims=True)
        db = jnp.sum(jnp.where(low, 0.0, both), axis=1, keepdims=True)
        neg = jnp.where(low, -db, -da)
        hi = neg.astype(BF)
        rest = (neg - hi.astype(F32)).astype(BF)
        fd = jnp.where(spot == 0, hi, jnp.where(spot == 1, rest, jnp.zeros_like(hi)))
        sa = mm(ka[...], jnp.where(low, q, fq), NT)
        sb = mm(kb[...], jnp.where(low, fq, q), NT)
        ea = mm(va[...], jnp.where(low, do, fd), NT)
        eb = mm(vb[...], jnp.where(low, fd, do), NT)
        pa = jnp.exp(sa)
        pb = jnp.exp(sb)
        dsa = (pa * ea).astype(BF)
        dsb = (pb * eb).astype(BF)
        dva[...] += mm(pa.astype(BF), do)
        dvb[...] += mm(pb.astype(BF), do)
        dka[...] += mm(dsa, q)
        dkb[...] += mm(dsb, q)
        dqt = jnp.where(top, mm(kt[...], dsa), mm(kt[...], dsb))
        dq = dqt.T * 0.125
        g_ref[0, at, :] = (dq * cos_ref[at, :] - swap_halves(dq) * sin_ref[at, :]).astype(BF)
        return carry

    lax.fori_loop(0, slots // block, step, 0)
    dk = jnp.where(low_all, dka[...], dkb[...])
    g_ref[1] = (dk * cos_ref[...] - swap_halves(dk) * sin_ref[...]).astype(BF)
    g_ref[2] = jnp.where(low_all, dva[...], dvb[...]).astype(BF)


def attention_backward(qkv, fo, fk, do, o, cos, sin, before, first, count, block=512):
    slots, width = qkv.shape
    pairs = width // 3 // PAIR
    blk = lambda off: pl.BlockSpec((slots, PAIR), lambda p: (0, off + p))
    fixed = pl.BlockSpec((slots, PAIR), lambda p: (0, 0))
    extra = () if before is None else (before,)
    elements = 2 * count * slots * slots
    return pl.pallas_call(
        functools.partial(attention_backward_kernel, block),
        grid=(count,),
        in_specs=[blk(first), blk(pairs + first), blk(2 * pairs + first), blk(first), fixed, blk(first), blk(first),
                  fixed, fixed] + [pl.BlockSpec(memory_space=pl.ANY)] * len(extra),
        out_specs=pl.BlockSpec((3, slots, PAIR), lambda p: (0, 0, first + p)),
        out_shape=jax.ShapeDtypeStruct((3, slots, pairs * PAIR), BF),
        scratch_shapes=[pltpu.VMEM((slots, PAIR), BF)] * 4 + [pltpu.VMEM((PAIR, slots), BF)]
        + [pltpu.VMEM((slots, PAIR), F32)] * 4,
        input_output_aliases={9: 0} if extra else {},
        cost_estimate=pl.CostEstimate(flops=elements * 2000, bytes_accessed=20 * slots * count * PAIR, transcendentals=elements),
        compiler_params=pltpu.CompilerParams(vmem_limit_bytes=62 * 2**20),
    )(qkv, qkv, qkv, fo, fk, do, o, cos, sin, *extra)


def attention_tables(segment, position, valid_slot):
    inverse = jnp.exp(jnp.arange(32, dtype=F32) * (-math.log(10000.0) / 32))
    angles = position.astype(F32)[:, None] * inverse[None, :]
    c, s = jnp.cos(angles), jnp.sin(angles)
    cos = jnp.concatenate([c, c, c, c], axis=1)
    sin = jnp.concatenate([-s, s, -s, s], axis=1)
    spot = jnp.arange(PAIR) % 64
    same = segment[:, None] == spot[None, :]
    fq = same.astype(BF)
    fk = jnp.where((spot < 8)[None, :], jnp.where(same & valid_slot[:, None], 0.0, -1e30),
                   jnp.where((spot < 11)[None, :], 1.0, 0.0)).astype(BF)
    return cos, sin, fq, fk


UNITS = 16
QKV_HALF = 3 * D // 2
SMALL_WIDE = 6 * COND + 128
FIRST_WIDE = QKV_HALF + 3 * COND + 128
UP_AT, DOWN_AT, OUT_AT, SECOND_WIDE = 0, FF // 2, FF // 2 + 2 * D, FF // 2 + 2 * D + D // 2
VECTOR_PART = (9 * D + FF) // UNITS
FLAT_ROWS = 80
HBM = pltpu.HBM
SMALL_VMEM = pl.BlockSpec(memory_space=pltpu.SMEM)


def whole(shape):
    return pl.BlockSpec(shape, lambda *_: (0,) * len(shape), pipeline_mode=pl.Buffered(1))


def line(flat_ref, start, count):
    return jnp.concatenate([flat_ref[start + i : start + i + 1, :] for i in range(count)], axis=1)


def unit_of(units, half, place):
    if len(units) == 10:
        kind, back = place // 4, place % 4
        return units[half * 5 + (kind if kind < 3 else 3 + back // 2)].at[back if kind < 3 else back % 2]
    return units[half * 8 + place // 4 * 2 + min(place % 4, 1)].at[max(place % 4 - 1, 0)]


def unit_copies(units, order, core, sems, plan, first_sem):
    copies = []
    for half in range(2):
        side = core if half == 0 else 1 - core
        for place in range(UNITS):
            origin = order[half * UNITS + place]
            for target, rows, column, width, by_origin, by_side, row, column_side, both in plan:
                if half == 1 and not both:
                    continue
                to_row = pl.multiple_of(origin * by_origin + side * by_side + row, 16)
                to_column = pl.multiple_of(side * column_side, 128) if column_side else 0
                copies.append(
                    pltpu.make_async_copy(
                        unit_of(units, half, place).at[pl.ds(0, rows), pl.ds(column, width)],
                        target.at[pl.ds(to_row, rows), pl.ds(to_column, width)],
                        sems.at[first_sem + len(copies)],
                    )
                )
    return copies


def layer_norm(values):
    average = jnp.mean(values, axis=-1, keepdims=True)
    centered = values - average
    root = lax.rsqrt(jnp.mean(centered * centered, axis=-1, keepdims=True) + 1e-05)
    return (centered * root, root)


def layer_norm_back(grad, normal, root, gain):
    scaled = grad * gain
    inner = jnp.mean(scaled * normal, axis=-1, keepdims=True)
    return root * (scaled - jnp.mean(scaled, axis=-1, keepdims=True) - normal * inner)


def first_kernel(rows, order_ref, core_ref, tiles_ref, *refs):
    units = refs[:10]
    x_ref, cond_ref, cos_ref, sin_ref, qkv_ref, first_ref, w_ref, mod_ref, flat_ref, modt, vecs, sems = refs[10:]
    step = pl.program_id(0)

    @pl.when(step == 0)
    def _():
        core = core_ref[0]
        small = unit_copies(units, order_ref, core, sems, (
            (vecs, 16, QKV_HALF + 3 * COND, 128, 16, 0, 0, 0, False),
            (modt, 48, QKV_HALF, 128, 288, 144, 0, 0, True),
            (modt, 48, QKV_HALF + 128, 128, 288, 144, 48, 0, True),
            (modt, 48, QKV_HALF + 256, 128, 288, 144, 96, 0, True),
        ), 0)
        large = unit_copies(units, order_ref, core, sems, (
            (w_ref, 48, 0, QKV_HALF, 48, 0, 0, QKV_HALF, True),
        ), len(small))
        for copy in small + large:
            copy.start()
        for copy in small:
            copy.wait()
        flat_ref[...] = jnp.zeros_like(flat_ref)
        lane = lax.broadcasted_iota(jnp.int32, (8, 128), 1)
        for part in range(UNITS):
            row, turn = divmod(VECTOR_PART * part, 128)
            piece = vecs[16 * part : 16 * part + 16, :].astype(F32)[:8]
            if turn:
                piece = pltpu.roll(piece, turn, 1)
                flat_ref[row + 1 : row + 6, :] += jnp.where(lane < turn, piece, 0.0)[:5]
                piece = jnp.where(lane >= turn, piece, 0.0)
            flat_ref[row : row + 5, :] += piece[:5]
        mod_ref[...] = mm(cond_ref[...], modt[...], NT) + line(flat_ref, (3 * D + FF) // 128, 6 * D // 128)
        for copy in large:
            copy.wait()

    gain = line(flat_ref, 0, D // 128)
    for part in range(rows // TILE):
        at = pl.ds(part * TILE, TILE)
        segment = tiles_ref[step * (rows // TILE) + part]
        normal, _ = layer_norm(x_ref[at, :].astype(F32))
        shift = mod_ref[pl.ds(segment, 1), 0:D]
        scale = mod_ref[pl.ds(segment, 1), D : 2 * D]
        first_ref[at, :] = (normal * (gain * (1.0 + scale)) + shift).astype(BF)
    first = first_ref[...]
    cos, sin = cos_ref[...], sin_ref[...]
    for kind in range(3):
        mixed = mm(first, w_ref[:, kind * D : (kind + 1) * D])
        if kind < 2:
            for pair in range(D // PAIR):
                part = mixed[:, pair * PAIR : (pair + 1) * PAIR]
                turned = part * cos + swap_halves(part) * sin
                if kind == 0:
                    turned = turned * HDIM ** (-0.5)
                qkv_ref[:, kind * D + pair * PAIR : kind * D + (pair + 1) * PAIR] = turned.astype(BF)
        else:
            qkv_ref[:, 2 * D :] = mixed.astype(BF)


def first_part(units, order, core, tiles, x, cond, cos, sin, rows=256):
    count = UNITS * (1 + 2 * 3 + 2)
    row = lambda width: pl.BlockSpec((rows, width), lambda i: (i, 0))
    shape = lambda s, t: jax.ShapeDtypeStruct(s, t)
    return pl.pallas_call(
        functools.partial(first_kernel, rows),
        grid=(SLOTS // rows,),
        in_specs=[SMALL_VMEM] * 3 + [pl.BlockSpec(memory_space=HBM)] * 10
        + [row(D), whole((NSEG, COND)), row(PAIR), row(PAIR)],
        out_specs=[row(3 * D), row(D), whole((D, 3 * D)), whole((NSEG, 6 * D)), whole((FLAT_ROWS, 128))],
        out_shape=[shape((SLOTS, 3 * D), BF), shape((SLOTS, D), BF), shape((D, 3 * D), BF),
                   shape((NSEG, 6 * D), F32), shape((FLAT_ROWS, 128), F32)],
        scratch_shapes=[pltpu.VMEM((6 * D, COND), BF), pltpu.VMEM((16 * UNITS, 128), BF), pltpu.SemaphoreType.DMA((count,))],
        cost_estimate=pl.CostEstimate(flops=2 * SLOTS * D * 3 * D, bytes_accessed=20 * 2**20, transcendentals=SLOTS),
        compiler_params=pltpu.CompilerParams(vmem_limit_bytes=56 * 2**20),
    )(order, core, tiles, *units, x, cond, cos, sin)


def middle_kernel(rows, order_ref, core_ref, tiles_ref, *refs):
    units = refs[:16]
    (att_all, x_ref, cot_ref, mask_ref, mod_ref, flat_ref,
     out_ref, gmid_ref, gatt_ref, sums_ref, bias_ref, mine_ref, give_ref,
     wo, wu, wd, hidden_s, second_s, grad_mlp_s, grad_up_s, grad_branch_s, branch_s, buffer, sems, out_sems) = refs[16:]
    step = pl.program_id(0)
    core = core_ref[0]

    @pl.when(step < SLOTS // rows)
    def _():
        middle_rows(
            rows, step, core, order_ref, tiles_ref, units, att_all, x_ref, cot_ref, mask_ref, mod_ref, flat_ref,
            out_ref, gmid_ref, gatt_ref, sums_ref, bias_ref,
            wo, wu, wd, hidden_s, second_s, grad_mlp_s, grad_up_s, grad_branch_s, branch_s, sems,
        )

    @pl.when(step >= SLOTS // rows)
    def _():
        later_grads(
            step - SLOTS // rows, core, hidden_s, second_s, att_all, grad_mlp_s, grad_up_s, grad_branch_s,
            mine_ref, give_ref, buffer, out_sems,
        )


def middle_rows(
    rows, step, core, order_ref, tiles_ref, units, att_all, x_ref, cot_ref, mask_ref, mod_ref, flat_ref,
    out_ref, gmid_ref, gatt_ref, sums_ref, bias_ref,
    wo, wu, wd, hidden_s, second_s, grad_mlp_s, grad_up_s, grad_branch_s, branch_s, sems,
):
    chunks = FF // D
    here = pl.ds(pl.multiple_of(step * rows, rows), rows)

    def part_of(part):
        return pl.ds(pl.multiple_of(step * rows + part * TILE, TILE), TILE)

    tiles = rows // TILE
    each = 2 * UNITS
    copies = [
        unit_copies(units, order_ref, core, sems, ((wo, 48, OUT_AT, D // 2, 48, 0, 0, D // 2, True),), 0),
        unit_copies(units, order_ref, core, sems, ((wu, 48, UP_AT, FF // 2, 48, 0, 0, FF // 2, True),), each),
        unit_copies(units, order_ref, core, sems, (
            (wd, 48, DOWN_AT, D, 192, 96, 0, 0, True),
            (wd, 48, DOWN_AT + D, D, 192, 96, 48, 0, True),
        ), 2 * each),
    ]

    @pl.when(step == 0)
    def _():
        for group in copies:
            for copy in group:
                copy.start()
        bias_ref[...] = jnp.zeros_like(bias_ref)
        for copy in copies[0]:
            copy.wait()

    def table(part, kind):
        return mod_ref[pl.ds(tiles_ref[step * tiles + part], 1), kind * D : (kind + 1) * D]

    def mask_column(part):
        row = mask_ref[pl.ds(step * tiles + part, 1), :]
        return jnp.broadcast_to(row, (TILE, TILE)).T[:, :1]

    branch_s[...] = mm(att_all[here, :], wo[...])
    gain = line(flat_ref, D // 128, D // 128)
    for part in range(tiles):
        at = pl.ds(part * TILE, TILE)
        middle = x_ref[at, :].astype(F32) + table(part, 2) * branch_s[at, :]
        gmid_ref[at, :] = middle
        normal, _ = layer_norm(middle)
        second_s[part_of(part), :] = (normal * (gain * (1.0 + table(part, 4))) + table(part, 3)).astype(BF)

    @pl.when(step == 0)
    def _():
        for group in copies[1:]:
            for copy in group:
                copy.wait()

    for part in range(tiles):
        at = pl.ds(part * TILE, TILE)
        grad_mlp = (cot_ref[at, :].astype(F32) * mask_column(part) * table(part, 5)).astype(BF)
        grad_mlp_s[part_of(part), :] = grad_mlp
        bias_ref[0:1, FF:] += jnp.sum(grad_mlp.astype(F32), axis=0, keepdims=True)
    second = second_s[here, :]
    grad_mlp = grad_mlp_s[here, :]
    factor = math.sqrt(2.0 / math.pi)
    feed, grad_second = None, None
    for j in range(chunks):
        at = pl.ds(j * D, D)
        u = mm(second, wu[:, at]) + line(flat_ref, 2 * D // 128 + j * (D // 128), D // 128)
        grad_hidden = mm(grad_mlp, wd[at, :], NT)
        square = u * u
        bent = jnp.tanh(u * (factor + (factor * 0.044715) * square))
        half = 0.5 * u
        bow = half * bent
        hidden = (half + bow).astype(BF)
        slope = (0.5 + 0.5 * bent) + (half - bow * bent) * (factor + (3 * factor * 0.044715) * square)
        grad_up = (grad_hidden * slope).astype(BF)
        hidden_s[here, at] = hidden
        grad_up_s[here, at] = grad_up
        bias_ref[0:1, at] += jnp.sum(grad_up.astype(F32), axis=0, keepdims=True)
        share, grad_share = mm(hidden, wd[at, :]), mm(grad_up, wu[:, at], NT)
        feed = share if feed is None else feed + share
        grad_second = grad_share if grad_second is None else grad_second + grad_share
    bias_down = line(flat_ref, (2 * D + FF) // 128, D // 128)
    for part in range(tiles):
        at = pl.ds(part * TILE, TILE)
        feed_out = feed[part * TILE : (part + 1) * TILE] + bias_down
        out_ref[at, :] = (gmid_ref[at, :] + table(part, 5) * feed_out).astype(BF)
        grad_out = cot_ref[at, :].astype(F32) * mask_column(part)
        sums_ref[part, 3:4, :] = jnp.sum(grad_out * feed_out, axis=0, keepdims=True)
    for part in range(tiles):
        at = pl.ds(part * TILE, TILE)
        normal, root = layer_norm(gmid_ref[at, :])
        grad = grad_second[part * TILE : (part + 1) * TILE]
        sums_ref[part, 1:2, :] = jnp.sum(grad, axis=0, keepdims=True)
        sums_ref[part, 2:3, :] = jnp.sum(grad * normal, axis=0, keepdims=True)
        grad_middle = cot_ref[at, :].astype(F32) * mask_column(part) + layer_norm_back(
            grad, normal, root, gain * (1.0 + table(part, 4))
        )
        gmid_ref[at, :] = grad_middle
        sums_ref[part, 0:1, :] = jnp.sum(grad_middle * branch_s[at, :], axis=0, keepdims=True)
        grad_branch_s[part_of(part), :] = (grad_middle * table(part, 2)).astype(BF)
    gatt_ref[...] = mm(grad_branch_s[here, :], wo[...], NT).astype(BF)


def later_grads(step, core, hidden_s, second_s, att_all, grad_mlp_s, grad_up_s, grad_branch_s, mine_ref, give_ref, buffer, sems):
    down_steps = FF // D
    steps = 2 * down_steps + 1
    slot = step % 2

    def wait(at_slot):
        for number in range(16):
            pltpu.make_async_copy(buffer.at[at_slot, number], buffer.at[at_slot, number], sems.at[at_slot, number]).wait()

    def send(source, side, place, number):
        for ref, wanted in ((mine_ref, 0), (give_ref, 1)):
            @pl.when((core ^ side) == wanted)
            def _():
                pltpu.make_async_copy(source, ref.at[place], sems.at[slot, number]).start()

    def keep(left, right):
        buffer[slot] = mm(left, right, TN).astype(BF).reshape(16, 48, D)

    @pl.when(step >= 2)
    def _():
        wait(slot)

    @pl.when(step < down_steps)
    def _():
        keep(hidden_s[:, pl.ds(pl.multiple_of(step * D, D), D)], grad_mlp_s[...])
        for number in range(16):
            local, side, block = number // 4, (number // 2) % 2, number % 2
            send(buffer.at[slot, number], side, (4 * step + local, pl.ds(0, 48), pl.ds(DOWN_AT + block * D, D)), number)

    @pl.when((step >= down_steps) & (step < steps - 1))
    def _():
        keep(second_s[...], grad_up_s[:, pl.ds(pl.multiple_of((step - down_steps) * D, D), D)])

    for j in range(down_steps):
        @pl.when(step == down_steps + j)
        def _():
            for number in range(16):
                send(buffer.at[slot, number], j // 2, (number, pl.ds(0, 48), pl.ds(UP_AT + (j % 2) * D, D)), number)

    @pl.when(step == steps - 1)
    def _():
        keep(att_all[...], grad_branch_s[...])
        for number in range(16):
            for side in range(2):
                source = buffer.at[slot, number, pl.ds(0, 48), pl.ds(side * (D // 2), D // 2)]
                send(source, side, (number, pl.ds(0, 48), pl.ds(OUT_AT, D // 2)), number)
        wait(1 - slot)
        wait(slot)


def middle_part(units, order, core, tiles, att, x, cot, mask, modulation, flat, rows=512):
    last = SLOTS // rows - 1
    row = lambda width: pl.BlockSpec((rows, width), lambda i: (jnp.minimum(i, last), 0))
    shape = lambda s, t: jax.ShapeDtypeStruct(s, t)
    units_shape = shape((UNITS, 48, SECOND_WIDE), BF)
    kept = lambda width: pltpu.VMEM((SLOTS, width), BF)
    return pl.pallas_call(
        functools.partial(middle_kernel, rows),
        grid=(SLOTS // rows + 2 * (FF // D) + 1,),
        in_specs=[SMALL_VMEM] * 3 + [pl.BlockSpec(memory_space=HBM)] * 16
        + [whole((SLOTS, D)), row(D), row(D), whole((BLOCKS, TILE)), whole((NSEG, 6 * D)), whole((FLAT_ROWS, 128))],
        out_specs=[row(D), row(D), row(D),
                   pl.BlockSpec((rows // TILE, 8, D), lambda i: (jnp.minimum(i, last), 0, 0)), whole((8, FF + D))]
        + [pl.BlockSpec(memory_space=HBM)] * 2,
        out_shape=[shape((SLOTS, D), BF), shape((SLOTS, D), F32), shape((SLOTS, D), BF), shape((BLOCKS, 8, D), F32),
                   shape((8, FF + D), F32), units_shape, units_shape],
        scratch_shapes=[pltpu.VMEM((D, D), BF), pltpu.VMEM((D, FF), BF), pltpu.VMEM((FF, D), BF),
                        kept(FF), kept(D), kept(D), kept(FF), kept(D),
                        pltpu.VMEM((rows, D), F32), pltpu.VMEM((2, 16, 48, D), BF),
                        pltpu.SemaphoreType.DMA((8 * UNITS,)), pltpu.SemaphoreType.DMA((2, 16))],
        cost_estimate=pl.CostEstimate(flops=6 * SLOTS * D * (D + 2 * FF), bytes_accessed=50 * 2**20, transcendentals=SLOTS * FF),
        compiler_params=pltpu.CompilerParams(vmem_limit_bytes=63 * 2**20),
    )(order, core, tiles, *units, att, x, cot, mask, modulation, flat)


def qkv_grads_kernel(core_ref, first_ref, g_ref, mine_ref, give_ref, units, sems):
    step = pl.program_id(0)
    core = core_ref[0]
    product = mm(first_ref[...], g_ref[0], TN).astype(BF).reshape(UNITS, 48, D)

    @pl.when(step == 0)
    def _():
        units[0, :, :, 0:D] = product

    @pl.when(step == 1)
    def _():
        units[0, :, :, D:] = product[:, :, : D // 2]
        units[1, :, :, 0 : D // 2] = product[:, :, D // 2 :]

    @pl.when(step == 2)
    def _():
        units[1, :, :, D // 2 :] = product
        copies = [
            pltpu.make_async_copy(units.at[core], mine_ref, sems.at[0]),
            pltpu.make_async_copy(units.at[1 - core], give_ref, sems.at[1]),
        ]
        for copy in copies:
            copy.start()
        for copy in copies:
            copy.wait()


def qkv_grads(core, first, g):
    shape = jax.ShapeDtypeStruct((UNITS, 48, QKV_HALF), BF)
    return pl.pallas_call(
        qkv_grads_kernel,
        grid=(3,),
        in_specs=[SMALL_VMEM, whole((SLOTS, D)), pl.BlockSpec((1, SLOTS, D), lambda i: (i, 0, 0))],
        out_specs=[pl.BlockSpec(memory_space=HBM)] * 2,
        out_shape=[shape, shape],
        scratch_shapes=[pltpu.VMEM((2, UNITS, 48, QKV_HALF), BF), pltpu.SemaphoreType.DMA((2,))],
        cost_estimate=pl.CostEstimate(flops=SLOTS * D * D, bytes_accessed=2**20, transcendentals=0),
        compiler_params=pltpu.CompilerParams(vmem_limit_bytes=48 * 2**20),
    )(core, first, g)


def last_kernel(rows, places_ref, tiles_ref, member_ref, g_ref, w_ref, x_ref, gmid_ref, mod_ref, flat_ref, cond_ref,
                sums_in, bias_in, gin_ref, own_ref, first_ref, second_ref, far_ref, sums, units, sems):
    step = pl.program_id(0)
    tiles = rows // TILE
    steps = SLOTS // rows
    gain = line(flat_ref, 0, D // 128)

    grad = None
    for kind in range(3):
        share = mm(g_ref[kind], w_ref[:, kind * D : (kind + 1) * D], NT)
        grad = share if grad is None else grad + share
    for part in range(tiles):
        at = pl.ds(part * TILE, TILE)
        tile = step * tiles + part
        segment = tiles_ref[tile]
        normal, root = layer_norm(x_ref[at, :].astype(F32))
        piece = grad[part * TILE : (part + 1) * TILE]
        scale = mod_ref[pl.ds(segment, 1), D : 2 * D]
        sums[pl.ds(tile, 1), 0:D] = jnp.sum(piece, axis=0, keepdims=True)
        sums[pl.ds(tile, 1), D : 2 * D] = jnp.sum(piece * normal, axis=0, keepdims=True)
        gin_ref[at, :] = gmid_ref[at, :] + layer_norm_back(piece, normal, root, gain * (1.0 + scale))

    @pl.when(step == steps - 1)
    def _():
        gain_two = line(flat_ref, D // 128, D // 128)
        for tile in range(BLOCKS):
            at = pl.ds(tile, 1)
            sums[at, 2 * D : 3 * D] = sums_in[tile, 0:1, :]
            sums[at, 3 * D : 4 * D] = sums_in[tile, 1:2, :]
            sums[at, 4 * D : 5 * D] = sums_in[tile, 2:3, :]
            sums[at, 5 * D : 6 * D] = sums_in[tile, 3:4, :]
        member = member_ref[...]
        scale_one = lax.dot_general(member, mod_ref[:, D : 2 * D], NN, precision=lax.Precision.HIGHEST, preferred_element_type=F32)
        scale_two = lax.dot_general(member, mod_ref[:, 4 * D : 5 * D], NN, precision=lax.Precision.HIGHEST, preferred_element_type=F32)
        grad_gain_one = jnp.sum(sums[:, D : 2 * D] * (1.0 + scale_one), axis=0, keepdims=True)
        grad_gain_two = jnp.sum(sums[:, 4 * D : 5 * D] * (1.0 + scale_two), axis=0, keepdims=True)
        sums[:, D : 2 * D] = sums[:, D : 2 * D] * gain
        sums[:, 4 * D : 5 * D] = sums[:, 4 * D : 5 * D] * gain_two
        by_segment = lax.dot_general(member, sums[...], TN, precision=lax.Precision.HIGHEST, preferred_element_type=F32)
        grad_mod = lax.dot_general(
            by_segment, cond_ref[...].astype(F32), TN, precision=lax.Precision.HIGHEST, preferred_element_type=F32
        ).astype(BF).reshape(4, 4, 6, 48, COND)
        for block in range(6):
            units[:, :, :, block * COND : (block + 1) * COND] = grad_mod[:, :, block]
        row = jnp.concatenate(
            [grad_gain_one, grad_gain_two, bias_in[0:1, :], jnp.sum(by_segment, axis=0, keepdims=True)], axis=1
        )
        lane = lax.broadcasted_iota(jnp.int32, (1, 128), 1)
        blank = jnp.zeros((43, 128), F32)
        for part in range(UNITS):
            start = VECTOR_PART * part
            pieces = []
            for number in range(5):
                first_row, turn = divmod(start + 128 * number, 128)
                piece = row[:, first_row * 128 : (first_row + 1) * 128]
                if turn:
                    following = (
                        row[:, (first_row + 1) * 128 : (first_row + 2) * 128]
                        if (first_row + 2) * 128 <= row.shape[1]
                        else jnp.zeros((1, 128), F32)
                    )
                    piece = jnp.where(
                        lane < 128 - turn, pltpu.roll(piece, 128 - turn, 1), pltpu.roll(following, 128 - turn, 1)
                    )
                if number == 4:
                    piece = jnp.where(lane < VECTOR_PART - 512, piece, 0.0)
                pieces.append(piece)
            stack = jnp.concatenate(pieces + [blank], axis=0).astype(BF)
            units[part // 4, part % 4, :, 6 * COND :] = stack
        copies = [
            pltpu.make_async_copy(units.at[:, places_ref[kind]], ref, sems.at[kind])
            for kind, ref in enumerate((own_ref, first_ref, second_ref, far_ref))
        ]
        for copy in copies:
            copy.start()
        for copy in copies:
            copy.wait()


def last_part(places, tiles, member, g, w, x, gmid, modulation, flat, cond, sums, bias, rows=256):
    row = lambda width: pl.BlockSpec((rows, width), lambda i: (i, 0))
    shape = jax.ShapeDtypeStruct((4, 48, SMALL_WIDE), BF)
    return pl.pallas_call(
        functools.partial(last_kernel, rows),
        grid=(SLOTS // rows,),
        in_specs=[SMALL_VMEM, SMALL_VMEM, whole((BLOCKS, NSEG)), pl.BlockSpec((3, rows, D), lambda i: (0, i, 0)), whole((D, 3 * D)),
                  row(D), row(D), whole((NSEG, 6 * D)), whole((FLAT_ROWS, 128)), whole((NSEG, COND)),
                  whole((BLOCKS, 8, D)), whole((8, FF + D))],
        out_specs=[row(D)] + [pl.BlockSpec(memory_space=HBM)] * 4,
        out_shape=[jax.ShapeDtypeStruct((SLOTS, D), F32)] + [shape] * 4,
        scratch_shapes=[pltpu.VMEM((BLOCKS, 6 * D), F32), pltpu.VMEM((4, 4, 48, SMALL_WIDE), BF),
                        pltpu.SemaphoreType.DMA((4,))],
        cost_estimate=pl.CostEstimate(flops=2 * SLOTS * D * 3 * D, bytes_accessed=30 * 2**20, transcendentals=SLOTS),
        compiler_params=pltpu.CompilerParams(vmem_limit_bytes=60 * 2**20),
    )(places, tiles, member, g, w, x, gmid, modulation, flat, cond, sums, bias)


def moments(weight_ref, first_ref, second_ref, gradient, first_out, second_out, direction_out, decay_rate=DECAY_RATE):
    weight = weight_ref[...]
    first_new = BETA_ONE * first_ref[...] + (1.0 - BETA_ONE) * gradient
    second_new = BETA_TWO * second_ref[...] + (1.0 - BETA_TWO) * gradient * gradient
    direction = (
        first_new
        / (1.0 - BETA_ONE**STEP)
        / (jnp.sqrt(second_new / (1.0 - BETA_TWO**STEP)) + EPSILON)
        + decay_rate * weight
    )
    first_out[...] = first_new
    second_out[...] = second_new
    direction_out[...] = direction
    return [jnp.sum(values * values, axis=(0, 1), keepdims=True) for values in (weight, direction)]


def squares_table(pairs):
    row = lax.broadcasted_iota(jnp.int32, (8, 128), 0)
    lane = lax.broadcasted_iota(jnp.int32, (8, 128), 1)
    table = jnp.zeros((8, 128), F32)
    for number, sums in pairs:
        for kind in range(2):
            table = jnp.where((row == kind) & (lane == number), sums[kind], table)
    return table


def update_later_kernel(side_ref, own_ref, other_ref, *refs):
    outs, table_ref = refs[9:18], refs[18]
    zero = side_ref[0] == 0
    own, other = own_ref[...].astype(F32), other_ref[...].astype(F32)
    halves = (jnp.where(zero, own, other), jnp.where(zero, other, own))
    out_grad = jnp.concatenate([half[:, OUT_AT:] for half in halves], axis=1)
    up_grad = jnp.concatenate([half[:, UP_AT : UP_AT + FF // 2] for half in halves], axis=1)
    down_grad = jnp.concatenate(
        [half[:, DOWN_AT + D * part : DOWN_AT + D * (part + 1)] for half in halves for part in range(2)], axis=0
    )
    table_ref[...] = squares_table(
        [
            (1 + place, moments(*refs[3 * place : 3 * place + 3], gradient, *outs[3 * place : 3 * place + 3]))
            for place, gradient in enumerate((out_grad, up_grad, down_grad))
        ]
    )


def update_sooner_kernel(side_ref, own_ref, other_ref, small_ref, *refs):
    outs, table_ref = refs[6:12], refs[12]
    zero = side_ref[0] == 0
    own, other = own_ref[...].astype(F32), other_ref[...].astype(F32)
    qkv_grad = jnp.concatenate([jnp.where(zero, own, other), jnp.where(zero, other, own)], axis=1)
    mod_grad = jnp.concatenate([small_ref[:, COND * part : COND * (part + 1)] for part in range(6)], axis=0)
    table_ref[...] = squares_table(
        [
            (4 * place, moments(*refs[3 * place : 3 * place + 3], gradient, *outs[3 * place : 3 * place + 3]))
            for place, gradient in enumerate((qkv_grad, mod_grad))
        ]
    )


def update_moments(kernel, side, parts, arrays):
    block = pl.BlockSpec(memory_space=pltpu.VMEM)
    shapes = [jax.ShapeDtypeStruct(arrays[3 * (i // 3)].shape, F32) for i in range(len(arrays))]
    *outs, table = pl.pallas_call(
        kernel,
        in_specs=[SMALL_VMEM] + [block] * (len(parts) + len(arrays)),
        out_specs=[block] * (len(arrays) + 1),
        out_shape=shapes + [jax.ShapeDtypeStruct((8, 128), F32)],
        compiler_params=pltpu.CompilerParams(vmem_limit_bytes=48 * 2**20),
    )(side, *parts, *arrays)
    return [outs[i : i + 3] for i in range(0, len(outs), 3)], table


def renew_kernel(table_ref, *refs):
    norms_ref = refs[15]
    roots = jnp.sqrt(table_ref[...])
    norms_ref[...] = roots[:2, :5]
    for number in range(5):
        trust = roots[0:1, number : number + 1] / (roots[1:2, number : number + 1] + EPSILON)
        refs[10 + number][...] = refs[number][...] - (MATRIX_RATE * trust) * refs[5 + number][...]


def renew(table, matrices, turns):
    block = pl.BlockSpec(memory_space=pltpu.VMEM)
    return pl.pallas_call(
        renew_kernel,
        in_specs=[block] * 11,
        out_specs=[block] * 6,
        out_shape=[jax.ShapeDtypeStruct(matrix.shape, F32) for matrix in matrices] + [jax.ShapeDtypeStruct((2, 5), F32)],
        compiler_params=pltpu.CompilerParams(vmem_limit_bytes=48 * 2**20),
    )(table, *matrices, *turns)


ALONG = ((1, 2), (2, 1))


def column_of(core, chip, kind):
    first, second = ALONG[core]
    return (chip % 4) ^ (0, first, second, first ^ second)[kind]


ORIGIN = np.array(
    [
        [[column_of(core, chip, kind) + 4 * ((chip // 4 - back) % 4) for kind in range(4) for back in range(4)]
         for chip in range(UNITS)]
        for core in range(2)
    ],
    np.int32,
)
PLACES = np.array(
    [
        [[column_of(core, chip, kind) for kind in range(4)] + [(chip // 4 + ahead) % 4 for ahead in range(4)]
         for chip in range(UNITS)]
        for core in range(2)
    ],
    np.int32,
)


def along_z(values, ahead):
    return lax.ppermute(values, "fsdp", [(chip, chip % 4 + 4 * ((chip // 4 + ahead) % 4)) for chip in range(UNITS)])


def along_plane(values, direction):
    moves = [
        (core * UNITS + chip, core * UNITS + (chip ^ ALONG[core][direction]))
        for core in range(2)
        for chip in range(UNITS)
    ]
    return lax.ppermute(values, ("rep", "fsdp"), moves)


def swap_core(values):
    return lax.ppermute(values, "rep", [(0, 1), (1, 0)])


def hold_back(later, sooner):
    return lax.optimization_barrier((later, sooner))[0]


def by_rounds():
    return lax.axis_size("fsdp") == UNITS


def far_from(near):
    return along_plane(near[0], 1)


def near_of(piece):
    return [along_plane(piece, 0), along_plane(piece, 1)]


def swapped(values):
    return [swap_core(one) for one in values]


def column_sums_kernel(counts, places_ref, *refs):
    outs = refs[len(refs) - len(counts) :]
    at = 0
    for out_ref, count in zip(outs, counts):
        total = refs[at][...].astype(F32) + refs[at + 1][...].astype(F32)
        for arrived in refs[at + 2 : at + 2 + count]:
            total = total + arrived[...].astype(F32).reshape(total.shape)
        out_ref[...] = total.astype(BF).reshape(out_ref.shape)
        at += 2 + count


def column_sums(places, mine, given, parts, apart=False):
    block = mine.shape[1:]
    pair = [values.reshape((4, 4) + block) for values in (mine, given)]
    specs, operands, counts = [], [], []
    for ahead in range(4) if apart else (None,):
        for kind, arrived in parts:
            if apart:
                pick = pl.BlockSpec((1, 1) + block, lambda i, s, kind=kind, ahead=ahead: (s[4 + ahead], s[kind], 0, 0))
                came = pl.BlockSpec((1,) + block, lambda i, s, ahead=ahead: (s[4 + ahead], 0, 0))
            else:
                pick = pl.BlockSpec((1, 1) + block, lambda i, s, kind=kind: (i, s[kind], 0, 0))
                came = pl.BlockSpec((1,) + block, lambda i, s: (i, 0, 0))
            specs += [pick, pick] + [came] * len(arrived)
            operands += pair + arrived
            counts.append(len(arrived))
    if apart:
        out_spec, out_shape = pl.BlockSpec(block, lambda i, s: (0, 0)), jax.ShapeDtypeStruct(block, BF)
    else:
        out_spec, out_shape = pl.BlockSpec((1,) + block, lambda i, s: (i, 0, 0)), jax.ShapeDtypeStruct((4,) + block, BF)
    return pl.pallas_call(
        functools.partial(column_sums_kernel, counts),
        grid_spec=pltpu.PrefetchScalarGridSpec(
            num_scalar_prefetch=1,
            grid=(1 if apart else 4,),
            in_specs=specs,
            out_specs=[out_spec] * len(counts),
        ),
        out_shape=[out_shape] * len(counts),
        cost_estimate=pl.CostEstimate(flops=0, bytes_accessed=(200 if apart else 12) * 2**20, transcendentals=0),
        compiler_params=pltpu.CompilerParams(vmem_limit_bytes=48 * 2**20),
    )(places, *operands)


class Scatter:
    def __init__(self, mine, give, places):
        self.mine, self.places = mine, places
        self.given = swap_core(give)

    def send_far(self, sooner=None):
        given = self.given if sooner is None else hold_back(self.given, sooner)
        far, second = column_sums(self.places, self.mine, given, [(3, []), (2, [])])
        self.far_came, self.second_came = along_plane(far, 1), along_plane(second, 1)
        return far

    def send_first(self, sooner=None):
        self.far_came, self.second_came = (
            (self.far_came, self.second_came) if sooner is None else hold_back((self.far_came, self.second_came), sooner)
        )
        (first,) = column_sums(self.places, self.mine, self.given, [(1, [self.far_came])])
        self.arrived = [along_plane(first, 0), self.second_came]
        return first

    def send_column(self, sooner=None):
        arrived = self.arrived if sooner is None else hold_back(self.arrived, sooner)
        units = column_sums(self.places, self.mine, self.given, [(0, arrived)], apart=True)
        self.own = units[0]
        self.came = [along_z(units[ahead], ahead) for ahead in range(1, 4)]
        return self.own

    def finish(self, sooner=None):
        came = self.came if sooner is None else hold_back(self.came, sooner)
        total = self.own.astype(F32)
        for part in came:
            total = total + part.astype(F32)
        own = total.astype(BF)
        return (own, swap_core(own))


def arrivals_kernel(outputs, *refs):
    inputs, outs = refs[1 : len(refs) - outputs], refs[len(refs) - outputs :]
    each = len(inputs) // outputs
    for number, out_ref in enumerate(outs):
        total = inputs[number * each][...].astype(F32)
        for part in inputs[number * each + 1 : (number + 1) * each]:
            total = total + part[...].astype(F32)
        out_ref[...] = total.reshape(out_ref.shape).astype(BF)


def arrival_sums(places, parts, apart):
    block = parts[0].shape[1:]
    if apart:
        specs = [
            pl.BlockSpec((1,) + block, lambda i, s, ahead=ahead: (s[4 + ahead], 0, 0)) for ahead in range(4) for _ in parts
        ]
        out_spec, out_shape, outputs = pl.BlockSpec(block, lambda i, s: (0, 0)), block, 4
    else:
        out_spec = pl.BlockSpec((4,) + block, lambda i, s: (0, 0, 0))
        specs, out_shape, outputs = [out_spec] * len(parts), (4,) + block, 1
    return pl.pallas_call(
        functools.partial(arrivals_kernel, outputs),
        grid_spec=pltpu.PrefetchScalarGridSpec(
            num_scalar_prefetch=1, grid=(1,), in_specs=specs, out_specs=[out_spec] * outputs
        ),
        out_shape=[jax.ShapeDtypeStruct(out_shape, BF)] * outputs,
    )(places, *(list(parts) * outputs))


class SmallScatter:
    def __init__(self, own, first, second, far, places):
        self.places, self.own, self.first = places, own, first
        self.far_came, self.second_came = along_plane(far, 1), along_plane(second, 1)

    def send_first(self, sooner):
        far_came, self.second_came = hold_back((self.far_came, self.second_came), sooner)
        (first,) = arrival_sums(self.places, [self.first, far_came], False)
        self.first_came = along_plane(first, 0)
        return first

    def send_column(self, sooner):
        came = hold_back(self.first_came, sooner)
        self.own, *units = arrival_sums(self.places, [self.own, came, self.second_came], True)
        self.came = [along_z(unit, ahead + 1) for ahead, unit in enumerate(units)]
        return self.own

    def finish(self):
        total = self.own.astype(F32)
        for part in self.came:
            total = total + part.astype(F32)
        own = total.astype(BF)
        return own.astype(F32) + swap_core(own).astype(F32)


def sum_small(values):
    for turn in (1, 2, 4, 8):
        values = values + lax.ppermute(values, "fsdp", [(chip, chip ^ turn) for chip in range(UNITS)])
    return values


def side_columns(matrix, core, width):
    return lax.dynamic_slice_in_dim(matrix, core * width, width, axis=1)


def side_rows(blocks, core):
    return lax.dynamic_index_in_dim(blocks, core, 1, keepdims=False)


def pack_first(qkv, mod_turned, vectors, core):
    count = vectors.shape[0]
    mod_blocks = side_rows(mod_turned.reshape(count, 2, 3, 48, COND), core)
    padded = jnp.pad(vectors, ((0, 0), (0, 640 - VECTOR_PART))).reshape(count, 5, 128)
    return jnp.concatenate(
        [
            side_columns(qkv, core, QKV_HALF).reshape(count, 48, QKV_HALF),
            mod_blocks.transpose(0, 2, 1, 3).reshape(count, 48, 3 * COND),
            jnp.pad(padded, ((0, 0), (0, 43), (0, 0))),
        ],
        axis=2,
    )


def pack_second(out, up, down, core):
    count = out.shape[0] // 48
    down_blocks = side_rows(down.reshape(count, 2, 2, 48, D), core)
    return jnp.concatenate(
        [
            side_columns(up, core, FF // 2).reshape(count, 48, FF // 2),
            down_blocks.transpose(0, 2, 1, 3).reshape(count, 48, 2 * D),
            side_columns(out, core, D // 2).reshape(count, 48, D // 2),
        ],
        axis=2,
    )


def unpack_qkv(sides):
    return jnp.concatenate([side for side in sides], axis=2).reshape(-1, 3 * D)


def unpack_small(own, first, second, far):
    units = jnp.stack([own, first, second, far], axis=1).reshape(UNITS, 48, SMALL_WIDE)
    turned = units[:, :, : 6 * COND].reshape(UNITS, 48, 6, COND).transpose(0, 2, 1, 3).reshape(6 * D, COND)
    vectors = units[:, :5, 6 * COND :].reshape(UNITS, 640)[:, :VECTOR_PART]
    return (turned.T, vectors.reshape(-1))


def unpack_second(sides):
    count = sides[0].shape[0]
    up = jnp.concatenate([side[:, :, UP_AT : UP_AT + FF // 2] for side in sides], axis=2).reshape(count * 48, FF)
    out = jnp.concatenate([side[:, :, OUT_AT:] for side in sides], axis=2).reshape(count * 48, D)
    down = jnp.stack([side[:, :, DOWN_AT : DOWN_AT + 2 * D] for side in sides], axis=1)
    down = down.reshape(count, 2, 48, 2, D).transpose(0, 1, 3, 2, 4).reshape(count * 192, D)
    return (out, up, down)


def gather_plain(parts, axes):
    return [lax.all_gather(part, "fsdp", axis=axis, tiled=True) for part, axis in zip(parts, axes)]


def virtual_units(pack, pieces=False):
    cuts = [0, 1, 4, 5, 8, 9, 12, 13, 16] if pieces else [0, 4, 8, 12, 14, 16]
    return [packed[start:stop] for packed in (pack(0), pack(1)) for start, stop in zip(cuts, cuts[1:])]


def reduce_plain(grads, axes):
    parts = [
        lax.psum_scatter(grad.astype(F32), "fsdp", scatter_dimension=axis, tiled=True) for grad, axis in zip(grads, axes)
    ]
    return tuple(lax.psum(part.astype(BF), "rep").astype(F32) for part in parts)


def adam_direction(weight, first_old, second_old, gradient, decay_rate):
    first_new = BETA_ONE * first_old + (1.0 - BETA_ONE) * gradient
    second_new = BETA_TWO * second_old + (1.0 - BETA_TWO) * gradient * gradient
    direction = (
        first_new
        / (1.0 - BETA_ONE**STEP)
        / (jnp.sqrt(second_new / (1.0 - BETA_TWO**STEP)) + EPSILON)
        + decay_rate * weight
    )
    return (first_new, second_new, direction)


def layout_tables(sizes_row, lengths_row):
    slot_ids = jnp.arange(SLOTS, dtype=jnp.int32)
    seg_ends = jnp.cumsum(sizes_row)
    starts = seg_ends - sizes_row
    segment = jnp.sum((slot_ids[:, None] >= seg_ends[None, :]).astype(jnp.int32), axis=1)
    member = segment[:, None] == jnp.arange(NSEG, dtype=jnp.int32)[None, :]
    offset = jnp.sum(jnp.where(member, starts[None, :], 0), axis=1)
    length_of = jnp.sum(jnp.where(member, lengths_row[None, :], 0), axis=1)
    position = slot_ids - offset
    return (segment, member, position, position < length_of)


def condition(steps_row):
    half_cond = COND // 2
    frequency = jnp.exp(jnp.arange(half_cond, dtype=F32) * (-math.log(10000.0) / half_cond))
    angles = steps_row.astype(F32)[:, None] * frequency[None, :]
    return jax.nn.silu(jnp.concatenate([jnp.cos(angles), jnp.sin(angles)], axis=1))


FORWARD_CALLS = (2, 3, 1)
BACKWARD_CALLS = (1, 3, 2)


def on_device(
    inputs, cotangent, seg_sizes, seq_lengths, timesteps, absorbed,
    qkv_weight, out_weight, up_weight, down_weight, mod_weight,
    qkv_first, out_first, up_first, down_first, mod_first,
    qkv_second, out_second, up_second, down_second, mod_second,
    vectors, vectors_first, vectors_second,
):
    rounds = by_rounds()
    chip = lax.axis_index("fsdp")
    core = lax.axis_index("rep")
    matrices = (qkv_weight, out_weight, up_weight, down_weight, mod_weight)
    qkv_low, out_low, up_low, down_low, mod_low = [matrix.astype(BF) for matrix in matrices]
    vector_low = vectors.astype(BF)
    if rounds:
        order = jnp.concatenate([jnp.asarray(ORIGIN)[core, chip], jnp.asarray(ORIGIN)[1 - core, chip]])
        places = jnp.asarray(PLACES)[core, chip]
        side = core[None].astype(jnp.int32)
        unit_first = pack_first(qkv_low, mod_low.T, vector_low[None], core)[0]
        unit_second = pack_second(out_low, up_low, down_low, core)[0]
        second_one = unit_second[None]
        first_back = [along_z(unit_first, back) for back in range(1, 4)]
        second_near = near_of(second_one)
        first_column = jnp.stack([unit_first] + first_back)
        first_near = near_of(first_column)
        second_from = hold_back(unit_second, first_column)
        second_back = [along_z(second_from, back) for back in range(1, 4)]
        first_near, second_near = lax.optimization_barrier((first_near, second_near))
        first_far = [along_plane(first_near[0][start : start + 2], 1) for start in (0, 2)]
        units_first, second_back = lax.optimization_barrier(([first_column] + first_near + first_far, second_back))
        units_first = units_first + swapped(units_first)
    else:
        order = jnp.concatenate([jnp.arange(UNITS, dtype=jnp.int32)] * 2)
        places = jnp.asarray(PLACES)[0, 0]
        side = jnp.zeros((1,), jnp.int32)
        qkv_all, mod_all, vector_all = gather_plain((qkv_low, mod_low, vector_low), (0, 1, 0))
        out_all, up_all, down_all = gather_plain((out_low, up_low, down_low), (0, 0, 0))
        units_first = virtual_units(lambda s: pack_first(qkv_all, mod_all.T, vector_all.reshape(UNITS, -1), s))
        units_second = virtual_units(lambda s: pack_second(out_all, up_all, down_all, s), True)

    segment, member, position, valid_slot = layout_tables(seg_sizes[0], seq_lengths[0])
    tiles = segment.reshape(BLOCKS, TILE)[:, 0]
    member_tile = member.reshape(BLOCKS, TILE, NSEG)[:, 0].astype(F32)
    condition_low = condition(timesteps[0]).astype(BF)
    cos, sin, feature_query, feature_key = attention_tables(segment, position, valid_slot)
    weight_mask = (absorbed[0] * valid_slot.astype(jnp.int32)).astype(F32).reshape(BLOCKS, TILE)
    row_in, row_cot = inputs[0], cotangent[0]

    mixed, first_low, qkv_full, modulation, flat = first_part(
        units_first, order, side, tiles, row_in, condition_low, cos, sin
    )
    forward, first_pair = None, 0
    if rounds:
        second_rest = jnp.stack(second_back)
        second_rest_near = near_of(second_rest)
    for number, count in enumerate(FORWARD_CALLS):
        if rounds and number == 1:
            second_rest_far = far_from(hold_back(second_rest_near, forward))
            second_own = [second_one, second_rest, second_near[0], second_rest_near[0], second_near[1], second_rest_near[1]]
            second_own.append(far_from(second_near))
            second_other = swapped(hold_back(second_own[:-1], forward)) + swapped(second_own[-1:])
        if rounds and number == 2:
            forward, second_rest_far = hold_back((forward, second_rest_far), second_other)
        forward = attention_forward(mixed, feature_query, feature_key, forward, first_pair, count)
        first_pair += count
    if rounds:
        units_second = second_own + [second_rest_far] + second_other + [swap_core(second_rest_far)]
    attended_low, feature = forward
    out_hidden, grad_middle, grad_attended, sums, bias_sums, mine_later, give_later = middle_part(
        units_second, order, side, tiles, attended_low, row_in, row_cot, weight_mask, modulation, flat
    )
    state = [None]

    def backward_part(number, came):
        grad_here = grad_attended if came is None else hold_back(grad_attended, came)
        state[0] = attention_backward(
            mixed, feature, feature_key, grad_here, attended_low, cos, sin, state[0],
            sum(BACKWARD_CALLS[:number]), BACKWARD_CALLS[number],
        )
        return state[0]

    def qkv_end(sooner=None):
        follows = state[0] if sooner is None else hold_back(state[0], sooner)
        return qkv_grads(side, first_low, follows)

    def row_end(sooner=None):
        follows = state[0] if sooner is None else hold_back(state[0], sooner)
        return last_part(
            places, tiles, member_tile, follows, qkv_full, row_in, grad_middle, modulation, flat, condition_low,
            sums, bias_sums,
        )

    vector_arrays = (vectors, vectors_first, vectors_second)
    of_qkv, of_out = (qkv_weight, qkv_first, qkv_second), (out_weight, out_first, out_second)
    of_up, of_down = (up_weight, up_first, up_second), (down_weight, down_first, down_second)
    of_mod = (mod_weight, mod_first, mod_second)
    if rounds:
        later = Scatter(mine_later, give_later, places)
        backward_part(0, None)
        sent = later.send_far(state[0])
        backward_part(1, sent)
        sent = later.send_first(state[0])
        backward_part(2, sent)
        qkv_parts = qkv_end(later.arrived)
        sooner = Scatter(*qkv_parts, places)
        sent = later.send_column(qkv_parts)
        sent = sooner.send_far(sent)
        grad_in, *small_parts = row_end(sent)
        small = SmallScatter(*small_parts, places)
        sent = sooner.send_first((grad_in, later.came[0], later.came[2]))
        sent = sooner.send_column(sent)
        sent = small.send_first((sent, later.came[1]))
        sent = small.send_column((sent, sooner.came))
        later_sums = later.finish(sent)
        (out_new, up_new, down_new), later_table = update_moments(
            update_later_kernel, side, later_sums, of_out + of_up + of_down
        )
        qkv_sums = sooner.finish(later_table)
        small_sums = small.finish()
        (qkv_new, mod_new), sooner_table = update_moments(
            update_sooner_kernel, side, qkv_sums + (small_sums,), of_qkv + tuple(part.T for part in of_mod)
        )
        results = [qkv_new, out_new, up_new, down_new, mod_new]
        *renewed, norm_roots = renew(
            sum_small(later_table + sooner_table),
            [*matrices[:4], mod_weight.T],
            [record[2] for record in results],
        )
        renewed[4] = renewed[4].T
        results[4] = [part.T for part in mod_new]
        grad_vectors = small_sums[:5, 6 * COND :].reshape(-1)[:VECTOR_PART]
    else:
        for number in range(3):
            backward_part(number, None)
        grad_out, grad_up, grad_down = reduce_plain(unpack_second((mine_later, give_later)), (0, 0, 0))
        grad_in, *small_parts = row_end()
        grad_qkv, grad_mod, grad_vectors = reduce_plain(
            (unpack_qkv(qkv_end()), *unpack_small(*small_parts)), (0, 1, 0)
        )
        grads = (grad_qkv, grad_out, grad_up, grad_down, grad_mod)
        olds = (of_qkv, of_out, of_up, of_down, of_mod)
        results = [adam_direction(*old, grad, DECAY_RATE) for old, grad in zip(olds, grads)]
        squares = [
            jnp.stack([jnp.sum(values[number] * values[number]) for number in range(5)])
            for values in (matrices, [record[2] for record in results])
        ]
        norm_roots = jnp.sqrt(lax.psum(jnp.stack(squares), "fsdp"))
        trust = norm_roots[0] / (norm_roots[1] + EPSILON)
        renewed = [matrices[number] - MATRIX_RATE * trust[number] * results[number][2] for number in range(5)]
    vector_record = adam_direction(*vector_arrays, grad_vectors, 0.0)
    return (
        out_hidden[None],
        grad_in[None],
        *renewed,
        *[record[0] for record in results],
        *[record[1] for record in results],
        vectors - VECTOR_RATE * vector_record[2],
        vector_record[0],
        vector_record[1],
        norm_roots,
    )


def solution(mesh):
    rows = P(("rep", "fsdp"))
    matrix, turned, vector = P("fsdp", None), P(None, "fsdp"), P("fsdp")
    five = (matrix, matrix, matrix, matrix, turned)
    return jax.shard_map(
        on_device,
        mesh=mesh,
        in_specs=(rows,) * 6 + five * 3 + (vector,) * 3,
        out_specs=(rows, rows) + five * 3 + (vector,) * 3 + (P(),),
        check_vma=False,
    )
```

```python
import functools
import math

import jax
import jax.numpy as jnp
import numpy as np
from jax import lax
from jax.experimental import pallas as pl
from jax.experimental.pallas import tpu as pltpu
from jax.sharding import PartitionSpec as P

D = 768
HEADS = 12
HDIM = 64
FF = 3072
COND = 128
SLOTS = 1024
NSEG = 8
STEP = 10
TILE = 128
BLOCKS = SLOTS // TILE

BETA_ONE = 0.9
BETA_TWO = 0.999
EPSILON = 1e-06
DECAY_RATE = 0.01
MATRIX_RATE = 0.3
VECTOR_RATE = 1.0

PAIR = 128
NT = (((1,), (1,)), ((), ()))
NN = (((1,), (0,)), ((), ()))
TN = (((0,), (0,)), ((), ()))
BF = jnp.bfloat16
F32 = jnp.float32


def mm(a, b, dims=NN):
    return lax.dot_general(a, b, dims, preferred_element_type=F32)


def swap_halves(v):
    lane = lax.broadcasted_iota(jnp.int32, v.shape, 1)
    return jnp.where(lane % 64 < 32, pltpu.roll(v, PAIR - 32, 1), pltpu.roll(v, 32, 1))


def attention_forward_kernel(block, q_ref, k_ref, v_ref, fq_ref, fk_ref, *refs):
    o_ref, fo_ref, ka, kb, va, vb = refs[-6:]
    slots = q_ref.shape[0]
    low_all = lax.broadcasted_iota(jnp.int32, (slots, PAIR), 1) < 64
    k_low = k_ref[...]
    v_low = v_ref[...]
    fk = fk_ref[...]
    one = jnp.ones((slots, PAIR), BF)
    ka[...] = jnp.where(low_all, k_low, fk)
    kb[...] = jnp.where(low_all, fk, k_low)
    va[...] = jnp.where(low_all, v_low, one)
    vb[...] = jnp.where(low_all, one, v_low)
    lane = lax.broadcasted_iota(jnp.int32, (block, PAIR), 1)
    low = lane < 64
    spot = lane % 64

    def step(i, carry):
        at = pl.ds(pl.multiple_of(i * block, block), block)
        q = q_ref[at, :]
        fq = fq_ref[at, :]
        sa = mm(jnp.where(low, q, fq), ka[...], NT)
        sb = mm(jnp.where(low, fq, q), kb[...], NT)
        ma = jnp.max(sa, axis=1, keepdims=True)
        mb = jnp.max(sb, axis=1, keepdims=True)
        pa = jnp.exp(sa - ma).astype(BF)
        pb = jnp.exp(sb - mb).astype(BF)
        oa = mm(pa, va[...])
        ob = mm(pb, vb[...])
        o = jnp.where(low, oa / pltpu.roll(oa, 64, 1), ob / pltpu.roll(ob, 64, 1))
        o_ref[at, :] = o.astype(o_ref.dtype)
        neg = jnp.where(low, -(mb + jnp.log(ob)), -(ma + jnp.log(oa)))
        hi = neg.astype(BF)
        rest = neg - hi.astype(F32)
        mid = rest.astype(BF)
        last = (rest - mid.astype(F32)).astype(BF)
        fo_ref[at, :] = jnp.where(spot == 8, hi, jnp.where(spot == 9, mid, jnp.where(spot == 10, last, fq)))
        return carry

    lax.fori_loop(0, slots // block, step, 0)


def attention_forward(qkv, fq, fk, before, first, count, block=1024):
    slots, width = qkv.shape
    pairs = width // 3 // PAIR
    blk = lambda off: pl.BlockSpec((slots, PAIR), lambda p: (0, off + p))
    fixed = pl.BlockSpec((slots, PAIR), lambda p: (0, 0))
    anywhere = pl.BlockSpec(memory_space=pl.ANY)
    shape = jax.ShapeDtypeStruct((slots, pairs * PAIR), BF)
    extra = () if before is None else before
    elements = 2 * count * slots * slots
    return pl.pallas_call(
        functools.partial(attention_forward_kernel, block),
        grid=(count,),
        in_specs=[blk(first), blk(pairs + first), blk(2 * pairs + first), fixed, fixed] + [anywhere] * len(extra),
        out_specs=[blk(first)] * 2,
        out_shape=[shape, shape],
        scratch_shapes=[pltpu.VMEM((slots, PAIR), BF)] * 4,
        input_output_aliases={5: 0, 6: 1} if extra else {},
        cost_estimate=pl.CostEstimate(flops=elements * 3000, bytes_accessed=10 * slots * count * PAIR, transcendentals=elements),
        compiler_params=pltpu.CompilerParams(vmem_limit_bytes=62 * 2**20),
    )(qkv, qkv, qkv, fq, fk, *extra)


def attention_backward_kernel(block, q_ref, k_ref, v_ref, fo_ref, fk_ref, do_ref, o_ref, cos_ref, sin_ref, *refs):
    g_ref, ka, kb, va, vb, kt, dka, dkb, dva, dvb = refs[-10:]
    slots = q_ref.shape[0]
    lane_all = lax.broadcasted_iota(jnp.int32, (slots, PAIR), 1)
    low_all = lane_all < 64
    fk = fk_ref[...]
    k_low = k_ref[...]
    v_low = v_ref[...]
    one = jnp.where(lane_all % 64 < 2, 1.0, 0.0).astype(BF)
    ka[...] = jnp.where(low_all, k_low, fk)
    kb[...] = jnp.where(low_all, fk, k_low)
    va[...] = jnp.where(low_all, v_low, one)
    vb[...] = jnp.where(low_all, one, v_low)
    kt[...] = k_low.T
    dka[...] = jnp.zeros_like(dka)
    dkb[...] = jnp.zeros_like(dkb)
    dva[...] = jnp.zeros_like(dva)
    dvb[...] = jnp.zeros_like(dvb)
    lane = lax.broadcasted_iota(jnp.int32, (block, PAIR), 1)
    low = lane < 64
    spot = lane % 64
    top = lax.broadcasted_iota(jnp.int32, (PAIR, block), 0) < 64

    def step(i, carry):
        at = pl.ds(pl.multiple_of(i * block, block), block)
        q = q_ref[at, :]
        fq = fo_ref[at, :]
        do = do_ref[at, :]
        both = do.astype(F32) * o_ref[at, :].astype(F32)
        da = jnp.sum(jnp.where(low, both, 0.0), axis=1, keepdims=True)
        db = jnp.sum(jnp.where(low, 0.0, both), axis=1, keepdims=True)
        neg = jnp.where(low, -db, -da)
        hi = neg.astype(BF)
        rest = (neg - hi.astype(F32)).astype(BF)
        fd = jnp.where(spot == 0, hi, jnp.where(spot == 1, rest, jnp.zeros_like(hi)))
        sa = mm(ka[...], jnp.where(low, q, fq), NT)
        sb = mm(kb[...], jnp.where(low, fq, q), NT)
        ea = mm(va[...], jnp.where(low, do, fd), NT)
        eb = mm(vb[...], jnp.where(low, fd, do), NT)
        pa = jnp.exp(sa)
        pb = jnp.exp(sb)
        dsa = (pa * ea).astype(BF)
        dsb = (pb * eb).astype(BF)
        dva[...] += mm(pa.astype(BF), do)
        dvb[...] += mm(pb.astype(BF), do)
        dka[...] += mm(dsa, q)
        dkb[...] += mm(dsb, q)
        dqt = jnp.where(top, mm(kt[...], dsa), mm(kt[...], dsb))
        dq = dqt.T * 0.125
        g_ref[0, at, :] = (dq * cos_ref[at, :] - swap_halves(dq) * sin_ref[at, :]).astype(BF)
        return carry

    lax.fori_loop(0, slots // block, step, 0)
    dk = jnp.where(low_all, dka[...], dkb[...])
    g_ref[1] = (dk * cos_ref[...] - swap_halves(dk) * sin_ref[...]).astype(BF)
    g_ref[2] = jnp.where(low_all, dva[...], dvb[...]).astype(BF)


def attention_backward(qkv, fo, fk, do, o, cos, sin, before, first, count, block=512):
    slots, width = qkv.shape
    pairs = width // 3 // PAIR
    blk = lambda off: pl.BlockSpec((slots, PAIR), lambda p: (0, off + p))
    fixed = pl.BlockSpec((slots, PAIR), lambda p: (0, 0))
    extra = () if before is None else (before,)
    elements = 2 * count * slots * slots
    return pl.pallas_call(
        functools.partial(attention_backward_kernel, block),
        grid=(count,),
        in_specs=[blk(first), blk(pairs + first), blk(2 * pairs + first), blk(first), fixed, blk(first), blk(first),
                  fixed, fixed] + [pl.BlockSpec(memory_space=pl.ANY)] * len(extra),
        out_specs=pl.BlockSpec((3, slots, PAIR), lambda p: (0, 0, first + p)),
        out_shape=jax.ShapeDtypeStruct((3, slots, pairs * PAIR), BF),
        scratch_shapes=[pltpu.VMEM((slots, PAIR), BF)] * 4 + [pltpu.VMEM((PAIR, slots), BF)]
        + [pltpu.VMEM((slots, PAIR), F32)] * 4,
        input_output_aliases={9: 0} if extra else {},
        cost_estimate=pl.CostEstimate(flops=elements * 2000, bytes_accessed=20 * slots * count * PAIR, transcendentals=elements),
        compiler_params=pltpu.CompilerParams(vmem_limit_bytes=62 * 2**20),
    )(qkv, qkv, qkv, fo, fk, do, o, cos, sin, *extra)


def attention_tables(segment, position, valid_slot):
    inverse = jnp.exp(jnp.arange(32, dtype=F32) * (-math.log(10000.0) / 32))
    angles = position.astype(F32)[:, None] * inverse[None, :]
    c, s = jnp.cos(angles), jnp.sin(angles)
    cos = jnp.concatenate([c, c, c, c], axis=1)
    sin = jnp.concatenate([-s, s, -s, s], axis=1)
    spot = jnp.arange(PAIR) % 64
    same = segment[:, None] == spot[None, :]
    fq = same.astype(BF)
    fk = jnp.where((spot < 8)[None, :], jnp.where(same & valid_slot[:, None], 0.0, -1e30),
                   jnp.where((spot < 11)[None, :], 1.0, 0.0)).astype(BF)
    return cos, sin, fq, fk


UNITS = 16
QKV_HALF = 3 * D // 2
SMALL_WIDE = 6 * COND + 128
FIRST_WIDE = QKV_HALF + 3 * COND + 128
UP_AT, DOWN_AT, OUT_AT, SECOND_WIDE = 0, FF // 2, FF // 2 + 2 * D, FF // 2 + 2 * D + D // 2
VECTOR_PART = (9 * D + FF) // UNITS
FLAT_ROWS = 80
HBM = pltpu.HBM
SMALL_VMEM = pl.BlockSpec(memory_space=pltpu.SMEM)


def whole(shape):
    return pl.BlockSpec(shape, lambda *_: (0,) * len(shape), pipeline_mode=pl.Buffered(1))


def line(flat_ref, start, count):
    return jnp.concatenate([flat_ref[start + i : start + i + 1, :] for i in range(count)], axis=1)


def unit_of(units, half, place):
    if len(units) == 10:
        kind, back = place // 4, place % 4
        return units[half * 5 + (kind if kind < 3 else 3 + back // 2)].at[back if kind < 3 else back % 2]
    return units[half * 8 + place // 4 * 2 + min(place % 4, 1)].at[max(place % 4 - 1, 0)]


def unit_copies(units, order, core, sems, plan, first_sem):
    copies = []
    for half in range(2):
        side = core if half == 0 else 1 - core
        for place in range(UNITS):
            origin = order[half * UNITS + place]
            for target, rows, column, width, by_origin, by_side, row, column_side, both in plan:
                if half == 1 and not both:
                    continue
                to_row = pl.multiple_of(origin * by_origin + side * by_side + row, 16)
                to_column = pl.multiple_of(side * column_side, 128) if column_side else 0
                copies.append(
                    pltpu.make_async_copy(
                        unit_of(units, half, place).at[pl.ds(0, rows), pl.ds(column, width)],
                        target.at[pl.ds(to_row, rows), pl.ds(to_column, width)],
                        sems.at[first_sem + len(copies)],
                    )
                )
    return copies


def layer_norm(values):
    average = jnp.mean(values, axis=-1, keepdims=True)
    centered = values - average
    root = lax.rsqrt(jnp.mean(centered * centered, axis=-1, keepdims=True) + 1e-05)
    return (centered * root, root)


def layer_norm_back(grad, normal, root, gain):
    scaled = grad * gain
    inner = jnp.mean(scaled * normal, axis=-1, keepdims=True)
    return root * (scaled - jnp.mean(scaled, axis=-1, keepdims=True) - normal * inner)


def first_kernel(rows, order_ref, core_ref, tiles_ref, *refs):
    units = refs[:10]
    x_ref, cond_ref, cos_ref, sin_ref, qkv_ref, first_ref, w_ref, mod_ref, flat_ref, modt, vecs, sems = refs[10:]
    step = pl.program_id(0)

    @pl.when(step == 0)
    def _():
        core = core_ref[0]
        small = unit_copies(units, order_ref, core, sems, (
            (vecs, 16, QKV_HALF + 3 * COND, 128, 16, 0, 0, 0, False),
            (modt, 48, QKV_HALF, 128, 288, 144, 0, 0, True),
            (modt, 48, QKV_HALF + 128, 128, 288, 144, 48, 0, True),
            (modt, 48, QKV_HALF + 256, 128, 288, 144, 96, 0, True),
        ), 0)
        large = unit_copies(units, order_ref, core, sems, (
            (w_ref, 48, 0, QKV_HALF, 48, 0, 0, QKV_HALF, True),
        ), len(small))
        for copy in small + large:
            copy.start()
        for copy in small:
            copy.wait()
        flat_ref[...] = jnp.zeros_like(flat_ref)
        lane = lax.broadcasted_iota(jnp.int32, (8, 128), 1)
        for part in range(UNITS):
            row, turn = divmod(VECTOR_PART * part, 128)
            piece = vecs[16 * part : 16 * part + 16, :].astype(F32)[:8]
            if turn:
                piece = pltpu.roll(piece, turn, 1)
                flat_ref[row + 1 : row + 6, :] += jnp.where(lane < turn, piece, 0.0)[:5]
                piece = jnp.where(lane >= turn, piece, 0.0)
            flat_ref[row : row + 5, :] += piece[:5]
        mod_ref[...] = mm(cond_ref[...], modt[...], NT) + line(flat_ref, (3 * D + FF) // 128, 6 * D // 128)
        for copy in large:
            copy.wait()

    gain = line(flat_ref, 0, D // 128)
    for part in range(rows // TILE):
        at = pl.ds(part * TILE, TILE)
        segment = tiles_ref[step * (rows // TILE) + part]
        normal, _ = layer_norm(x_ref[at, :].astype(F32))
        shift = mod_ref[pl.ds(segment, 1), 0:D]
        scale = mod_ref[pl.ds(segment, 1), D : 2 * D]
        first_ref[at, :] = (normal * (gain * (1.0 + scale)) + shift).astype(BF)
    first = first_ref[...]
    cos, sin = cos_ref[...], sin_ref[...]
    for kind in range(3):
        mixed = mm(first, w_ref[:, kind * D : (kind + 1) * D])
        if kind < 2:
            for pair in range(D // PAIR):
                part = mixed[:, pair * PAIR : (pair + 1) * PAIR]
                turned = part * cos + swap_halves(part) * sin
                if kind == 0:
                    turned = turned * HDIM ** (-0.5)
                qkv_ref[:, kind * D + pair * PAIR : kind * D + (pair + 1) * PAIR] = turned.astype(BF)
        else:
            qkv_ref[:, 2 * D :] = mixed.astype(BF)


def first_part(units, order, core, tiles, x, cond, cos, sin, rows=256):
    count = UNITS * (1 + 2 * 3 + 2)
    row = lambda width: pl.BlockSpec((rows, width), lambda i: (i, 0))
    shape = lambda s, t: jax.ShapeDtypeStruct(s, t)
    return pl.pallas_call(
        functools.partial(first_kernel, rows),
        grid=(SLOTS // rows,),
        in_specs=[SMALL_VMEM] * 3 + [pl.BlockSpec(memory_space=HBM)] * 10
        + [row(D), whole((NSEG, COND)), row(PAIR), row(PAIR)],
        out_specs=[row(3 * D), row(D), whole((D, 3 * D)), whole((NSEG, 6 * D)), whole((FLAT_ROWS, 128))],
        out_shape=[shape((SLOTS, 3 * D), BF), shape((SLOTS, D), BF), shape((D, 3 * D), BF),
                   shape((NSEG, 6 * D), F32), shape((FLAT_ROWS, 128), F32)],
        scratch_shapes=[pltpu.VMEM((6 * D, COND), BF), pltpu.VMEM((16 * UNITS, 128), BF), pltpu.SemaphoreType.DMA((count,))],
        cost_estimate=pl.CostEstimate(flops=2 * SLOTS * D * 3 * D, bytes_accessed=20 * 2**20, transcendentals=SLOTS),
        compiler_params=pltpu.CompilerParams(vmem_limit_bytes=56 * 2**20),
    )(order, core, tiles, *units, x, cond, cos, sin)


def middle_kernel(rows, order_ref, core_ref, tiles_ref, *refs):
    units = refs[:16]
    (att_all, x_ref, cot_ref, mask_ref, mod_ref, flat_ref,
     out_ref, gmid_ref, gatt_ref, sums_ref, bias_ref, mine_ref, give_ref,
     wo, wu, wd, hidden_s, second_s, grad_mlp_s, grad_up_s, grad_branch_s, branch_s, buffer, sems, out_sems) = refs[16:]
    step = pl.program_id(0)
    core = core_ref[0]

    @pl.when(step < SLOTS // rows)
    def _():
        middle_rows(
            rows, step, core, order_ref, tiles_ref, units, att_all, x_ref, cot_ref, mask_ref, mod_ref, flat_ref,
            out_ref, gmid_ref, gatt_ref, sums_ref, bias_ref,
            wo, wu, wd, hidden_s, second_s, grad_mlp_s, grad_up_s, grad_branch_s, branch_s, sems,
        )

    @pl.when(step >= SLOTS // rows)
    def _():
        later_grads(
            step - SLOTS // rows, core, hidden_s, second_s, att_all, grad_mlp_s, grad_up_s, grad_branch_s,
            mine_ref, give_ref, buffer, out_sems,
        )


def middle_rows(
    rows, step, core, order_ref, tiles_ref, units, att_all, x_ref, cot_ref, mask_ref, mod_ref, flat_ref,
    out_ref, gmid_ref, gatt_ref, sums_ref, bias_ref,
    wo, wu, wd, hidden_s, second_s, grad_mlp_s, grad_up_s, grad_branch_s, branch_s, sems,
):
    chunks = FF // D
    here = pl.ds(pl.multiple_of(step * rows, rows), rows)

    def part_of(part):
        return pl.ds(pl.multiple_of(step * rows + part * TILE, TILE), TILE)

    tiles = rows // TILE
    each = 2 * UNITS
    copies = [
        unit_copies(units, order_ref, core, sems, ((wo, 48, OUT_AT, D // 2, 48, 0, 0, D // 2, True),), 0),
        unit_copies(units, order_ref, core, sems, ((wu, 48, UP_AT, FF // 2, 48, 0, 0, FF // 2, True),), each),
        unit_copies(units, order_ref, core, sems, (
            (wd, 48, DOWN_AT, D, 192, 96, 0, 0, True),
            (wd, 48, DOWN_AT + D, D, 192, 96, 48, 0, True),
        ), 2 * each),
    ]

    @pl.when(step == 0)
    def _():
        for group in copies:
            for copy in group:
                copy.start()
        bias_ref[...] = jnp.zeros_like(bias_ref)
        for copy in copies[0]:
            copy.wait()

    def table(part, kind):
        return mod_ref[pl.ds(tiles_ref[step * tiles + part], 1), kind * D : (kind + 1) * D]

    def mask_column(part):
        row = mask_ref[pl.ds(step * tiles + part, 1), :]
        return jnp.broadcast_to(row, (TILE, TILE)).T[:, :1]

    branch_s[...] = mm(att_all[here, :], wo[...])
    gain = line(flat_ref, D // 128, D // 128)
    for part in range(tiles):
        at = pl.ds(part * TILE, TILE)
        middle = x_ref[at, :].astype(F32) + table(part, 2) * branch_s[at, :]
        gmid_ref[at, :] = middle
        normal, _ = layer_norm(middle)
        second_s[part_of(part), :] = (normal * (gain * (1.0 + table(part, 4))) + table(part, 3)).astype(BF)

    @pl.when(step == 0)
    def _():
        for group in copies[1:]:
            for copy in group:
                copy.wait()

    for part in range(tiles):
        at = pl.ds(part * TILE, TILE)
        grad_mlp = (cot_ref[at, :].astype(F32) * mask_column(part) * table(part, 5)).astype(BF)
        grad_mlp_s[part_of(part), :] = grad_mlp
        bias_ref[0:1, FF:] += jnp.sum(grad_mlp.astype(F32), axis=0, keepdims=True)
    second = second_s[here, :]
    grad_mlp = grad_mlp_s[here, :]
    factor = math.sqrt(2.0 / math.pi)
    feed, grad_second = None, None
    for j in range(chunks):
        at = pl.ds(j * D, D)
        u = mm(second, wu[:, at]) + line(flat_ref, 2 * D // 128 + j * (D // 128), D // 128)
        grad_hidden = mm(grad_mlp, wd[at, :], NT)
        square = u * u
        bent = jnp.tanh(u * (factor + (factor * 0.044715) * square))
        half = 0.5 * u
        bow = half * bent
        hidden = (half + bow).astype(BF)
        slope = (0.5 + 0.5 * bent) + (half - bow * bent) * (factor + (3 * factor * 0.044715) * square)
        grad_up = (grad_hidden * slope).astype(BF)
        hidden_s[here, at] = hidden
        grad_up_s[here, at] = grad_up
        bias_ref[0:1, at] += jnp.sum(grad_up.astype(F32), axis=0, keepdims=True)
        share, grad_share = mm(hidden, wd[at, :]), mm(grad_up, wu[:, at], NT)
        feed = share if feed is None else feed + share
        grad_second = grad_share if grad_second is None else grad_second + grad_share
    bias_down = line(flat_ref, (2 * D + FF) // 128, D // 128)
    for part in range(tiles):
        at = pl.ds(part * TILE, TILE)
        feed_out = feed[part * TILE : (part + 1) * TILE] + bias_down
        out_ref[at, :] = (gmid_ref[at, :] + table(part, 5) * feed_out).astype(BF)
        grad_out = cot_ref[at, :].astype(F32) * mask_column(part)
        sums_ref[part, 3:4, :] = jnp.sum(grad_out * feed_out, axis=0, keepdims=True)
    for part in range(tiles):
        at = pl.ds(part * TILE, TILE)
        normal, root = layer_norm(gmid_ref[at, :])
        grad = grad_second[part * TILE : (part + 1) * TILE]
        sums_ref[part, 1:2, :] = jnp.sum(grad, axis=0, keepdims=True)
        sums_ref[part, 2:3, :] = jnp.sum(grad * normal, axis=0, keepdims=True)
        grad_middle = cot_ref[at, :].astype(F32) * mask_column(part) + layer_norm_back(
            grad, normal, root, gain * (1.0 + table(part, 4))
        )
        gmid_ref[at, :] = grad_middle
        sums_ref[part, 0:1, :] = jnp.sum(grad_middle * branch_s[at, :], axis=0, keepdims=True)
        grad_branch_s[part_of(part), :] = (grad_middle * table(part, 2)).astype(BF)
    gatt_ref[...] = mm(grad_branch_s[here, :], wo[...], NT).astype(BF)


def later_grads(step, core, hidden_s, second_s, att_all, grad_mlp_s, grad_up_s, grad_branch_s, mine_ref, give_ref, buffer, sems):
    down_steps = FF // D
    steps = 2 * down_steps + 1
    slot = step % 2

    def wait(at_slot):
        for number in range(16):
            pltpu.make_async_copy(buffer.at[at_slot, number], buffer.at[at_slot, number], sems.at[at_slot, number]).wait()

    def send(source, side, place, number):
        for ref, wanted in ((mine_ref, 0), (give_ref, 1)):
            @pl.when((core ^ side) == wanted)
            def _():
                pltpu.make_async_copy(source, ref.at[place], sems.at[slot, number]).start()

    def keep(left, right):
        buffer[slot] = mm(left, right, TN).astype(BF).reshape(16, 48, D)

    @pl.when(step >= 2)
    def _():
        wait(slot)

    @pl.when(step < down_steps)
    def _():
        keep(hidden_s[:, pl.ds(pl.multiple_of(step * D, D), D)], grad_mlp_s[...])
        for number in range(16):
            local, side, block = number // 4, (number // 2) % 2, number % 2
            send(buffer.at[slot, number], side, (4 * step + local, pl.ds(0, 48), pl.ds(DOWN_AT + block * D, D)), number)

    @pl.when((step >= down_steps) & (step < steps - 1))
    def _():
        keep(second_s[...], grad_up_s[:, pl.ds(pl.multiple_of((step - down_steps) * D, D), D)])

    for j in range(down_steps):
        @pl.when(step == down_steps + j)
        def _():
            for number in range(16):
                send(buffer.at[slot, number], j // 2, (number, pl.ds(0, 48), pl.ds(UP_AT + (j % 2) * D, D)), number)

    @pl.when(step == steps - 1)
    def _():
        keep(att_all[...], grad_branch_s[...])
        for number in range(16):
            for side in range(2):
                source = buffer.at[slot, number, pl.ds(0, 48), pl.ds(side * (D // 2), D // 2)]
                send(source, side, (number, pl.ds(0, 48), pl.ds(OUT_AT, D // 2)), number)
        wait(1 - slot)
        wait(slot)


def middle_part(units, order, core, tiles, att, x, cot, mask, modulation, flat, rows=512):
    last = SLOTS // rows - 1
    row = lambda width: pl.BlockSpec((rows, width), lambda i: (jnp.minimum(i, last), 0))
    shape = lambda s, t: jax.ShapeDtypeStruct(s, t)
    units_shape = shape((UNITS, 48, SECOND_WIDE), BF)
    kept = lambda width: pltpu.VMEM((SLOTS, width), BF)
    return pl.pallas_call(
        functools.partial(middle_kernel, rows),
        grid=(SLOTS // rows + 2 * (FF // D) + 1,),
        in_specs=[SMALL_VMEM] * 3 + [pl.BlockSpec(memory_space=HBM)] * 16
        + [whole((SLOTS, D)), row(D), row(D), whole((BLOCKS, TILE)), whole((NSEG, 6 * D)), whole((FLAT_ROWS, 128))],
        out_specs=[row(D), row(D), row(D),
                   pl.BlockSpec((rows // TILE, 8, D), lambda i: (jnp.minimum(i, last), 0, 0)), whole((8, FF + D))]
        + [pl.BlockSpec(memory_space=HBM)] * 2,
        out_shape=[shape((SLOTS, D), BF), shape((SLOTS, D), F32), shape((SLOTS, D), BF), shape((BLOCKS, 8, D), F32),
                   shape((8, FF + D), F32), units_shape, units_shape],
        scratch_shapes=[pltpu.VMEM((D, D), BF), pltpu.VMEM((D, FF), BF), pltpu.VMEM((FF, D), BF),
                        kept(FF), kept(D), kept(D), kept(FF), kept(D),
                        pltpu.VMEM((rows, D), F32), pltpu.VMEM((2, 16, 48, D), BF),
                        pltpu.SemaphoreType.DMA((8 * UNITS,)), pltpu.SemaphoreType.DMA((2, 16))],
        cost_estimate=pl.CostEstimate(flops=6 * SLOTS * D * (D + 2 * FF), bytes_accessed=50 * 2**20, transcendentals=SLOTS * FF),
        compiler_params=pltpu.CompilerParams(vmem_limit_bytes=63 * 2**20),
    )(order, core, tiles, *units, att, x, cot, mask, modulation, flat)


def qkv_grads_kernel(core_ref, first_ref, g_ref, mine_ref, give_ref, units, sems):
    step = pl.program_id(0)
    core = core_ref[0]
    product = mm(first_ref[...], g_ref[0], TN).astype(BF).reshape(UNITS, 48, D)

    @pl.when(step == 0)
    def _():
        units[0, :, :, 0:D] = product

    @pl.when(step == 1)
    def _():
        units[0, :, :, D:] = product[:, :, : D // 2]
        units[1, :, :, 0 : D // 2] = product[:, :, D // 2 :]

    @pl.when(step == 2)
    def _():
        units[1, :, :, D // 2 :] = product
        copies = [
            pltpu.make_async_copy(units.at[core], mine_ref, sems.at[0]),
            pltpu.make_async_copy(units.at[1 - core], give_ref, sems.at[1]),
        ]
        for copy in copies:
            copy.start()
        for copy in copies:
            copy.wait()


def qkv_grads(core, first, g):
    shape = jax.ShapeDtypeStruct((UNITS, 48, QKV_HALF), BF)
    return pl.pallas_call(
        qkv_grads_kernel,
        grid=(3,),
        in_specs=[SMALL_VMEM, whole((SLOTS, D)), pl.BlockSpec((1, SLOTS, D), lambda i: (i, 0, 0))],
        out_specs=[pl.BlockSpec(memory_space=HBM)] * 2,
        out_shape=[shape, shape],
        scratch_shapes=[pltpu.VMEM((2, UNITS, 48, QKV_HALF), BF), pltpu.SemaphoreType.DMA((2,))],
        cost_estimate=pl.CostEstimate(flops=SLOTS * D * D, bytes_accessed=2**20, transcendentals=0),
        compiler_params=pltpu.CompilerParams(vmem_limit_bytes=62 * 2**20),
    )(core, first, g)


def last_kernel(rows, places_ref, tiles_ref, member_ref, g_ref, w_ref, x_ref, gmid_ref, mod_ref, flat_ref, cond_ref,
                sums_in, bias_in, gin_ref, own_ref, first_ref, second_ref, far_ref, sums, units, sems):
    step = pl.program_id(0)
    tiles = rows // TILE
    steps = SLOTS // rows
    gain = line(flat_ref, 0, D // 128)

    grad = None
    for kind in range(3):
        share = mm(g_ref[kind], w_ref[:, kind * D : (kind + 1) * D], NT)
        grad = share if grad is None else grad + share
    for part in range(tiles):
        at = pl.ds(part * TILE, TILE)
        tile = step * tiles + part
        segment = tiles_ref[tile]
        normal, root = layer_norm(x_ref[at, :].astype(F32))
        piece = grad[part * TILE : (part + 1) * TILE]
        scale = mod_ref[pl.ds(segment, 1), D : 2 * D]
        sums[pl.ds(tile, 1), 0:D] = jnp.sum(piece, axis=0, keepdims=True)
        sums[pl.ds(tile, 1), D : 2 * D] = jnp.sum(piece * normal, axis=0, keepdims=True)
        gin_ref[at, :] = gmid_ref[at, :] + layer_norm_back(piece, normal, root, gain * (1.0 + scale))

    @pl.when(step == steps - 1)
    def _():
        gain_two = line(flat_ref, D // 128, D // 128)
        for tile in range(BLOCKS):
            at = pl.ds(tile, 1)
            sums[at, 2 * D : 3 * D] = sums_in[tile, 0:1, :]
            sums[at, 3 * D : 4 * D] = sums_in[tile, 1:2, :]
            sums[at, 4 * D : 5 * D] = sums_in[tile, 2:3, :]
            sums[at, 5 * D : 6 * D] = sums_in[tile, 3:4, :]
        member = member_ref[...]
        scale_one = lax.dot_general(member, mod_ref[:, D : 2 * D], NN, precision=lax.Precision.HIGHEST, preferred_element_type=F32)
        scale_two = lax.dot_general(member, mod_ref[:, 4 * D : 5 * D], NN, precision=lax.Precision.HIGHEST, preferred_element_type=F32)
        grad_gain_one = jnp.sum(sums[:, D : 2 * D] * (1.0 + scale_one), axis=0, keepdims=True)
        grad_gain_two = jnp.sum(sums[:, 4 * D : 5 * D] * (1.0 + scale_two), axis=0, keepdims=True)
        sums[:, D : 2 * D] = sums[:, D : 2 * D] * gain
        sums[:, 4 * D : 5 * D] = sums[:, 4 * D : 5 * D] * gain_two
        by_segment = lax.dot_general(member, sums[...], TN, precision=lax.Precision.HIGHEST, preferred_element_type=F32)
        grad_mod = lax.dot_general(
            by_segment, cond_ref[...].astype(F32), TN, precision=lax.Precision.HIGHEST, preferred_element_type=F32
        ).astype(BF).reshape(4, 4, 6, 48, COND)
        for block in range(6):
            units[:, :, :, block * COND : (block + 1) * COND] = grad_mod[:, :, block]
        row = jnp.concatenate(
            [grad_gain_one, grad_gain_two, bias_in[0:1, :], jnp.sum(by_segment, axis=0, keepdims=True)], axis=1
        )
        lane = lax.broadcasted_iota(jnp.int32, (1, 128), 1)
        blank = jnp.zeros((43, 128), F32)
        for part in range(UNITS):
            start = VECTOR_PART * part
            pieces = []
            for number in range(5):
                first_row, turn = divmod(start + 128 * number, 128)
                piece = row[:, first_row * 128 : (first_row + 1) * 128]
                if turn:
                    following = (
                        row[:, (first_row + 1) * 128 : (first_row + 2) * 128]
                        if (first_row + 2) * 128 <= row.shape[1]
                        else jnp.zeros((1, 128), F32)
                    )
                    piece = jnp.where(
                        lane < 128 - turn, pltpu.roll(piece, 128 - turn, 1), pltpu.roll(following, 128 - turn, 1)
                    )
                if number == 4:
                    piece = jnp.where(lane < VECTOR_PART - 512, piece, 0.0)
                pieces.append(piece)
            stack = jnp.concatenate(pieces + [blank], axis=0).astype(BF)
            units[part // 4, part % 4, :, 6 * COND :] = stack
        copies = [
            pltpu.make_async_copy(units.at[:, places_ref[kind]], ref, sems.at[kind])
            for kind, ref in enumerate((own_ref, first_ref, second_ref, far_ref))
        ]
        for copy in copies:
            copy.start()
        for copy in copies:
            copy.wait()


def last_part(places, tiles, member, g, w, x, gmid, modulation, flat, cond, sums, bias, rows=256):
    row = lambda width: pl.BlockSpec((rows, width), lambda i: (i, 0))
    shape = jax.ShapeDtypeStruct((4, 48, SMALL_WIDE), BF)
    return pl.pallas_call(
        functools.partial(last_kernel, rows),
        grid=(SLOTS // rows,),
        in_specs=[SMALL_VMEM, SMALL_VMEM, whole((BLOCKS, NSEG)), pl.BlockSpec((3, rows, D), lambda i: (0, i, 0)), whole((D, 3 * D)),
                  row(D), row(D), whole((NSEG, 6 * D)), whole((FLAT_ROWS, 128)), whole((NSEG, COND)),
                  whole((BLOCKS, 8, D)), whole((8, FF + D))],
        out_specs=[row(D)] + [pl.BlockSpec(memory_space=HBM)] * 4,
        out_shape=[jax.ShapeDtypeStruct((SLOTS, D), F32)] + [shape] * 4,
        scratch_shapes=[pltpu.VMEM((BLOCKS, 6 * D), F32), pltpu.VMEM((4, 4, 48, SMALL_WIDE), BF),
                        pltpu.SemaphoreType.DMA((4,))],
        cost_estimate=pl.CostEstimate(flops=2 * SLOTS * D * 3 * D, bytes_accessed=30 * 2**20, transcendentals=SLOTS),
        compiler_params=pltpu.CompilerParams(vmem_limit_bytes=60 * 2**20),
    )(places, tiles, member, g, w, x, gmid, modulation, flat, cond, sums, bias)


def moments(weight_ref, first_ref, second_ref, gradient, first_out, second_out, direction_out, decay_rate=DECAY_RATE):
    weight = weight_ref[...]
    first_new = BETA_ONE * first_ref[...] + (1.0 - BETA_ONE) * gradient
    second_new = BETA_TWO * second_ref[...] + (1.0 - BETA_TWO) * gradient * gradient
    direction = (
        first_new
        / (1.0 - BETA_ONE**STEP)
        / (jnp.sqrt(second_new / (1.0 - BETA_TWO**STEP)) + EPSILON)
        + decay_rate * weight
    )
    first_out[...] = first_new
    second_out[...] = second_new
    direction_out[...] = direction
    return [jnp.sum(values * values, axis=(0, 1), keepdims=True) for values in (weight, direction)]


def squares_table(pairs):
    row = lax.broadcasted_iota(jnp.int32, (8, 128), 0)
    lane = lax.broadcasted_iota(jnp.int32, (8, 128), 1)
    table = jnp.zeros((8, 128), F32)
    for number, sums in pairs:
        for kind in range(2):
            table = jnp.where((row == kind) & (lane == number), sums[kind], table)
    return table


def update_later_kernel(side_ref, own_ref, other_ref, *refs):
    outs, table_ref = refs[9:18], refs[18]
    zero = side_ref[0] == 0
    own, other = own_ref[...].astype(F32), other_ref[...].astype(F32)
    halves = (jnp.where(zero, own, other), jnp.where(zero, other, own))
    out_grad = jnp.concatenate([half[:, OUT_AT:] for half in halves], axis=1)
    up_grad = jnp.concatenate([half[:, UP_AT : UP_AT + FF // 2] for half in halves], axis=1)
    down_grad = jnp.concatenate(
        [half[:, DOWN_AT + D * part : DOWN_AT + D * (part + 1)] for half in halves for part in range(2)], axis=0
    )
    table_ref[...] = squares_table(
        [
            (1 + place, moments(*refs[3 * place : 3 * place + 3], gradient, *outs[3 * place : 3 * place + 3]))
            for place, gradient in enumerate((out_grad, up_grad, down_grad))
        ]
    )


def update_sooner_kernel(side_ref, own_ref, other_ref, small_ref, *refs):
    outs, table_ref = refs[6:12], refs[12]
    zero = side_ref[0] == 0
    own, other = own_ref[...].astype(F32), other_ref[...].astype(F32)
    qkv_grad = jnp.concatenate([jnp.where(zero, own, other), jnp.where(zero, other, own)], axis=1)
    mod_grad = jnp.concatenate([small_ref[:, COND * part : COND * (part + 1)] for part in range(6)], axis=0)
    table_ref[...] = squares_table(
        [
            (4 * place, moments(*refs[3 * place : 3 * place + 3], gradient, *outs[3 * place : 3 * place + 3]))
            for place, gradient in enumerate((qkv_grad, mod_grad))
        ]
    )


def update_moments(kernel, side, parts, arrays):
    block = pl.BlockSpec(memory_space=pltpu.VMEM)
    shapes = [jax.ShapeDtypeStruct(arrays[3 * (i // 3)].shape, F32) for i in range(len(arrays))]
    *outs, table = pl.pallas_call(
        kernel,
        in_specs=[SMALL_VMEM] + [block] * (len(parts) + len(arrays)),
        out_specs=[block] * (len(arrays) + 1),
        out_shape=shapes + [jax.ShapeDtypeStruct((8, 128), F32)],
        compiler_params=pltpu.CompilerParams(vmem_limit_bytes=48 * 2**20),
    )(side, *parts, *arrays)
    return [outs[i : i + 3] for i in range(0, len(outs), 3)], table


def renew_kernel(table_ref, *refs):
    norms_ref = refs[15]
    roots = jnp.sqrt(table_ref[...])
    norms_ref[...] = roots[:2, :5]
    for number in range(5):
        trust = roots[0:1, number : number + 1] / (roots[1:2, number : number + 1] + EPSILON)
        refs[10 + number][...] = refs[number][...] - (MATRIX_RATE * trust) * refs[5 + number][...]


def renew(table, matrices, turns):
    block = pl.BlockSpec(memory_space=pltpu.VMEM)
    return pl.pallas_call(
        renew_kernel,
        in_specs=[block] * 11,
        out_specs=[block] * 6,
        out_shape=[jax.ShapeDtypeStruct(matrix.shape, F32) for matrix in matrices] + [jax.ShapeDtypeStruct((2, 5), F32)],
        compiler_params=pltpu.CompilerParams(vmem_limit_bytes=48 * 2**20),
    )(table, *matrices, *turns)


ALONG = ((1, 2), (2, 1))


def column_of(core, chip, kind):
    first, second = ALONG[core]
    return (chip % 4) ^ (0, first, second, first ^ second)[kind]


ORIGIN = np.array(
    [
        [[column_of(core, chip, kind) + 4 * ((chip // 4 - back) % 4) for kind in range(4) for back in range(4)]
         for chip in range(UNITS)]
        for core in range(2)
    ],
    np.int32,
)
PLACES = np.array(
    [
        [[column_of(core, chip, kind) for kind in range(4)] + [(chip // 4 + ahead) % 4 for ahead in range(4)]
         for chip in range(UNITS)]
        for core in range(2)
    ],
    np.int32,
)


def along_z(values, ahead):
    return lax.ppermute(values, "fsdp", [(chip, chip % 4 + 4 * ((chip // 4 + ahead) % 4)) for chip in range(UNITS)])


def along_plane(values, direction):
    moves = [
        (core * UNITS + chip, core * UNITS + (chip ^ ALONG[core][direction]))
        for core in range(2)
        for chip in range(UNITS)
    ]
    return lax.ppermute(values, ("rep", "fsdp"), moves)


def swap_core(values):
    return lax.ppermute(values, "rep", [(0, 1), (1, 0)])


def hold_back(later, sooner):
    return lax.optimization_barrier((later, sooner))[0]


def by_rounds():
    return lax.axis_size("fsdp") == UNITS


def far_from(near):
    return along_plane(near[0], 1)


def near_of(piece):
    return [along_plane(piece, 0), along_plane(piece, 1)]


def swapped(values):
    return [swap_core(one) for one in values]


def column_sums_kernel(counts, places_ref, *refs):
    outs = refs[len(refs) - len(counts) :]
    at = 0
    for out_ref, count in zip(outs, counts):
        total = refs[at][...].astype(F32) + refs[at + 1][...].astype(F32)
        for arrived in refs[at + 2 : at + 2 + count]:
            total = total + arrived[...].astype(F32).reshape(total.shape)
        out_ref[...] = total.astype(BF).reshape(out_ref.shape)
        at += 2 + count


def column_sums(places, mine, given, parts, apart=False):
    block = mine.shape[1:]
    pair = [values.reshape((4, 4) + block) for values in (mine, given)]
    specs, operands, counts = [], [], []
    for ahead in range(4) if apart else (None,):
        for kind, arrived in parts:
            if apart:
                pick = pl.BlockSpec((1, 1) + block, lambda i, s, kind=kind, ahead=ahead: (s[4 + ahead], s[kind], 0, 0))
                came = pl.BlockSpec((1,) + block, lambda i, s, ahead=ahead: (s[4 + ahead], 0, 0))
            else:
                pick = pl.BlockSpec((1, 1) + block, lambda i, s, kind=kind: (i, s[kind], 0, 0))
                came = pl.BlockSpec((1,) + block, lambda i, s: (i, 0, 0))
            specs += [pick, pick] + [came] * len(arrived)
            operands += pair + arrived
            counts.append(len(arrived))
    if apart:
        out_spec, out_shape = pl.BlockSpec(block, lambda i, s: (0, 0)), jax.ShapeDtypeStruct(block, BF)
    else:
        out_spec, out_shape = pl.BlockSpec((1,) + block, lambda i, s: (i, 0, 0)), jax.ShapeDtypeStruct((4,) + block, BF)
    return pl.pallas_call(
        functools.partial(column_sums_kernel, counts),
        grid_spec=pltpu.PrefetchScalarGridSpec(
            num_scalar_prefetch=1,
            grid=(1 if apart else 4,),
            in_specs=specs,
            out_specs=[out_spec] * len(counts),
        ),
        out_shape=[out_shape] * len(counts),
        cost_estimate=pl.CostEstimate(flops=0, bytes_accessed=(200 if apart else 12) * 2**20, transcendentals=0),
        compiler_params=pltpu.CompilerParams(vmem_limit_bytes=(62 if block[1] > D * 3 else 48) * 2**20),
    )(places, *operands)


class Scatter:
    def __init__(self, mine, give, places):
        self.mine, self.places = mine, places
        self.given = swap_core(give)

    def send_far(self, sooner=None):
        given = self.given if sooner is None else hold_back(self.given, sooner)
        far, second = column_sums(self.places, self.mine, given, [(3, []), (2, [])])
        self.far_came, self.second_came = along_plane(far, 1), along_plane(second, 1)
        return far

    def send_first(self, sooner=None):
        self.far_came, self.second_came = (
            (self.far_came, self.second_came) if sooner is None else hold_back((self.far_came, self.second_came), sooner)
        )
        (first,) = column_sums(self.places, self.mine, self.given, [(1, [self.far_came])])
        self.arrived = [along_plane(first, 0), self.second_came]
        return first

    def send_far_alone(self, sooner):
        (far,) = column_sums(self.places, self.mine, hold_back(self.given, sooner), [(3, [])])
        self.far_came = along_plane(far, 1)
        return far

    def send_neighbours(self, sooner):
        far_came = hold_back(self.far_came, sooner)
        first, second = column_sums(self.places, self.mine, self.given, [(1, [far_came]), (2, [])])
        self.arrived = [along_plane(first, 0), along_plane(second, 1)]
        return first

    def send_column(self, sooner=None):
        arrived = self.arrived if sooner is None else hold_back(self.arrived, sooner)
        units = column_sums(self.places, self.mine, self.given, [(0, arrived)], apart=True)
        self.own = units[0]
        self.came = [along_z(units[ahead], ahead) for ahead in range(1, 4)]
        return self.own

    def finish(self, sooner=None):
        came = self.came if sooner is None else hold_back(self.came, sooner)
        total = self.own.astype(F32)
        for part in came:
            total = total + part.astype(F32)
        own = total.astype(BF)
        return (own, swap_core(own))


def arrivals_kernel(outputs, *refs):
    inputs, outs = refs[1 : len(refs) - outputs], refs[len(refs) - outputs :]
    each = len(inputs) // outputs
    for number, out_ref in enumerate(outs):
        total = inputs[number * each][...].astype(F32)
        for part in inputs[number * each + 1 : (number + 1) * each]:
            total = total + part[...].astype(F32)
        out_ref[...] = total.reshape(out_ref.shape).astype(BF)


def arrival_sums(places, parts, apart):
    block = parts[0].shape[1:]
    if apart:
        specs = [
            pl.BlockSpec((1,) + block, lambda i, s, ahead=ahead: (s[4 + ahead], 0, 0)) for ahead in range(4) for _ in parts
        ]
        out_spec, out_shape, outputs = pl.BlockSpec(block, lambda i, s: (0, 0)), block, 4
    else:
        out_spec = pl.BlockSpec((4,) + block, lambda i, s: (0, 0, 0))
        specs, out_shape, outputs = [out_spec] * len(parts), (4,) + block, 1
    return pl.pallas_call(
        functools.partial(arrivals_kernel, outputs),
        grid_spec=pltpu.PrefetchScalarGridSpec(
            num_scalar_prefetch=1, grid=(1,), in_specs=specs, out_specs=[out_spec] * outputs
        ),
        out_shape=[jax.ShapeDtypeStruct(out_shape, BF)] * outputs,
    )(places, *(list(parts) * outputs))


class SmallScatter:
    def __init__(self, own, first, second, far, places):
        self.places, self.own, self.first = places, own, first
        self.far_came, self.second_came = along_plane(far, 1), along_plane(second, 1)

    def send_first(self, sooner):
        far_came, self.second_came = hold_back((self.far_came, self.second_came), sooner)
        first = (self.first.astype(F32) + far_came.astype(F32)).astype(BF)
        self.first_came = along_plane(first, 0)
        return first

    def send_column(self, sooner):
        came = hold_back(self.first_came, sooner)
        self.own, *units = arrival_sums(self.places, [self.own, came, self.second_came], True)
        self.came = [along_z(unit, ahead + 1) for ahead, unit in enumerate(units)]
        return self.own

    def finish(self, sooner):
        total = self.own.astype(F32)
        for part in hold_back(self.came, sooner):
            total = total + part.astype(F32)
        own = total.astype(BF)
        return own.astype(F32) + swap_core(own).astype(F32)


def sum_small(values):
    for turns in ((1, 2, 3), (4, 8, 12)):
        came = [lax.ppermute(values, "fsdp", [(chip, chip ^ turn) for chip in range(UNITS)]) for turn in turns]
        values = (values + came[0]) + (came[1] + came[2])
    return values


def side_columns(matrix, core, width):
    return lax.dynamic_slice_in_dim(matrix, core * width, width, axis=1)


def side_rows(blocks, core):
    return lax.dynamic_index_in_dim(blocks, core, 1, keepdims=False)


def pack_first(qkv, mod_turned, vectors, core):
    count = vectors.shape[0]
    mod_blocks = side_rows(mod_turned.reshape(count, 2, 3, 48, COND), core)
    padded = jnp.pad(vectors, ((0, 0), (0, 640 - VECTOR_PART))).reshape(count, 5, 128)
    return jnp.concatenate(
        [
            side_columns(qkv, core, QKV_HALF).reshape(count, 48, QKV_HALF),
            mod_blocks.transpose(0, 2, 1, 3).reshape(count, 48, 3 * COND),
            jnp.pad(padded, ((0, 0), (0, 43), (0, 0))),
        ],
        axis=2,
    )


def pack_second(out, up, down, core):
    count = out.shape[0] // 48
    down_blocks = side_rows(down.reshape(count, 2, 2, 48, D), core)
    return jnp.concatenate(
        [
            side_columns(up, core, FF // 2).reshape(count, 48, FF // 2),
            down_blocks.transpose(0, 2, 1, 3).reshape(count, 48, 2 * D),
            side_columns(out, core, D // 2).reshape(count, 48, D // 2),
        ],
        axis=2,
    )


def unpack_qkv(sides):
    return jnp.concatenate([side for side in sides], axis=2).reshape(-1, 3 * D)


def unpack_small(own, first, second, far):
    units = jnp.stack([own, first, second, far], axis=1).reshape(UNITS, 48, SMALL_WIDE)
    turned = units[:, :, : 6 * COND].reshape(UNITS, 48, 6, COND).transpose(0, 2, 1, 3).reshape(6 * D, COND)
    vectors = units[:, :5, 6 * COND :].reshape(UNITS, 640)[:, :VECTOR_PART]
    return (turned.T, vectors.reshape(-1))


def unpack_second(sides):
    count = sides[0].shape[0]
    up = jnp.concatenate([side[:, :, UP_AT : UP_AT + FF // 2] for side in sides], axis=2).reshape(count * 48, FF)
    out = jnp.concatenate([side[:, :, OUT_AT:] for side in sides], axis=2).reshape(count * 48, D)
    down = jnp.stack([side[:, :, DOWN_AT : DOWN_AT + 2 * D] for side in sides], axis=1)
    down = down.reshape(count, 2, 48, 2, D).transpose(0, 1, 3, 2, 4).reshape(count * 192, D)
    return (out, up, down)


def gather_plain(parts, axes):
    return [lax.all_gather(part, "fsdp", axis=axis, tiled=True) for part, axis in zip(parts, axes)]


def virtual_units(pack, pieces=False):
    cuts = [0, 1, 4, 5, 8, 9, 12, 13, 16] if pieces else [0, 4, 8, 12, 14, 16]
    return [packed[start:stop] for packed in (pack(0), pack(1)) for start, stop in zip(cuts, cuts[1:])]


def reduce_plain(grads, axes):
    parts = [
        lax.psum_scatter(grad.astype(F32), "fsdp", scatter_dimension=axis, tiled=True) for grad, axis in zip(grads, axes)
    ]
    return tuple(lax.psum(part.astype(BF), "rep").astype(F32) for part in parts)


def adam_direction(weight, first_old, second_old, gradient, decay_rate):
    first_new = BETA_ONE * first_old + (1.0 - BETA_ONE) * gradient
    second_new = BETA_TWO * second_old + (1.0 - BETA_TWO) * gradient * gradient
    direction = (
        first_new
        / (1.0 - BETA_ONE**STEP)
        / (jnp.sqrt(second_new / (1.0 - BETA_TWO**STEP)) + EPSILON)
        + decay_rate * weight
    )
    return (first_new, second_new, direction)


def layout_tables(sizes_row, lengths_row):
    slot_ids = jnp.arange(SLOTS, dtype=jnp.int32)
    seg_ends = jnp.cumsum(sizes_row)
    starts = seg_ends - sizes_row
    segment = jnp.sum((slot_ids[:, None] >= seg_ends[None, :]).astype(jnp.int32), axis=1)
    member = segment[:, None] == jnp.arange(NSEG, dtype=jnp.int32)[None, :]
    offset = jnp.sum(jnp.where(member, starts[None, :], 0), axis=1)
    length_of = jnp.sum(jnp.where(member, lengths_row[None, :], 0), axis=1)
    position = slot_ids - offset
    return (segment, member, position, position < length_of)


def condition(steps_row):
    half_cond = COND // 2
    frequency = jnp.exp(jnp.arange(half_cond, dtype=F32) * (-math.log(10000.0) / half_cond))
    angles = steps_row.astype(F32)[:, None] * frequency[None, :]
    return jax.nn.silu(jnp.concatenate([jnp.cos(angles), jnp.sin(angles)], axis=1))


FORWARD_CALLS = (2, 3, 1)
BACKWARD_CALLS = (1, 2, 3)


def on_device(
    inputs, cotangent, seg_sizes, seq_lengths, timesteps, absorbed,
    qkv_weight, out_weight, up_weight, down_weight, mod_weight,
    qkv_first, out_first, up_first, down_first, mod_first,
    qkv_second, out_second, up_second, down_second, mod_second,
    vectors, vectors_first, vectors_second,
):
    rounds = by_rounds()
    chip = lax.axis_index("fsdp")
    core = lax.axis_index("rep")
    matrices = (qkv_weight, out_weight, up_weight, down_weight, mod_weight)
    qkv_low, out_low, up_low, down_low, mod_low = [matrix.astype(BF) for matrix in matrices]
    vector_low = vectors.astype(BF)
    if rounds:
        order = jnp.concatenate([jnp.asarray(ORIGIN)[core, chip], jnp.asarray(ORIGIN)[1 - core, chip]])
        places = jnp.asarray(PLACES)[core, chip]
        side = core[None].astype(jnp.int32)
        unit_first = pack_first(qkv_low, mod_low.T, vector_low[None], core)[0]
        unit_second = pack_second(out_low, up_low, down_low, core)[0]
        second_one = unit_second[None]
        first_back = [along_z(unit_first, back) for back in range(1, 4)]
        second_near = near_of(second_one)
        first_column = jnp.stack([unit_first] + first_back)
        first_near = near_of(first_column)
        second_from = hold_back(unit_second, first_column)
        second_back = [along_z(second_from, back) for back in range(1, 4)]
        first_near, second_near = lax.optimization_barrier((first_near, second_near))
        first_far = [along_plane(first_near[0][start : start + 2], 1) for start in (0, 2)]
        units_first, second_back = lax.optimization_barrier(([first_column] + first_near + first_far, second_back))
        units_first = units_first + swapped(units_first)
    else:
        order = jnp.concatenate([jnp.arange(UNITS, dtype=jnp.int32)] * 2)
        places = jnp.asarray(PLACES)[0, 0]
        side = jnp.zeros((1,), jnp.int32)
        qkv_all, mod_all, vector_all = gather_plain((qkv_low, mod_low, vector_low), (0, 1, 0))
        out_all, up_all, down_all = gather_plain((out_low, up_low, down_low), (0, 0, 0))
        units_first = virtual_units(lambda s: pack_first(qkv_all, mod_all.T, vector_all.reshape(UNITS, -1), s))
        units_second = virtual_units(lambda s: pack_second(out_all, up_all, down_all, s), True)

    segment, member, position, valid_slot = layout_tables(seg_sizes[0], seq_lengths[0])
    tiles = segment.reshape(BLOCKS, TILE)[:, 0]
    member_tile = member.reshape(BLOCKS, TILE, NSEG)[:, 0].astype(F32)
    condition_low = condition(timesteps[0]).astype(BF)
    cos, sin, feature_query, feature_key = attention_tables(segment, position, valid_slot)
    weight_mask = (absorbed[0] * valid_slot.astype(jnp.int32)).astype(F32).reshape(BLOCKS, TILE)
    row_in, row_cot = inputs[0], cotangent[0]

    mixed, first_low, qkv_full, modulation, flat = first_part(
        units_first, order, side, tiles, row_in, condition_low, cos, sin
    )
    forward, first_pair = None, 0
    if rounds:
        second_rest = jnp.stack(second_back)
        second_rest_near = near_of(second_rest)
    for number, count in enumerate(FORWARD_CALLS):
        if rounds and number == 1:
            second_rest_far = far_from(hold_back(second_rest_near, forward))
            second_own = [second_one, second_rest, second_near[0], second_rest_near[0], second_near[1], second_rest_near[1]]
            second_own.append(far_from(second_near))
            second_other = swapped(hold_back(second_own[:-1], forward)) + swapped(second_own[-1:])
        if rounds and number == 2:
            forward, second_rest_far = hold_back((forward, second_rest_far), second_other)
        forward = attention_forward(mixed, feature_query, feature_key, forward, first_pair, count)
        first_pair += count
    if rounds:
        units_second = second_own + [second_rest_far] + second_other + [swap_core(second_rest_far)]
    attended_low, feature = forward
    out_hidden, grad_middle, grad_attended, sums, bias_sums, mine_later, give_later = middle_part(
        units_second, order, side, tiles, attended_low, row_in, row_cot, weight_mask, modulation, flat
    )
    state = [None]

    def backward_part(number, came):
        grad_here = grad_attended if came is None else hold_back(grad_attended, came)
        state[0] = attention_backward(
            mixed, feature, feature_key, grad_here, attended_low, cos, sin, state[0],
            sum(BACKWARD_CALLS[:number]), BACKWARD_CALLS[number],
        )
        return state[0]

    def qkv_end(sooner=None):
        follows = state[0] if sooner is None else hold_back(state[0], sooner)
        return qkv_grads(side, first_low, follows)

    def row_end(sooner=None):
        follows = state[0] if sooner is None else hold_back(state[0], sooner)
        return last_part(
            places, tiles, member_tile, follows, qkv_full, row_in, grad_middle, modulation, flat, condition_low,
            sums, bias_sums,
        )

    vector_arrays = (vectors, vectors_first, vectors_second)
    of_qkv, of_out = (qkv_weight, qkv_first, qkv_second), (out_weight, out_first, out_second)
    of_up, of_down = (up_weight, up_first, up_second), (down_weight, down_first, down_second)
    of_mod = (mod_weight, mod_first, mod_second)
    if rounds:
        later = Scatter(mine_later, give_later, places)
        backward_part(0, None)
        sent = later.send_far_alone(state[0])
        backward_part(1, sent)
        sent = later.send_neighbours(state[0])
        backward_part(2, sent)
        qkv_parts = qkv_end(later.arrived)
        sooner = Scatter(*qkv_parts, places)
        sent = later.send_column(qkv_parts)
        sent = sooner.send_far(sent)
        grad_in, *small_parts = row_end(sent)
        small = SmallScatter(*small_parts, places)
        sent = sooner.send_first((grad_in, later.came[0], later.came[2]))
        sent = sooner.send_column(sent)
        sent = small.send_first((sent, later.came[1], sooner.came[0]))
        sent = small.send_column((sent, sooner.came))
        later_sums = later.finish(sent)
        (out_new, up_new, down_new), later_table = update_moments(
            update_later_kernel, side, later_sums, of_out + of_up + of_down
        )
        qkv_sums = sooner.finish(later_table)
        small_sums = small.finish(later_table)
        (qkv_new, mod_new), sooner_table = update_moments(
            update_sooner_kernel, side, qkv_sums + (small_sums,), of_qkv + tuple(part.T for part in of_mod)
        )
        results = [qkv_new, out_new, up_new, down_new, mod_new]
        *renewed, norm_roots = renew(
            sum_small(later_table + sooner_table),
            [*matrices[:4], mod_weight.T],
            [record[2] for record in results],
        )
        renewed[4] = renewed[4].T
        results[4] = [part.T for part in mod_new]
        grad_vectors = small_sums[:5, 6 * COND :].reshape(-1)[:VECTOR_PART]
    else:
        for number in range(3):
            backward_part(number, None)
        grad_out, grad_up, grad_down = reduce_plain(unpack_second((mine_later, give_later)), (0, 0, 0))
        grad_in, *small_parts = row_end()
        grad_qkv, grad_mod, grad_vectors = reduce_plain(
            (unpack_qkv(qkv_end()), *unpack_small(*small_parts)), (0, 1, 0)
        )
        grads = (grad_qkv, grad_out, grad_up, grad_down, grad_mod)
        olds = (of_qkv, of_out, of_up, of_down, of_mod)
        results = [adam_direction(*old, grad, DECAY_RATE) for old, grad in zip(olds, grads)]
        squares = [
            jnp.stack([jnp.sum(values[number] * values[number]) for number in range(5)])
            for values in (matrices, [record[2] for record in results])
        ]
        norm_roots = jnp.sqrt(lax.psum(jnp.stack(squares), "fsdp"))
        trust = norm_roots[0] / (norm_roots[1] + EPSILON)
        renewed = [matrices[number] - MATRIX_RATE * trust[number] * results[number][2] for number in range(5)]
    vector_record = adam_direction(*vector_arrays, grad_vectors, 0.0)
    return (
        out_hidden[None],
        grad_in[None],
        *renewed,
        *[record[0] for record in results],
        *[record[1] for record in results],
        vectors - VECTOR_RATE * vector_record[2],
        vector_record[0],
        vector_record[1],
        norm_roots,
    )


def solution(mesh):
    rows = P(("rep", "fsdp"))
    matrix, turned, vector = P("fsdp", None), P(None, "fsdp"), P("fsdp")
    five = (matrix, matrix, matrix, matrix, turned)
    return jax.shard_map(
        on_device,
        mesh=mesh,
        in_specs=(rows,) * 6 + five * 3 + (vector,) * 3,
        out_specs=(rows, rows) + five * 3 + (vector,) * 3 + (P(),),
        check_vma=False,
    )
```

```python
import functools
import math

import jax
import jax.numpy as jnp
import numpy as np
from jax import lax
from jax.experimental import pallas as pl
from jax.experimental.pallas import tpu as pltpu
from jax.sharding import PartitionSpec as P

D = 768
HEADS = 12
HDIM = 64
FF = 3072
COND = 128
SLOTS = 1024
NSEG = 8
STEP = 10
TILE = 128
BLOCKS = SLOTS // TILE

BETA_ONE = 0.9
BETA_TWO = 0.999
EPSILON = 1e-06
DECAY_RATE = 0.01
MATRIX_RATE = 0.3
VECTOR_RATE = 1.0

PAIR = 128
NT = (((1,), (1,)), ((), ()))
NN = (((1,), (0,)), ((), ()))
TN = (((0,), (0,)), ((), ()))
BF = jnp.bfloat16
F32 = jnp.float32


def mm(a, b, dims=NN):
    return lax.dot_general(a, b, dims, preferred_element_type=F32)


def in_parts(values):
    high = values.astype(BF)
    rest = values - high.astype(F32)
    middle = rest.astype(BF)
    return jnp.concatenate([high, middle, (rest - middle.astype(F32)).astype(BF)], axis=0)


def swap_halves(v):
    lane = lax.broadcasted_iota(jnp.int32, v.shape, 1)
    return jnp.where(lane % 64 < 32, pltpu.roll(v, PAIR - 32, 1), pltpu.roll(v, 32, 1))


def attention_forward_kernel(block, q_ref, k_ref, v_ref, fq_ref, fk_ref, *refs):
    o_ref, fo_ref, ka, kb, va, vb = refs[-6:]
    slots = q_ref.shape[0]
    low_all = lax.broadcasted_iota(jnp.int32, (slots, PAIR), 1) < 64
    k_low = k_ref[...]
    v_low = v_ref[...]
    fk = fk_ref[...]
    one = jnp.ones((slots, PAIR), BF)
    ka[...] = jnp.where(low_all, k_low, fk)
    kb[...] = jnp.where(low_all, fk, k_low)
    va[...] = jnp.where(low_all, v_low, one)
    vb[...] = jnp.where(low_all, one, v_low)
    lane = lax.broadcasted_iota(jnp.int32, (block, PAIR), 1)
    low = lane < 64
    spot = lane % 64

    def step(i, carry):
        at = pl.ds(pl.multiple_of(i * block, block), block)
        q = q_ref[at, :]
        fq = fq_ref[at, :]
        sa = mm(jnp.where(low, q, fq), ka[...], NT)
        sb = mm(jnp.where(low, fq, q), kb[...], NT)
        ma = jnp.max(sa, axis=1, keepdims=True)
        mb = jnp.max(sb, axis=1, keepdims=True)
        pa = jnp.exp(sa - ma).astype(BF)
        pb = jnp.exp(sb - mb).astype(BF)
        oa = mm(pa, va[...])
        ob = mm(pb, vb[...])
        o = jnp.where(low, oa / pltpu.roll(oa, 64, 1), ob / pltpu.roll(ob, 64, 1))
        o_ref[at, :] = o.astype(o_ref.dtype)
        neg = jnp.where(low, -(mb + jnp.log(ob)), -(ma + jnp.log(oa)))
        hi = neg.astype(BF)
        rest = neg - hi.astype(F32)
        mid = rest.astype(BF)
        last = (rest - mid.astype(F32)).astype(BF)
        fo_ref[at, :] = jnp.where(spot == 8, hi, jnp.where(spot == 9, mid, jnp.where(spot == 10, last, fq)))
        return carry

    lax.fori_loop(0, slots // block, step, 0)


def attention_forward(qkv, fq, fk, before, first, count, block=1024):
    slots, width = qkv.shape
    pairs = width // 3 // PAIR
    blk = lambda off: pl.BlockSpec((slots, PAIR), lambda p: (0, off + p))
    fixed = pl.BlockSpec((slots, PAIR), lambda p: (0, 0))
    anywhere = pl.BlockSpec(memory_space=pl.ANY)
    shape = jax.ShapeDtypeStruct((slots, pairs * PAIR), BF)
    extra = () if before is None else before
    elements = 2 * count * slots * slots
    return pl.pallas_call(
        functools.partial(attention_forward_kernel, block),
        grid=(count,),
        in_specs=[blk(first), blk(pairs + first), blk(2 * pairs + first), fixed, fixed] + [anywhere] * len(extra),
        out_specs=[blk(first)] * 2,
        out_shape=[shape, shape],
        scratch_shapes=[pltpu.VMEM((slots, PAIR), BF)] * 4,
        input_output_aliases={5: 0, 6: 1} if extra else {},
        cost_estimate=pl.CostEstimate(flops=elements * 3000, bytes_accessed=10 * slots * count * PAIR, transcendentals=elements),
        compiler_params=pltpu.CompilerParams(vmem_limit_bytes=62 * 2**20),
    )(qkv, qkv, qkv, fq, fk, *extra)


def attention_backward_kernel(block, q_ref, k_ref, v_ref, fo_ref, fk_ref, do_ref, o_ref, cos_ref, sin_ref, *refs):
    g_ref, ka, kb, va, vb, kt, dka, dkb, dva, dvb = refs[-10:]
    slots = q_ref.shape[0]
    lane_all = lax.broadcasted_iota(jnp.int32, (slots, PAIR), 1)
    low_all = lane_all < 64
    fk = fk_ref[...]
    k_low = k_ref[...]
    v_low = v_ref[...]
    one = jnp.where(lane_all % 64 < 2, 1.0, 0.0).astype(BF)
    ka[...] = jnp.where(low_all, k_low, fk)
    kb[...] = jnp.where(low_all, fk, k_low)
    va[...] = jnp.where(low_all, v_low, one)
    vb[...] = jnp.where(low_all, one, v_low)
    kt[...] = k_low.T
    dka[...] = jnp.zeros_like(dka)
    dkb[...] = jnp.zeros_like(dkb)
    dva[...] = jnp.zeros_like(dva)
    dvb[...] = jnp.zeros_like(dvb)
    lane = lax.broadcasted_iota(jnp.int32, (block, PAIR), 1)
    low = lane < 64
    spot = lane % 64
    top = lax.broadcasted_iota(jnp.int32, (PAIR, block), 0) < 64

    def step(i, carry):
        at = pl.ds(pl.multiple_of(i * block, block), block)
        q = q_ref[at, :]
        fq = fo_ref[at, :]
        do = do_ref[at, :]
        both = do.astype(F32) * o_ref[at, :].astype(F32)
        da = jnp.sum(jnp.where(low, both, 0.0), axis=1, keepdims=True)
        db = jnp.sum(jnp.where(low, 0.0, both), axis=1, keepdims=True)
        neg = jnp.where(low, -db, -da)
        hi = neg.astype(BF)
        rest = (neg - hi.astype(F32)).astype(BF)
        fd = jnp.where(spot == 0, hi, jnp.where(spot == 1, rest, jnp.zeros_like(hi)))
        sa = mm(ka[...], jnp.where(low, q, fq), NT)
        sb = mm(kb[...], jnp.where(low, fq, q), NT)
        ea = mm(va[...], jnp.where(low, do, fd), NT)
        eb = mm(vb[...], jnp.where(low, fd, do), NT)
        pa = jnp.exp(sa)
        pb = jnp.exp(sb)
        dsa = (pa * ea).astype(BF)
        dsb = (pb * eb).astype(BF)
        dva[...] += mm(pa.astype(BF), do)
        dvb[...] += mm(pb.astype(BF), do)
        dka[...] += mm(dsa, q)
        dkb[...] += mm(dsb, q)
        dqt = jnp.where(top, mm(kt[...], dsa), mm(kt[...], dsb))
        dq = dqt.T * 0.125
        g_ref[0, at, :] = (dq * cos_ref[at, :] - swap_halves(dq) * sin_ref[at, :]).astype(BF)
        return carry

    lax.fori_loop(0, slots // block, step, 0)
    dk = jnp.where(low_all, dka[...], dkb[...])
    g_ref[1] = (dk * cos_ref[...] - swap_halves(dk) * sin_ref[...]).astype(BF)
    g_ref[2] = jnp.where(low_all, dva[...], dvb[...]).astype(BF)


def attention_backward(qkv, fo, fk, do, o, cos, sin, before, first, count, block=512):
    slots, width = qkv.shape
    pairs = width // 3 // PAIR
    blk = lambda off: pl.BlockSpec((slots, PAIR), lambda p: (0, off + p))
    fixed = pl.BlockSpec((slots, PAIR), lambda p: (0, 0))
    extra = () if before is None else (before,)
    elements = 2 * count * slots * slots
    return pl.pallas_call(
        functools.partial(attention_backward_kernel, block),
        grid=(count,),
        in_specs=[blk(first), blk(pairs + first), blk(2 * pairs + first), blk(first), fixed, blk(first), blk(first),
                  fixed, fixed] + [pl.BlockSpec(memory_space=pl.ANY)] * len(extra),
        out_specs=pl.BlockSpec((3, slots, PAIR), lambda p: (0, 0, first + p)),
        out_shape=jax.ShapeDtypeStruct((3, slots, pairs * PAIR), BF),
        scratch_shapes=[pltpu.VMEM((slots, PAIR), BF)] * 4 + [pltpu.VMEM((PAIR, slots), BF)]
        + [pltpu.VMEM((slots, PAIR), F32)] * 4,
        input_output_aliases={9: 0} if extra else {},
        cost_estimate=pl.CostEstimate(flops=elements * 2000, bytes_accessed=20 * slots * count * PAIR, transcendentals=elements),
        compiler_params=pltpu.CompilerParams(vmem_limit_bytes=62 * 2**20),
    )(qkv, qkv, qkv, fo, fk, do, o, cos, sin, *extra)


def attention_tables(segment, position, valid_slot):
    inverse = jnp.exp(jnp.arange(32, dtype=F32) * (-math.log(10000.0) / 32))
    angles = position.astype(F32)[:, None] * inverse[None, :]
    c, s = jnp.cos(angles), jnp.sin(angles)
    cos = jnp.concatenate([c, c, c, c], axis=1)
    sin = jnp.concatenate([-s, s, -s, s], axis=1)
    spot = jnp.arange(PAIR) % 64
    same = segment[:, None] == spot[None, :]
    fq = same.astype(BF)
    fk = jnp.where((spot < 8)[None, :], jnp.where(same & valid_slot[:, None], 0.0, -1e30),
                   jnp.where((spot < 11)[None, :], 1.0, 0.0)).astype(BF)
    return cos, sin, fq, fk


UNITS = 16
QKV_HALF = 3 * D // 2
SMALL_WIDE = 6 * COND + 128
FIRST_WIDE = QKV_HALF + 3 * COND + 128
UP_AT, DOWN_AT, OUT_AT, SECOND_WIDE = 0, FF // 2, FF // 2 + 2 * D, FF // 2 + 2 * D + D // 2
VECTOR_PART = (9 * D + FF) // UNITS
FLAT_ROWS = 80
HBM = pltpu.HBM
SMALL_VMEM = pl.BlockSpec(memory_space=pltpu.SMEM)


def whole(shape):
    return pl.BlockSpec(shape, lambda *_: (0,) * len(shape), pipeline_mode=pl.Buffered(1))


def line(flat_ref, start, count):
    return jnp.concatenate([flat_ref[start + i : start + i + 1, :] for i in range(count)], axis=1)


def unit_of(units, half, place):
    if len(units) == 10:
        kind, back = place // 4, place % 4
        return units[half * 5 + (kind if kind < 3 else 3 + back // 2)].at[back if kind < 3 else back % 2]
    return units[half * 8 + place // 4 * 2 + min(place % 4, 1)].at[max(place % 4 - 1, 0)]


def unit_copies(units, order, core, sems, plan, first_sem):
    copies = []
    for half in range(2):
        side = core if half == 0 else 1 - core
        for place in range(UNITS):
            origin = order[half * UNITS + place]
            for target, rows, column, width, by_origin, by_side, row, column_side, both in plan:
                if half == 1 and not both:
                    continue
                to_row = pl.multiple_of(origin * by_origin + side * by_side + row, 16)
                to_column = pl.multiple_of(side * column_side, 128) if column_side else 0
                copies.append(
                    pltpu.make_async_copy(
                        unit_of(units, half, place).at[pl.ds(0, rows), pl.ds(column, width)],
                        target.at[pl.ds(to_row, rows), pl.ds(to_column, width)],
                        sems.at[first_sem + len(copies)],
                    )
                )
    return copies


def layer_norm(values):
    average = jnp.mean(values, axis=-1, keepdims=True)
    centered = values - average
    root = lax.rsqrt(jnp.mean(centered * centered, axis=-1, keepdims=True) + 1e-05)
    return (centered * root, root)


def layer_norm_back(grad, normal, root, gain):
    scaled = grad * gain
    inner = jnp.mean(scaled * normal, axis=-1, keepdims=True)
    return root * (scaled - jnp.mean(scaled, axis=-1, keepdims=True) - normal * inner)


def first_kernel(rows, order_ref, core_ref, tiles_ref, *refs):
    units = refs[:10]
    x_ref, cond_ref, cos_ref, sin_ref, qkv_ref, first_ref, w_ref, mod_ref, flat_ref, modt, vecs, sems = refs[10:]
    step = pl.program_id(0)

    small = unit_copies(units, order_ref, core_ref[0], sems, (
        (vecs, 16, QKV_HALF + 3 * COND, 128, 16, 0, 0, 0, False),
        (modt, 48, QKV_HALF, 128, 288, 144, 0, 0, True),
        (modt, 48, QKV_HALF + 128, 128, 288, 144, 48, 0, True),
        (modt, 48, QKV_HALF + 256, 128, 288, 144, 96, 0, True),
    ), 0)
    large = unit_copies(units, order_ref, core_ref[0], sems, (
        (w_ref, 48, 0, QKV_HALF, 48, 0, 0, QKV_HALF, True),
    ), len(small))

    @pl.when(step == 0)
    def _():
        for copy in small + large:
            copy.start()
        for copy in small:
            copy.wait()
        flat_ref[...] = jnp.zeros_like(flat_ref)
        lane = lax.broadcasted_iota(jnp.int32, (8, 128), 1)
        for part in range(UNITS):
            row, turn = divmod(VECTOR_PART * part, 128)
            piece = vecs[16 * part : 16 * part + 16, :].astype(F32)[:8]
            if turn:
                piece = pltpu.roll(piece, turn, 1)
                flat_ref[row + 1 : row + 6, :] += jnp.where(lane < turn, piece, 0.0)[:5]
                piece = jnp.where(lane >= turn, piece, 0.0)
            flat_ref[row : row + 5, :] += piece[:5]
        mod_ref[...] = mm(cond_ref[...], modt[...], NT) + line(flat_ref, (3 * D + FF) // 128, 6 * D // 128)

    gain = line(flat_ref, 0, D // 128)
    for part in range(rows // TILE):
        at = pl.ds(part * TILE, TILE)
        segment = tiles_ref[step * (rows // TILE) + part]
        normal, _ = layer_norm(x_ref[at, :].astype(F32))
        shift = mod_ref[pl.ds(segment, 1), 0:D]
        scale = mod_ref[pl.ds(segment, 1), D : 2 * D]
        first_ref[at, :] = (normal * (gain * (1.0 + scale)) + shift).astype(BF)
    first = first_ref[...]
    cos, sin = cos_ref[...], sin_ref[...]

    @pl.when(step == 0)
    def _():
        for copy in large:
            copy.wait()

    for kind in range(3):
        mixed = mm(first, w_ref[:, kind * D : (kind + 1) * D])
        if kind < 2:
            for pair in range(D // PAIR):
                part = mixed[:, pair * PAIR : (pair + 1) * PAIR]
                turned = part * cos + swap_halves(part) * sin
                if kind == 0:
                    turned = turned * HDIM ** (-0.5)
                qkv_ref[:, kind * D + pair * PAIR : kind * D + (pair + 1) * PAIR] = turned.astype(BF)
        else:
            qkv_ref[:, 2 * D :] = mixed.astype(BF)


def first_part(units, order, core, tiles, x, cond, cos, sin, rows=256):
    count = UNITS * (1 + 2 * 3 + 2)
    row = lambda width: pl.BlockSpec((rows, width), lambda i: (i, 0))
    shape = lambda s, t: jax.ShapeDtypeStruct(s, t)
    return pl.pallas_call(
        functools.partial(first_kernel, rows),
        grid=(SLOTS // rows,),
        in_specs=[SMALL_VMEM] * 3 + [pl.BlockSpec(memory_space=HBM)] * 10
        + [row(D), whole((NSEG, COND)), row(PAIR), row(PAIR)],
        out_specs=[row(3 * D), row(D), whole((D, 3 * D)), whole((NSEG, 6 * D)), whole((FLAT_ROWS, 128))],
        out_shape=[shape((SLOTS, 3 * D), BF), shape((SLOTS, D), BF), shape((D, 3 * D), BF),
                   shape((NSEG, 6 * D), F32), shape((FLAT_ROWS, 128), F32)],
        scratch_shapes=[pltpu.VMEM((6 * D, COND), BF), pltpu.VMEM((16 * UNITS, 128), BF), pltpu.SemaphoreType.DMA((count,))],
        cost_estimate=pl.CostEstimate(flops=2 * SLOTS * D * 3 * D, bytes_accessed=20 * 2**20, transcendentals=SLOTS),
        compiler_params=pltpu.CompilerParams(vmem_limit_bytes=56 * 2**20),
    )(order, core, tiles, *units, x, cond, cos, sin)


def middle_kernel(rows, order_ref, core_ref, tiles_ref, *refs):
    units = refs[:16]
    (att_all, x_ref, cot_ref, mask_ref, mod_ref, flat_ref,
     out_ref, gmid_ref, gatt_ref, sums_ref, bias_ref, mine_ref, give_ref,
     wo, wu, wd, hidden_s, second_s, grad_mlp_s, grad_up_s, grad_branch_s, branch_s, buffer, sems, out_sems) = refs[16:]
    step = pl.program_id(0)
    core = core_ref[0]

    @pl.when(step < SLOTS // rows)
    def _():
        middle_rows(
            rows, step, core, order_ref, tiles_ref, units, att_all, x_ref, cot_ref, mask_ref, mod_ref, flat_ref,
            out_ref, gmid_ref, gatt_ref, sums_ref, bias_ref,
            wo, wu, wd, hidden_s, second_s, grad_mlp_s, grad_up_s, grad_branch_s, branch_s, sems,
        )

    @pl.when(step >= SLOTS // rows)
    def _():
        later_grads(
            step - SLOTS // rows, core, hidden_s, second_s, att_all, grad_mlp_s, grad_up_s, grad_branch_s,
            mine_ref, give_ref, buffer, out_sems,
        )


def middle_rows(
    rows, step, core, order_ref, tiles_ref, units, att_all, x_ref, cot_ref, mask_ref, mod_ref, flat_ref,
    out_ref, gmid_ref, gatt_ref, sums_ref, bias_ref,
    wo, wu, wd, hidden_s, second_s, grad_mlp_s, grad_up_s, grad_branch_s, branch_s, sems,
):
    chunks = FF // D
    here = pl.ds(pl.multiple_of(step * rows, rows), rows)

    def part_of(part):
        return pl.ds(pl.multiple_of(step * rows + part * TILE, TILE), TILE)

    tiles = rows // TILE
    each = 2 * UNITS
    copies = [
        unit_copies(units, order_ref, core, sems, ((wo, 48, OUT_AT, D // 2, 48, 0, 0, D // 2, True),), 0),
        unit_copies(units, order_ref, core, sems, ((wu, 48, UP_AT, FF // 2, 48, 0, 0, FF // 2, True),), each),
        unit_copies(units, order_ref, core, sems, (
            (wd, 48, DOWN_AT, D, 192, 96, 0, 0, True),
            (wd, 48, DOWN_AT + D, D, 192, 96, 48, 0, True),
        ), 2 * each),
    ]

    @pl.when(step == 0)
    def _():
        for group in copies:
            for copy in group:
                copy.start()
        bias_ref[...] = jnp.zeros_like(bias_ref)
        for copy in copies[0]:
            copy.wait()

    def table(part, kind):
        return mod_ref[pl.ds(tiles_ref[step * tiles + part], 1), kind * D : (kind + 1) * D]

    def mask_column(part):
        row = mask_ref[pl.ds(step * tiles + part, 1), :]
        return jnp.broadcast_to(row, (TILE, TILE)).T[:, :1]

    branch_s[...] = mm(att_all[here, :], wo[...])
    gain = line(flat_ref, D // 128, D // 128)
    for part in range(tiles):
        at = pl.ds(part * TILE, TILE)
        middle = x_ref[at, :].astype(F32) + table(part, 2) * branch_s[at, :]
        gmid_ref[at, :] = middle
        normal, _ = layer_norm(middle)
        second_s[part_of(part), :] = (normal * (gain * (1.0 + table(part, 4))) + table(part, 3)).astype(BF)

    @pl.when(step == 0)
    def _():
        for group in copies[1:]:
            for copy in group:
                copy.wait()

    for part in range(tiles):
        at = pl.ds(part * TILE, TILE)
        grad_mlp = (cot_ref[at, :].astype(F32) * mask_column(part) * table(part, 5)).astype(BF)
        grad_mlp_s[part_of(part), :] = grad_mlp
        bias_ref[0:1, FF:] += jnp.sum(grad_mlp.astype(F32), axis=0, keepdims=True)
    second = second_s[here, :]
    grad_mlp = grad_mlp_s[here, :]
    factor = math.sqrt(2.0 / math.pi)
    feed, grad_second = None, None
    for j in range(chunks):
        at = pl.ds(j * D, D)
        u = mm(second, wu[:, at]) + line(flat_ref, 2 * D // 128 + j * (D // 128), D // 128)
        grad_hidden = mm(grad_mlp, wd[at, :], NT)
        square = u * u
        bent = jnp.tanh(u * (factor + (factor * 0.044715) * square))
        half = 0.5 * u
        bow = half * bent
        hidden = (half + bow).astype(BF)
        slope = (0.5 + 0.5 * bent) + (half - bow * bent) * (factor + (3 * factor * 0.044715) * square)
        grad_up = (grad_hidden * slope).astype(BF)
        hidden_s[here, at] = hidden
        grad_up_s[here, at] = grad_up
        bias_ref[0:1, at] += jnp.sum(grad_up.astype(F32), axis=0, keepdims=True)
        share, grad_share = mm(hidden, wd[at, :]), mm(grad_up, wu[:, at], NT)
        feed = share if feed is None else feed + share
        grad_second = grad_share if grad_second is None else grad_second + grad_share
    bias_down = line(flat_ref, (2 * D + FF) // 128, D // 128)
    for part in range(tiles):
        at = pl.ds(part * TILE, TILE)
        feed_out = feed[part * TILE : (part + 1) * TILE] + bias_down
        out_ref[at, :] = (gmid_ref[at, :] + table(part, 5) * feed_out).astype(BF)
        grad_out = cot_ref[at, :].astype(F32) * mask_column(part)
        sums_ref[part, 3:4, :] = jnp.sum(grad_out * feed_out, axis=0, keepdims=True)
    for part in range(tiles):
        at = pl.ds(part * TILE, TILE)
        normal, root = layer_norm(gmid_ref[at, :])
        grad = grad_second[part * TILE : (part + 1) * TILE]
        sums_ref[part, 1:2, :] = jnp.sum(grad, axis=0, keepdims=True)
        sums_ref[part, 2:3, :] = jnp.sum(grad * normal, axis=0, keepdims=True)
        grad_middle = cot_ref[at, :].astype(F32) * mask_column(part) + layer_norm_back(
            grad, normal, root, gain * (1.0 + table(part, 4))
        )
        gmid_ref[at, :] = grad_middle
        sums_ref[part, 0:1, :] = jnp.sum(grad_middle * branch_s[at, :], axis=0, keepdims=True)
        grad_branch_s[part_of(part), :] = (grad_middle * table(part, 2)).astype(BF)
    gatt_ref[...] = mm(grad_branch_s[here, :], wo[...], NT).astype(BF)


def later_grads(step, core, hidden_s, second_s, att_all, grad_mlp_s, grad_up_s, grad_branch_s, mine_ref, give_ref, buffer, sems):
    down_steps = FF // D
    steps = 2 * down_steps + 1
    slot = step % 2

    def wait(at_slot):
        for number in range(16):
            pltpu.make_async_copy(buffer.at[at_slot, number], buffer.at[at_slot, number], sems.at[at_slot, number]).wait()

    def send(source, side, place, number):
        for ref, wanted in ((mine_ref, 0), (give_ref, 1)):
            @pl.when((core ^ side) == wanted)
            def _():
                pltpu.make_async_copy(source, ref.at[place], sems.at[slot, number]).start()

    def keep(left, right):
        buffer[slot] = mm(left, right, TN).astype(BF).reshape(16, 48, D)

    @pl.when(step >= 2)
    def _():
        wait(slot)

    @pl.when(step < down_steps)
    def _():
        keep(hidden_s[:, pl.ds(pl.multiple_of(step * D, D), D)], grad_mlp_s[...])
        for number in range(16):
            local, side, block = number // 4, (number // 2) % 2, number % 2
            send(buffer.at[slot, number], side, (4 * step + local, pl.ds(0, 48), pl.ds(DOWN_AT + block * D, D)), number)

    @pl.when((step >= down_steps) & (step < steps - 1))
    def _():
        keep(second_s[...], grad_up_s[:, pl.ds(pl.multiple_of((step - down_steps) * D, D), D)])

    for j in range(down_steps):
        @pl.when(step == down_steps + j)
        def _():
            for number in range(16):
                send(buffer.at[slot, number], j // 2, (number, pl.ds(0, 48), pl.ds(UP_AT + (j % 2) * D, D)), number)

    @pl.when(step == steps - 1)
    def _():
        keep(att_all[...], grad_branch_s[...])
        for number in range(16):
            for side in range(2):
                source = buffer.at[slot, number, pl.ds(0, 48), pl.ds(side * (D // 2), D // 2)]
                send(source, side, (number, pl.ds(0, 48), pl.ds(OUT_AT, D // 2)), number)
        wait(1 - slot)
        wait(slot)


def middle_part(units, order, core, tiles, att, x, cot, mask, modulation, flat, rows=512):
    last = SLOTS // rows - 1
    row = lambda width: pl.BlockSpec((rows, width), lambda i: (jnp.minimum(i, last), 0))
    shape = lambda s, t: jax.ShapeDtypeStruct(s, t)
    units_shape = shape((UNITS, 48, SECOND_WIDE), BF)
    kept = lambda width: pltpu.VMEM((SLOTS, width), BF)
    return pl.pallas_call(
        functools.partial(middle_kernel, rows),
        grid=(SLOTS // rows + 2 * (FF // D) + 1,),
        in_specs=[SMALL_VMEM] * 3 + [pl.BlockSpec(memory_space=HBM)] * 16
        + [whole((SLOTS, D)), row(D), row(D), whole((BLOCKS, TILE)), whole((NSEG, 6 * D)), whole((FLAT_ROWS, 128))],
        out_specs=[row(D), row(D), row(D),
                   pl.BlockSpec((rows // TILE, 8, D), lambda i: (jnp.minimum(i, last), 0, 0)), whole((8, FF + D))]
        + [pl.BlockSpec(memory_space=HBM)] * 2,
        out_shape=[shape((SLOTS, D), BF), shape((SLOTS, D), F32), shape((SLOTS, D), BF), shape((BLOCKS, 8, D), F32),
                   shape((8, FF + D), F32), units_shape, units_shape],
        scratch_shapes=[pltpu.VMEM((D, D), BF), pltpu.VMEM((D, FF), BF), pltpu.VMEM((FF, D), BF),
                        kept(FF), kept(D), kept(D), kept(FF), kept(D),
                        pltpu.VMEM((rows, D), F32), pltpu.VMEM((2, 16, 48, D), BF),
                        pltpu.SemaphoreType.DMA((8 * UNITS,)), pltpu.SemaphoreType.DMA((2, 16))],
        cost_estimate=pl.CostEstimate(flops=6 * SLOTS * D * (D + 2 * FF), bytes_accessed=50 * 2**20, transcendentals=SLOTS * FF),
        compiler_params=pltpu.CompilerParams(vmem_limit_bytes=63 * 2**20),
    )(order, core, tiles, *units, att, x, cot, mask, modulation, flat)


def qkv_grads_kernel(core_ref, first_ref, g_ref, mine_ref, give_ref, units, sems):
    step = pl.program_id(0)
    core = core_ref[0]
    product = mm(first_ref[...], g_ref[0], TN).astype(BF).reshape(UNITS, 48, D)

    @pl.when(step == 0)
    def _():
        units[0, :, :, 0:D] = product

    @pl.when(step == 1)
    def _():
        units[0, :, :, D:] = product[:, :, : D // 2]
        units[1, :, :, 0 : D // 2] = product[:, :, D // 2 :]

    @pl.when(step == 2)
    def _():
        units[1, :, :, D // 2 :] = product
        copies = [
            pltpu.make_async_copy(units.at[core], mine_ref, sems.at[0]),
            pltpu.make_async_copy(units.at[1 - core], give_ref, sems.at[1]),
        ]
        for copy in copies:
            copy.start()
        for copy in copies:
            copy.wait()


def qkv_grads(core, first, g):
    shape = jax.ShapeDtypeStruct((UNITS, 48, QKV_HALF), BF)
    return pl.pallas_call(
        qkv_grads_kernel,
        grid=(3,),
        in_specs=[SMALL_VMEM, whole((SLOTS, D)), pl.BlockSpec((1, SLOTS, D), lambda i: (i, 0, 0))],
        out_specs=[pl.BlockSpec(memory_space=HBM)] * 2,
        out_shape=[shape, shape],
        scratch_shapes=[pltpu.VMEM((2, UNITS, 48, QKV_HALF), BF), pltpu.SemaphoreType.DMA((2,))],
        cost_estimate=pl.CostEstimate(flops=SLOTS * D * D, bytes_accessed=2**20, transcendentals=0),
        compiler_params=pltpu.CompilerParams(vmem_limit_bytes=62 * 2**20),
    )(core, first, g)


def last_kernel(rows, places_ref, tiles_ref, member_ref, g_ref, w_ref, x_ref, gmid_ref, mod_ref, flat_ref, cond_ref,
                sums_in, bias_in, gin_ref, own_ref, first_ref, second_ref, far_ref, sums, units, sems):
    step = pl.program_id(0)
    tiles = rows // TILE
    steps = SLOTS // rows
    gain = line(flat_ref, 0, D // 128)

    grad = None
    for kind in range(3):
        share = mm(g_ref[kind], w_ref[:, kind * D : (kind + 1) * D], NT)
        grad = share if grad is None else grad + share
    for part in range(tiles):
        at = pl.ds(part * TILE, TILE)
        tile = step * tiles + part
        segment = tiles_ref[tile]
        normal, root = layer_norm(x_ref[at, :].astype(F32))
        piece = grad[part * TILE : (part + 1) * TILE]
        scale = mod_ref[pl.ds(segment, 1), D : 2 * D]
        sums[pl.ds(tile, 1), 0:D] = jnp.sum(piece, axis=0, keepdims=True)
        sums[pl.ds(tile, 1), D : 2 * D] = jnp.sum(piece * normal, axis=0, keepdims=True)
        gin_ref[at, :] = gmid_ref[at, :] + layer_norm_back(piece, normal, root, gain * (1.0 + scale))

    @pl.when(step == steps - 1)
    def _():
        gain_two = line(flat_ref, D // 128, D // 128)
        for tile in range(BLOCKS):
            at = pl.ds(tile, 1)
            sums[at, 2 * D : 3 * D] = sums_in[tile, 0:1, :]
            sums[at, 3 * D : 4 * D] = sums_in[tile, 1:2, :]
            sums[at, 4 * D : 5 * D] = sums_in[tile, 2:3, :]
            sums[at, 5 * D : 6 * D] = sums_in[tile, 3:4, :]
        member = member_ref[...].astype(BF)
        scales = [mod_ref[pl.ds(tiles_ref[tile], 1), :] for tile in range(BLOCKS)]
        scale_one = jnp.concatenate([scale[:, D : 2 * D] for scale in scales], axis=0)
        scale_two = jnp.concatenate([scale[:, 4 * D : 5 * D] for scale in scales], axis=0)
        grad_gain_one = jnp.sum(sums[:, D : 2 * D] * (1.0 + scale_one), axis=0, keepdims=True)
        grad_gain_two = jnp.sum(sums[:, 4 * D : 5 * D] * (1.0 + scale_two), axis=0, keepdims=True)
        sums[:, D : 2 * D] = sums[:, D : 2 * D] * gain
        sums[:, 4 * D : 5 * D] = sums[:, 4 * D : 5 * D] * gain_two
        by_segment = mm(jnp.concatenate([member] * 3, axis=0), in_parts(sums[...]), TN)
        grad_mod = mm(in_parts(by_segment), jnp.concatenate([cond_ref[...]] * 3, axis=0), TN).astype(BF).reshape(4, 4, 6, 48, COND)
        for block in range(6):
            units[:, :, :, block * COND : (block + 1) * COND] = grad_mod[:, :, block]
        row = jnp.concatenate(
            [grad_gain_one, grad_gain_two, bias_in[0:1, :], jnp.sum(by_segment, axis=0, keepdims=True)], axis=1
        )
        lane = lax.broadcasted_iota(jnp.int32, (1, 128), 1)
        blank = jnp.zeros((43, 128), F32)
        for part in range(UNITS):
            start = VECTOR_PART * part
            pieces = []
            for number in range(5):
                first_row, turn = divmod(start + 128 * number, 128)
                piece = row[:, first_row * 128 : (first_row + 1) * 128]
                if turn:
                    following = (
                        row[:, (first_row + 1) * 128 : (first_row + 2) * 128]
                        if (first_row + 2) * 128 <= row.shape[1]
                        else jnp.zeros((1, 128), F32)
                    )
                    piece = jnp.where(
                        lane < 128 - turn, pltpu.roll(piece, 128 - turn, 1), pltpu.roll(following, 128 - turn, 1)
                    )
                if number == 4:
                    piece = jnp.where(lane < VECTOR_PART - 512, piece, 0.0)
                pieces.append(piece)
            stack = jnp.concatenate(pieces + [blank], axis=0).astype(BF)
            units[part // 4, part % 4, :, 6 * COND :] = stack
        copies = [
            pltpu.make_async_copy(units.at[:, places_ref[kind]], ref, sems.at[kind])
            for kind, ref in enumerate((own_ref, first_ref, second_ref, far_ref))
        ]
        for copy in copies:
            copy.start()
        for copy in copies:
            copy.wait()


def last_part(places, tiles, member, g, w, x, gmid, modulation, flat, cond, sums, bias, rows=256):
    row = lambda width: pl.BlockSpec((rows, width), lambda i: (i, 0))
    shape = jax.ShapeDtypeStruct((4, 48, SMALL_WIDE), BF)
    return pl.pallas_call(
        functools.partial(last_kernel, rows),
        grid=(SLOTS // rows,),
        in_specs=[SMALL_VMEM, SMALL_VMEM, whole((BLOCKS, NSEG)), pl.BlockSpec((3, rows, D), lambda i: (0, i, 0)), whole((D, 3 * D)),
                  row(D), row(D), whole((NSEG, 6 * D)), whole((FLAT_ROWS, 128)), whole((NSEG, COND)),
                  whole((BLOCKS, 8, D)), whole((8, FF + D))],
        out_specs=[row(D)] + [pl.BlockSpec(memory_space=HBM)] * 4,
        out_shape=[jax.ShapeDtypeStruct((SLOTS, D), F32)] + [shape] * 4,
        scratch_shapes=[pltpu.VMEM((BLOCKS, 6 * D), F32), pltpu.VMEM((4, 4, 48, SMALL_WIDE), BF),
                        pltpu.SemaphoreType.DMA((4,))],
        cost_estimate=pl.CostEstimate(flops=2 * SLOTS * D * 3 * D, bytes_accessed=30 * 2**20, transcendentals=SLOTS),
        compiler_params=pltpu.CompilerParams(vmem_limit_bytes=60 * 2**20),
    )(places, tiles, member, g, w, x, gmid, modulation, flat, cond, sums, bias)


def moments(weight_ref, first_ref, second_ref, gradient, first_out, second_out, direction_out, decay_rate=DECAY_RATE):
    weight = weight_ref[...]
    first_new = BETA_ONE * first_ref[...] + (1.0 - BETA_ONE) * gradient
    second_new = BETA_TWO * second_ref[...] + (1.0 - BETA_TWO) * gradient * gradient
    direction = (
        first_new
        / (1.0 - BETA_ONE**STEP)
        / (jnp.sqrt(second_new / (1.0 - BETA_TWO**STEP)) + EPSILON)
        + decay_rate * weight
    )
    first_out[...] = first_new
    second_out[...] = second_new
    direction_out[...] = direction
    return [jnp.sum(values * values, axis=(0, 1), keepdims=True) for values in (weight, direction)]


def squares_table(pairs):
    row = lax.broadcasted_iota(jnp.int32, (8, 128), 0)
    lane = lax.broadcasted_iota(jnp.int32, (8, 128), 1)
    table = jnp.zeros((8, 128), F32)
    for number, sums in pairs:
        for kind in range(2):
            table = jnp.where((row == kind) & (lane == number), sums[kind], table)
    return table


def update_later_kernel(side_ref, own_ref, other_ref, *refs):
    outs, table_ref = refs[9:18], refs[18]
    zero = side_ref[0] == 0
    own, other = own_ref[...].astype(F32), other_ref[...].astype(F32)
    halves = (jnp.where(zero, own, other), jnp.where(zero, other, own))
    out_grad = jnp.concatenate([half[:, OUT_AT:] for half in halves], axis=1)
    up_grad = jnp.concatenate([half[:, UP_AT : UP_AT + FF // 2] for half in halves], axis=1)
    down_grad = jnp.concatenate(
        [half[:, DOWN_AT + D * part : DOWN_AT + D * (part + 1)] for half in halves for part in range(2)], axis=0
    )
    table_ref[...] = squares_table(
        [
            (1 + place, moments(*refs[3 * place : 3 * place + 3], gradient, *outs[3 * place : 3 * place + 3]))
            for place, gradient in enumerate((out_grad, up_grad, down_grad))
        ]
    )


def update_sooner_kernel(side_ref, own_ref, other_ref, small_ref, *refs):
    outs, table_ref = refs[6:12], refs[12]
    zero = side_ref[0] == 0
    own, other = own_ref[...].astype(F32), other_ref[...].astype(F32)
    qkv_grad = jnp.concatenate([jnp.where(zero, own, other), jnp.where(zero, other, own)], axis=1)
    mod_grad = jnp.concatenate([small_ref[:, COND * part : COND * (part + 1)] for part in range(6)], axis=0)
    table_ref[...] = squares_table(
        [
            (4 * place, moments(*refs[3 * place : 3 * place + 3], gradient, *outs[3 * place : 3 * place + 3]))
            for place, gradient in enumerate((qkv_grad, mod_grad))
        ]
    )


def update_moments(kernel, side, parts, arrays):
    block = pl.BlockSpec(memory_space=pltpu.VMEM)
    shapes = [jax.ShapeDtypeStruct(arrays[3 * (i // 3)].shape, F32) for i in range(len(arrays))]
    *outs, table = pl.pallas_call(
        kernel,
        in_specs=[SMALL_VMEM] + [block] * (len(parts) + len(arrays)),
        out_specs=[block] * (len(arrays) + 1),
        out_shape=shapes + [jax.ShapeDtypeStruct((8, 128), F32)],
        compiler_params=pltpu.CompilerParams(vmem_limit_bytes=48 * 2**20),
    )(side, *parts, *arrays)
    return [outs[i : i + 3] for i in range(0, len(outs), 3)], table


def renew_kernel(table_ref, *refs):
    norms_ref = refs[15]
    roots = jnp.sqrt(table_ref[...])
    norms_ref[...] = roots[:2, :5]
    for number in range(5):
        trust = roots[0:1, number : number + 1] / (roots[1:2, number : number + 1] + EPSILON)
        refs[10 + number][...] = refs[number][...] - (MATRIX_RATE * trust) * refs[5 + number][...]


def renew(table, matrices, turns):
    block = pl.BlockSpec(memory_space=pltpu.VMEM)
    return pl.pallas_call(
        renew_kernel,
        in_specs=[block] * 11,
        out_specs=[block] * 6,
        out_shape=[jax.ShapeDtypeStruct(matrix.shape, F32) for matrix in matrices] + [jax.ShapeDtypeStruct((2, 5), F32)],
        compiler_params=pltpu.CompilerParams(vmem_limit_bytes=48 * 2**20),
    )(table, *matrices, *turns)


ALONG = ((1, 2), (2, 1))


def column_of(core, chip, kind):
    first, second = ALONG[core]
    return (chip % 4) ^ (0, first, second, first ^ second)[kind]


ORIGIN = np.array(
    [
        [[column_of(core, chip, kind) + 4 * ((chip // 4 - back) % 4) for kind in range(4) for back in range(4)]
         for chip in range(UNITS)]
        for core in range(2)
    ],
    np.int32,
)
PLACES = np.array(
    [
        [[column_of(core, chip, kind) for kind in range(4)] + [(chip // 4 + ahead) % 4 for ahead in range(4)]
         for chip in range(UNITS)]
        for core in range(2)
    ],
    np.int32,
)


def along_z(values, ahead):
    return lax.ppermute(values, "fsdp", [(chip, chip % 4 + 4 * ((chip // 4 + ahead) % 4)) for chip in range(UNITS)])


def along_plane(values, direction):
    moves = [
        (core * UNITS + chip, core * UNITS + (chip ^ ALONG[core][direction]))
        for core in range(2)
        for chip in range(UNITS)
    ]
    return lax.ppermute(values, ("rep", "fsdp"), moves)


def swap_core(values):
    return lax.ppermute(values, "rep", [(0, 1), (1, 0)])


def hold_back(later, sooner):
    return lax.optimization_barrier((later, sooner))[0]


def by_rounds():
    return lax.axis_size("fsdp") == UNITS


def far_from(near):
    return along_plane(near[0], 1)


def near_of(piece):
    return [along_plane(piece, 0), along_plane(piece, 1)]


def swapped(values):
    return [swap_core(one) for one in values]


def column_sums_kernel(counts, places_ref, *refs):
    outs = refs[len(refs) - len(counts) :]
    at = 0
    for out_ref, count in zip(outs, counts):
        total = refs[at][...].astype(F32) + refs[at + 1][...].astype(F32)
        for arrived in refs[at + 2 : at + 2 + count]:
            total = total + arrived[...].astype(F32).reshape(total.shape)
        out_ref[...] = total.astype(BF).reshape(out_ref.shape)
        at += 2 + count


def column_sums(places, mine, given, parts, apart=False):
    block = mine.shape[1:]
    pair = [values.reshape((4, 4) + block) for values in (mine, given)]
    specs, operands, counts = [], [], []
    for ahead in range(4) if apart else (None,):
        for kind, arrived in parts:
            if apart:
                pick = pl.BlockSpec((1, 1) + block, lambda i, s, kind=kind, ahead=ahead: (s[4 + ahead], s[kind], 0, 0))
                came = pl.BlockSpec((1,) + block, lambda i, s, ahead=ahead: (s[4 + ahead], 0, 0))
            else:
                pick = pl.BlockSpec((1, 1) + block, lambda i, s, kind=kind: (i, s[kind], 0, 0))
                came = pl.BlockSpec((1,) + block, lambda i, s: (i, 0, 0))
            specs += [pick, pick] + [came] * len(arrived)
            operands += pair + arrived
            counts.append(len(arrived))
    if apart:
        out_spec, out_shape = pl.BlockSpec(block, lambda i, s: (0, 0)), jax.ShapeDtypeStruct(block, BF)
    else:
        out_spec, out_shape = pl.BlockSpec((1,) + block, lambda i, s: (i, 0, 0)), jax.ShapeDtypeStruct((4,) + block, BF)
    return pl.pallas_call(
        functools.partial(column_sums_kernel, counts),
        grid_spec=pltpu.PrefetchScalarGridSpec(
            num_scalar_prefetch=1,
            grid=(1 if apart else 4,),
            in_specs=specs,
            out_specs=[out_spec] * len(counts),
        ),
        out_shape=[out_shape] * len(counts),
        cost_estimate=pl.CostEstimate(flops=0, bytes_accessed=(200 if apart else 12) * 2**20, transcendentals=0),
        compiler_params=pltpu.CompilerParams(vmem_limit_bytes=(62 if block[1] > D * 3 else 48) * 2**20),
    )(places, *operands)


class Scatter:
    def __init__(self, mine, give, places):
        self.mine, self.places = mine, places
        self.given = swap_core(give)

    def send_far(self, sooner=None):
        given = self.given if sooner is None else hold_back(self.given, sooner)
        far, second = column_sums(self.places, self.mine, given, [(3, []), (2, [])])
        self.far_came, self.second_came = along_plane(far, 1), along_plane(second, 1)
        return far

    def send_first(self, sooner=None):
        self.far_came, self.second_came = (
            (self.far_came, self.second_came) if sooner is None else hold_back((self.far_came, self.second_came), sooner)
        )
        (first,) = column_sums(self.places, self.mine, self.given, [(1, [self.far_came])])
        self.arrived = [along_plane(first, 0), self.second_came]
        return first

    def send_far_alone(self, sooner):
        (far,) = column_sums(self.places, self.mine, hold_back(self.given, sooner), [(3, [])])
        self.far_came = along_plane(far, 1)
        return far

    def send_neighbours(self, sooner):
        far_came = hold_back(self.far_came, sooner)
        first, second = column_sums(self.places, self.mine, self.given, [(1, [far_came]), (2, [])])
        self.arrived = [along_plane(first, 0), along_plane(second, 1)]
        return first

    def send_column(self, sooner=None):
        arrived = self.arrived if sooner is None else hold_back(self.arrived, sooner)
        units = column_sums(self.places, self.mine, self.given, [(0, arrived)], apart=True)
        self.own = units[0]
        self.came = [along_z(units[ahead], ahead) for ahead in range(1, 4)]
        return self.own

    def finish(self, sooner=None):
        came = self.came if sooner is None else hold_back(self.came, sooner)
        total = self.own.astype(F32)
        for part in came:
            total = total + part.astype(F32)
        own = total.astype(BF)
        return (own, swap_core(own))


def arrivals_kernel(outputs, *refs):
    inputs, outs = refs[1 : len(refs) - outputs], refs[len(refs) - outputs :]
    each = len(inputs) // outputs
    for number, out_ref in enumerate(outs):
        total = inputs[number * each][...].astype(F32)
        for part in inputs[number * each + 1 : (number + 1) * each]:
            total = total + part[...].astype(F32)
        out_ref[...] = total.reshape(out_ref.shape).astype(BF)


def arrival_sums(places, parts, apart):
    block = parts[0].shape[1:]
    if apart:
        specs = [
            pl.BlockSpec((1,) + block, lambda i, s, ahead=ahead: (s[4 + ahead], 0, 0)) for ahead in range(4) for _ in parts
        ]
        out_spec, out_shape, outputs = pl.BlockSpec(block, lambda i, s: (0, 0)), block, 4
    else:
        out_spec = pl.BlockSpec((4,) + block, lambda i, s: (0, 0, 0))
        specs, out_shape, outputs = [out_spec] * len(parts), (4,) + block, 1
    return pl.pallas_call(
        functools.partial(arrivals_kernel, outputs),
        grid_spec=pltpu.PrefetchScalarGridSpec(
            num_scalar_prefetch=1, grid=(1,), in_specs=specs, out_specs=[out_spec] * outputs
        ),
        out_shape=[jax.ShapeDtypeStruct(out_shape, BF)] * outputs,
    )(places, *(list(parts) * outputs))


class SmallScatter:
    def __init__(self, own, first, second, far, places):
        self.places, self.own, self.first = places, own, first
        self.far_came, self.second_came = along_plane(far, 1), along_plane(second, 1)

    def send_first(self, sooner):
        far_came, self.second_came = hold_back((self.far_came, self.second_came), sooner)
        first = (self.first.astype(F32) + far_came.astype(F32)).astype(BF)
        self.first_came = along_plane(first, 0)
        return first

    def send_column(self, sooner):
        came = hold_back(self.first_came, sooner)
        self.own, *units = arrival_sums(self.places, [self.own, came, self.second_came], True)
        self.came = [along_z(unit, ahead + 1) for ahead, unit in enumerate(units)]
        return self.own

    def finish(self, sooner):
        total = self.own.astype(F32)
        for part in hold_back(self.came, sooner):
            total = total + part.astype(F32)
        own = total.astype(BF)
        return own.astype(F32) + swap_core(own).astype(F32)


def sum_small(values):
    for turns in ((1, 2, 3), (4, 8, 12)):
        came = [lax.ppermute(values, "fsdp", [(chip, chip ^ turn) for chip in range(UNITS)]) for turn in turns]
        values = (values + came[0]) + (came[1] + came[2])
    return values


def side_columns(matrix, core, width):
    return lax.dynamic_slice_in_dim(matrix, core * width, width, axis=1)


def side_rows(blocks, core):
    return lax.dynamic_index_in_dim(blocks, core, 1, keepdims=False)


def pack_first(qkv, mod_turned, vectors, core):
    count = vectors.shape[0]
    mod_blocks = side_rows(mod_turned.reshape(count, 2, 3, 48, COND), core)
    padded = jnp.pad(vectors, ((0, 0), (0, 640 - VECTOR_PART))).reshape(count, 5, 128)
    return jnp.concatenate(
        [
            side_columns(qkv, core, QKV_HALF).reshape(count, 48, QKV_HALF),
            mod_blocks.transpose(0, 2, 1, 3).reshape(count, 48, 3 * COND),
            jnp.pad(padded, ((0, 0), (0, 43), (0, 0))),
        ],
        axis=2,
    )


def pack_second(out, up, down, core):
    count = out.shape[0] // 48
    down_blocks = side_rows(down.reshape(count, 2, 2, 48, D), core)
    return jnp.concatenate(
        [
            side_columns(up, core, FF // 2).reshape(count, 48, FF // 2),
            down_blocks.transpose(0, 2, 1, 3).reshape(count, 48, 2 * D),
            side_columns(out, core, D // 2).reshape(count, 48, D // 2),
        ],
        axis=2,
    )


def unpack_qkv(sides):
    return jnp.concatenate([side for side in sides], axis=2).reshape(-1, 3 * D)


def unpack_small(own, first, second, far):
    units = jnp.stack([own, first, second, far], axis=1).reshape(UNITS, 48, SMALL_WIDE)
    turned = units[:, :, : 6 * COND].reshape(UNITS, 48, 6, COND).transpose(0, 2, 1, 3).reshape(6 * D, COND)
    vectors = units[:, :5, 6 * COND :].reshape(UNITS, 640)[:, :VECTOR_PART]
    return (turned.T, vectors.reshape(-1))


def unpack_second(sides):
    count = sides[0].shape[0]
    up = jnp.concatenate([side[:, :, UP_AT : UP_AT + FF // 2] for side in sides], axis=2).reshape(count * 48, FF)
    out = jnp.concatenate([side[:, :, OUT_AT:] for side in sides], axis=2).reshape(count * 48, D)
    down = jnp.stack([side[:, :, DOWN_AT : DOWN_AT + 2 * D] for side in sides], axis=1)
    down = down.reshape(count, 2, 48, 2, D).transpose(0, 1, 3, 2, 4).reshape(count * 192, D)
    return (out, up, down)


def gather_plain(parts, axes):
    return [lax.all_gather(part, "fsdp", axis=axis, tiled=True) for part, axis in zip(parts, axes)]


def virtual_units(pack, pieces=False):
    cuts = [0, 1, 4, 5, 8, 9, 12, 13, 16] if pieces else [0, 4, 8, 12, 14, 16]
    return [packed[start:stop] for packed in (pack(0), pack(1)) for start, stop in zip(cuts, cuts[1:])]


def reduce_plain(grads, axes):
    parts = [
        lax.psum_scatter(grad.astype(F32), "fsdp", scatter_dimension=axis, tiled=True) for grad, axis in zip(grads, axes)
    ]
    return tuple(lax.psum(part.astype(BF), "rep").astype(F32) for part in parts)


def adam_direction(weight, first_old, second_old, gradient, decay_rate):
    first_new = BETA_ONE * first_old + (1.0 - BETA_ONE) * gradient
    second_new = BETA_TWO * second_old + (1.0 - BETA_TWO) * gradient * gradient
    direction = (
        first_new
        / (1.0 - BETA_ONE**STEP)
        / (jnp.sqrt(second_new / (1.0 - BETA_TWO**STEP)) + EPSILON)
        + decay_rate * weight
    )
    return (first_new, second_new, direction)


def layout_tables(sizes_row, lengths_row):
    slot_ids = jnp.arange(SLOTS, dtype=jnp.int32)
    seg_ends = jnp.cumsum(sizes_row)
    starts = seg_ends - sizes_row
    segment = jnp.sum((slot_ids[:, None] >= seg_ends[None, :]).astype(jnp.int32), axis=1)
    member = segment[:, None] == jnp.arange(NSEG, dtype=jnp.int32)[None, :]
    offset = jnp.sum(jnp.where(member, starts[None, :], 0), axis=1)
    length_of = jnp.sum(jnp.where(member, lengths_row[None, :], 0), axis=1)
    position = slot_ids - offset
    return (segment, member, position, position < length_of)


def condition(steps_row):
    half_cond = COND // 2
    frequency = jnp.exp(jnp.arange(half_cond, dtype=F32) * (-math.log(10000.0) / half_cond))
    angles = steps_row.astype(F32)[:, None] * frequency[None, :]
    return jax.nn.silu(jnp.concatenate([jnp.cos(angles), jnp.sin(angles)], axis=1))


FORWARD_CALLS = (2, 3, 1)
BACKWARD_CALLS = (1, 2, 3)


def on_device(
    inputs, cotangent, seg_sizes, seq_lengths, timesteps, absorbed,
    qkv_weight, out_weight, up_weight, down_weight, mod_weight,
    qkv_first, out_first, up_first, down_first, mod_first,
    qkv_second, out_second, up_second, down_second, mod_second,
    vectors, vectors_first, vectors_second,
):
    rounds = by_rounds()
    chip = lax.axis_index("fsdp")
    core = lax.axis_index("rep")
    matrices = (qkv_weight, out_weight, up_weight, down_weight, mod_weight)
    qkv_low, out_low, up_low, down_low, mod_low = [matrix.astype(BF) for matrix in matrices]
    vector_low = vectors.astype(BF)
    if rounds:
        order = jnp.concatenate([jnp.asarray(ORIGIN)[core, chip], jnp.asarray(ORIGIN)[1 - core, chip]])
        places = jnp.asarray(PLACES)[core, chip]
        order, places = lax.optimization_barrier((order, places))
        side = core[None].astype(jnp.int32)
        unit_first = pack_first(qkv_low, mod_low.T, vector_low[None], core)[0]
        unit_second = pack_second(out_low, up_low, down_low, core)[0]
        second_one = unit_second[None]
        first_back = [along_z(unit_first, back) for back in range(1, 4)]
        second_near = near_of(second_one)
        first_column = jnp.stack([unit_first] + first_back)
        first_near = near_of(first_column)
        second_from = hold_back(unit_second, first_column)
        second_back = [along_z(second_from, back) for back in range(1, 4)]
        first_near, second_near = lax.optimization_barrier((first_near, second_near))
        first_far = [along_plane(first_near[0][start : start + 2], 1) for start in (0, 2)]
        units_first, second_back = lax.optimization_barrier(([first_column] + first_near + first_far, second_back))
        units_first = units_first + swapped(units_first)
    else:
        order = jnp.concatenate([jnp.arange(UNITS, dtype=jnp.int32)] * 2)
        places = jnp.asarray(PLACES)[0, 0]
        side = jnp.zeros((1,), jnp.int32)
        qkv_all, mod_all, vector_all = gather_plain((qkv_low, mod_low, vector_low), (0, 1, 0))
        out_all, up_all, down_all = gather_plain((out_low, up_low, down_low), (0, 0, 0))
        units_first = virtual_units(lambda s: pack_first(qkv_all, mod_all.T, vector_all.reshape(UNITS, -1), s))
        units_second = virtual_units(lambda s: pack_second(out_all, up_all, down_all, s), True)

    segment, member, position, valid_slot = layout_tables(seg_sizes[0], seq_lengths[0])
    tiles = segment.reshape(BLOCKS, TILE)[:, 0]
    member_tile = member.reshape(BLOCKS, TILE, NSEG)[:, 0].astype(F32)
    condition_low = condition(timesteps[0]).astype(BF)
    cos, sin, feature_query, feature_key = attention_tables(segment, position, valid_slot)
    weight_mask = (absorbed[0] * valid_slot.astype(jnp.int32)).astype(F32).reshape(BLOCKS, TILE)
    row_in, row_cot = inputs[0], cotangent[0]

    mixed, first_low, qkv_full, modulation, flat = first_part(
        units_first, order, side, tiles, row_in, condition_low, cos, sin
    )
    forward, first_pair = None, 0
    if rounds:
        second_rest = jnp.stack(second_back)
        second_rest_near = near_of(second_rest)
    for number, count in enumerate(FORWARD_CALLS):
        if rounds and number == 1:
            second_rest_far = far_from(hold_back(second_rest_near, forward))
            second_own = [second_one, second_rest, second_near[0], second_rest_near[0], second_near[1], second_rest_near[1]]
            second_own.append(far_from(second_near))
            second_other = swapped(hold_back(second_own[:-1], forward)) + swapped(second_own[-1:])
        if rounds and number == 2:
            forward, second_rest_far = hold_back((forward, second_rest_far), second_other)
        forward = attention_forward(mixed, feature_query, feature_key, forward, first_pair, count)
        first_pair += count
    if rounds:
        units_second = second_own + [second_rest_far] + second_other + [swap_core(second_rest_far)]
    attended_low, feature = forward
    out_hidden, grad_middle, grad_attended, sums, bias_sums, mine_later, give_later = middle_part(
        units_second, order, side, tiles, attended_low, row_in, row_cot, weight_mask, modulation, flat
    )
    state = [None]

    def backward_part(number, came):
        grad_here = grad_attended if came is None else hold_back(grad_attended, came)
        state[0] = attention_backward(
            mixed, feature, feature_key, grad_here, attended_low, cos, sin, state[0],
            sum(BACKWARD_CALLS[:number]), BACKWARD_CALLS[number],
        )
        return state[0]

    def qkv_end(sooner=None):
        follows = state[0] if sooner is None else hold_back(state[0], sooner)
        return qkv_grads(side, first_low, follows)

    def row_end(sooner=None):
        follows = state[0] if sooner is None else hold_back(state[0], sooner)
        return last_part(
            places, tiles, member_tile, follows, qkv_full, row_in, grad_middle, modulation, flat, condition_low,
            sums, bias_sums,
        )

    vector_arrays = (vectors, vectors_first, vectors_second)
    of_qkv, of_out = (qkv_weight, qkv_first, qkv_second), (out_weight, out_first, out_second)
    of_up, of_down = (up_weight, up_first, up_second), (down_weight, down_first, down_second)
    of_mod = (mod_weight, mod_first, mod_second)
    if rounds:
        later = Scatter(mine_later, give_later, places)
        backward_part(0, None)
        sent = later.send_far_alone(state[0])
        backward_part(1, sent)
        sent = later.send_neighbours(state[0])
        backward_part(2, sent)
        qkv_parts = qkv_end(later.arrived)
        sooner = Scatter(*qkv_parts, places)
        sent = later.send_column(qkv_parts)
        sent = sooner.send_far(sent)
        grad_in, *small_parts = row_end(sent)
        small = SmallScatter(*small_parts, places)
        sent = sooner.send_first((grad_in, later.came[0], later.came[2]))
        sent = sooner.send_column(sent)
        sent = small.send_first((sent, later.came[1], sooner.came[0]))
        sent = small.send_column((sent, sooner.came[:2]))
        later_sums = later.finish(sent)
        (out_new, up_new, down_new), later_table = update_moments(
            update_later_kernel, side, later_sums, of_out + of_up + of_down
        )
        qkv_sums = sooner.finish(later_table)
        small_sums = small.finish(later_table)
        (qkv_new, mod_new), sooner_table = update_moments(
            update_sooner_kernel, side, qkv_sums + (small_sums,), of_qkv + tuple(part.T for part in of_mod)
        )
        results = [qkv_new, out_new, up_new, down_new, mod_new]
        *renewed, norm_roots = renew(
            sum_small(later_table + sooner_table),
            [*matrices[:4], mod_weight.T],
            [record[2] for record in results],
        )
        renewed[4] = renewed[4].T
        results[4] = [part.T for part in mod_new]
        grad_vectors = small_sums[:5, 6 * COND :].reshape(-1)[:VECTOR_PART]
    else:
        for number in range(3):
            backward_part(number, None)
        grad_out, grad_up, grad_down = reduce_plain(unpack_second((mine_later, give_later)), (0, 0, 0))
        grad_in, *small_parts = row_end()
        grad_qkv, grad_mod, grad_vectors = reduce_plain(
            (unpack_qkv(qkv_end()), *unpack_small(*small_parts)), (0, 1, 0)
        )
        grads = (grad_qkv, grad_out, grad_up, grad_down, grad_mod)
        olds = (of_qkv, of_out, of_up, of_down, of_mod)
        results = [adam_direction(*old, grad, DECAY_RATE) for old, grad in zip(olds, grads)]
        squares = [
            jnp.stack([jnp.sum(values[number] * values[number]) for number in range(5)])
            for values in (matrices, [record[2] for record in results])
        ]
        norm_roots = jnp.sqrt(lax.psum(jnp.stack(squares), "fsdp"))
        trust = norm_roots[0] / (norm_roots[1] + EPSILON)
        renewed = [matrices[number] - MATRIX_RATE * trust[number] * results[number][2] for number in range(5)]
    vector_record = adam_direction(*vector_arrays, grad_vectors, 0.0)
    return (
        out_hidden[None],
        grad_in[None],
        *renewed,
        *[record[0] for record in results],
        *[record[1] for record in results],
        vectors - VECTOR_RATE * vector_record[2],
        vector_record[0],
        vector_record[1],
        norm_roots,
    )


def solution(mesh):
    rows = P(("rep", "fsdp"))
    matrix, turned, vector = P("fsdp", None), P(None, "fsdp"), P("fsdp")
    five = (matrix, matrix, matrix, matrix, turned)
    return jax.shard_map(
        on_device,
        mesh=mesh,
        in_specs=(rows,) * 6 + five * 3 + (vector,) * 3,
        out_specs=(rows, rows) + five * 3 + (vector,) * 3 + (P(),),
        check_vma=False,
    )
```
